32 devices in a mesh: sector: 4 (over y, core), axial: 8 (over z, x).
Axes of the slice: x: 2, y: 2, z: 4, core: 2. Of those that a mesh axis runs over, the one named last changes fastest.
Arguments:
- adjoint: float32 [5, 64, 32768], P(None, None, ('sector', 'axial')), may hold values from -6 to 6
- velocity: bfloat16 [3, 64, 32768], P(None, None, ('sector', 'axial')), may hold values from -6 to 6
- drag: float32 [32768], P(('sector', 'axial')), may hold values from 0.5 to 5
- block_weight: float32 [32768], P(('sector', 'axial')), may hold values from 0.2 to 1
- flux_jac: float32 [3, 5, 5], replicated, may hold values from -2.5 to 2.5
- face_own: float32 [6, 5, 5], replicated, may hold values from -4 to 4
- face_nbr: float32 [6, 5, 5], replicated, may hold values from -4 to 4
- nbr_local: int32 [6, 32768], P(None, ('sector', 'axial')), may hold values from 0 to 1024, as said below
- sector_slots: int32 [2, 8192], P(None, ('sector', 'axial')), may hold values from 0 to 1023, as said below
- axial_slots: int32 [2, 8192], P(None, ('sector', 'axial')), may hold values from 0 to 1023, as said below
- sector_live: int32 [4, 8, 2], P('sector', 'axial'), may hold values from 128 to 256, as said below
- elem_block: int32 [32768], P(('sector', 'axial')), may hold values from 0 to 4095, as said below
Outputs:
- adjoint_next: float32 [5, 64, 32768], P(None, None, ('sector', 'axial'))
- block_grad: float32 [4096], P(('sector', 'axial'))
The draws below stay inside these ranges and needn't reach their ends.
Inputs may be any that keep to these rules, and one draw needn't show every extreme that they name: The elements of one device fill a block of 4 x 64 x 4 cells in some order; nbr_local is symmetric: across face f of element e lies face f xor 1 of element nbr_local[f, e]; the value 1024 marks faces on the device boundary. `sector_slots`: each row lists 256 distinct local elements of the device; slot s of one device's upper row and slot s of the next device's lower row are the two sides of one face with matching node order. `axial_slots`: each row lists 256 distinct local elements of the device; slot s of one device's upper row and slot s of the next slab's lower row are the two sides of one face with matching node order. `sector_live`: A device's upper count equals the lower count of the device one higher in sector index (cyclically). `elem_block`: the owner of an element's block (block // 128, in joint device order) is the element's own device or the one just before or after it, cyclically.
All inputs are finite; a program needn't handle non-finite values.
Results may differ from the reference program's by a relative error of at most 0.0006.
Values sent between devices are 32-bit elements; how exact they have to be, the bound alone decides.
A program may use at most 128 MiB of HBM per device.

```python
import math
import jax
import jax.numpy as jnp
import numpy as np
from jax import lax

FIELDS = 5
NODES = 64
SPAN = 4
RADIAL = 64
E_DEV = 1024
FACES = 256
SECTORS = 4
SLABS = 8
ELEMENTS = 32768
BLOCKS = 4096
BLK_DEV = 128


def cell_layout(key):
    devices = SECTORS * SLABS

    def one_device(device_id):
        return jax.random.permutation(jax.random.fold_in(jax.random.fold_in(key, 101), device_id), E_DEV).astype(jnp.int32)
    return jax.vmap(one_device)(jnp.arange(devices, dtype=jnp.int32))


def draw_nbr_local(key, part):
    devices = SECTORS * SLABS
    layout = cell_layout(key)
    cell_ids = jnp.arange(E_DEV, dtype=jnp.int32)
    along_x = cell_ids // (RADIAL * SPAN)
    along_y = cell_ids // SPAN % RADIAL
    along_z = cell_ids % SPAN
    neighbour_steps = [(along_x > 0, -RADIAL * SPAN), (along_x < SPAN - 1, RADIAL * SPAN), (along_y > 0, -SPAN), (along_y < RADIAL - 1, SPAN), (along_z > 0, -1), (along_z < SPAN - 1, 1)]
    device_rows = jnp.arange(devices, dtype=jnp.int32)[:, None]
    stacked_rows = []
    for present, offset in neighbour_steps:
        target = jnp.where(present, cell_ids + offset, 0)
        neighbour = jnp.where(present[None, :], layout[:, target], E_DEV)
        by_element = jnp.zeros_like(layout).at[device_rows, layout].set(neighbour)
        stacked_rows.append(by_element.reshape(-1))
    return jnp.stack(stacked_rows).astype(jnp.int32)


def draw_sector_slots(key, part):
    layout = cell_layout(key)
    slot_ids = jnp.arange(FACES, dtype=jnp.int32)
    lower_row = layout[:, slot_ids].reshape(-1)
    upper_row = layout[:, (SPAN - 1) * RADIAL * SPAN + slot_ids].reshape(-1)
    return jnp.stack([lower_row, upper_row]).astype(jnp.int32)


def draw_axial_slots(key, part):
    layout = cell_layout(key)
    slot_ids = jnp.arange(FACES, dtype=jnp.int32)
    lower_row = layout[:, slot_ids * SPAN].reshape(-1)
    upper_row = layout[:, slot_ids * SPAN + SPAN - 1].reshape(-1)
    return jnp.stack([lower_row, upper_row]).astype(jnp.int32)


def draw_sector_live(key, part):
    counts = jax.random.randint(jax.random.fold_in(key, 202), (SECTORS, SLABS), FACES // 2, FACES + 1).astype(jnp.int32)
    counts = counts.at[0].set(FACES).at[1].set(FACES // 2)
    return jnp.stack([jnp.roll(counts, 1, axis=0), counts], axis=-1).astype(jnp.int32)


def draw_elem_block(key, part):
    element_ids = jnp.arange(ELEMENTS, dtype=jnp.int32)
    device_ids = element_ids // E_DEV
    local_ids = element_ids % E_DEV
    offsets = jax.random.randint(jax.random.fold_in(key, 303), (ELEMENTS,), -BLK_DEV, 2 * BLK_DEV).astype(jnp.int32)
    offsets = jnp.where(local_ids == 0, -1, jnp.where(local_ids == 1, 0, offsets))
    return ((device_ids * BLK_DEV + offsets) % BLOCKS).astype(jnp.int32)


def block_scale(key, shape, cuts, least, high):
    loudness, own = 1.0, jax.random.fold_in(key, 6)
    for dim, parts in cuts:
        heights = jnp.exp(jax.random.uniform(jax.random.fold_in(own, dim), (parts,), jnp.float32, least / len(cuts), high / len(cuts)))
        loudness = loudness * jnp.repeat(heights, shape[dim] // parts).reshape([-1 if axis == dim else 1 for axis in range(len(shape))])
    return loudness


def scatter_about(stream_key, extent, spread, bound, pieces=(), kind=jnp.bfloat16):
    values = jax.random.normal(stream_key, extent, jnp.float32) * spread
    if len(pieces) > 0:
        values = block_scale(stream_key, extent, pieces, -0.22, 0.18) * values
    return jnp.clip(values, min=-bound, max=bound).astype(kind)


def setup_inputs(seed: int = 0) -> dict:
    splits = jax.random.split(jax.random.key(seed), 13)
    adjoint = scatter_about(splits[0], (FIELDS, NODES, ELEMENTS), 1.0, 6.0, ((2, 32),), jnp.float32)
    velocity = scatter_about(splits[1], (3, NODES, ELEMENTS), 1.0, 6.0, ((2, 32),))
    drag = jnp.clip(jnp.exp(math.log(5.0) - 2.3025851 * jax.random.uniform(splits[2], (ELEMENTS,), jnp.float32) ** block_scale(splits[2], (ELEMENTS,), ((0, 32),), -0.2, 0.2)), 0.5, 5.0)
    block_weight = jnp.clip(0.2 + 0.8 * jax.random.uniform(splits[3], (ELEMENTS,), jnp.float32) ** block_scale(splits[3], (ELEMENTS,), ((0, 32),), -0.2, 0.2), 0.2, 1.0)
    flux_jac = scatter_about(splits[4], (3, FIELDS, FIELDS), FIELDS ** -0.5, 2.5, (), jnp.float32)
    face_own = scatter_about(splits[5], (6, FIELDS, FIELDS), 1.0, 4.0, (), jnp.float32)
    face_nbr = scatter_about(splits[6], (6, FIELDS, FIELDS), 1.0, 4.0, (), jnp.float32)
    nbr_local = draw_nbr_local(jax.random.fold_in(splits[12], 71), 0)
    sector_slots = draw_sector_slots(jax.random.fold_in(splits[12], 71), 0)
    axial_slots = draw_axial_slots(jax.random.fold_in(splits[12], 71), 0)
    sector_live = draw_sector_live(jax.random.fold_in(splits[12], 71), 0)
    elem_block = draw_elem_block(jax.random.fold_in(splits[12], 71), 0)
    return dict(adjoint=adjoint, velocity=velocity, drag=drag, block_weight=block_weight, flux_jac=flux_jac, face_own=face_own, face_nbr=face_nbr, nbr_local=nbr_local, sector_slots=sector_slots, axial_slots=axial_slots, sector_live=sector_live, elem_block=elem_block)


PRECISE = lax.Precision.HIGHEST

def lobatto_tables():
    points = np.array([-1.0, -1.0 / np.sqrt(5.0), 1.0 / np.sqrt(5.0), 1.0])
    weights = np.array([1.0, 5.0, 5.0, 1.0]) / 6.0
    scales = np.array([np.prod([points[i] - points[k] for k in range(4) if k != i]) for i in range(4)])
    derivative = np.zeros((4, 4))
    for i in range(4):
        for p in range(4):
            if i != p:
                derivative[i, p] = scales[i] / scales[p] / (points[i] - points[p])
            else:
                derivative[i, p] = sum((1.0 / (points[i] - points[k]) for k in range(4) if k != i))
    node_weight = (weights[:, None, None] * weights[None, :, None] * weights[None, None, :]).reshape(64) / 8.0
    return (derivative, node_weight)

def volume_term(adjoint, flux_jac, derivative):
    fields, node_count, elem_count = adjoint.shape
    node_cube = adjoint.reshape(fields, 4, 4, 4, elem_count)
    along_a = jnp.einsum('pi,hpbge->hibge', derivative, node_cube, precision=PRECISE)
    along_b = jnp.einsum('pi,hapge->haige', derivative, node_cube, precision=PRECISE)
    along_g = jnp.einsum('pi,habpe->habie', derivative, node_cube, precision=PRECISE)
    stacked = jnp.stack([along_a, along_b, along_g]).reshape(3, fields, node_count, elem_count)
    return jnp.einsum('dhc,dhne->cne', flux_jac, stacked, precision=PRECISE)

def face_traces(adjoint):
    fields, node_count, elem_count = adjoint.shape
    node_cube = adjoint.reshape(fields, 4, 4, 4, elem_count)
    face_slabs = [node_cube[:, 0], node_cube[:, 3], node_cube[:, :, 0], node_cube[:, :, 3], node_cube[:, :, :, 0], node_cube[:, :, :, 3]]
    return jnp.stack([slab.reshape(fields, 16, elem_count) for slab in face_slabs])

def lift_faces(surface):
    face_count, fields, face_nodes, elem_count = surface.shape
    face_tiles = surface.reshape(6, fields, 4, 4, elem_count)
    node_cube = jnp.zeros((fields, 4, 4, 4, elem_count), jnp.float32)
    node_cube = node_cube.at[:, 0].add(face_tiles[0]).at[:, 3].add(face_tiles[1])
    node_cube = node_cube.at[:, :, 0].add(face_tiles[2]).at[:, :, 3].add(face_tiles[3])
    node_cube = node_cube.at[:, :, :, 0].add(face_tiles[4]).at[:, :, :, 3].add(face_tiles[5])
    return node_cube.reshape(fields, 64, elem_count)

def finish_update(adjoint, velocity, drag, nbr_local, sector_slots, axial_slots, live_counts, received, flux_jac, face_own, face_nbr):
    derivative_np, weight_np = lobatto_tables()
    derivative = jnp.asarray(derivative_np, dtype=jnp.float32)
    node_weight = jnp.asarray(weight_np, dtype=jnp.float32)
    fields, node_count, elem_count = adjoint.shape
    traces = face_traces(adjoint)
    inside = nbr_local < elem_count
    clamped = jnp.where(inside, nbr_local, 0)
    partners = []
    for face_id in range(6):
        partner_tr = jnp.take(traces[face_id ^ 1], clamped[face_id], axis=2)
        partners.append(jnp.where(inside[face_id][None, None, :], partner_tr, 0.0))
    slot_count = sector_slots.shape[1]
    positions = jnp.arange(slot_count, dtype=jnp.int32)
    mask_low = (positions < live_counts[0]).astype(jnp.float32)
    mask_high = (positions < live_counts[1]).astype(jnp.float32)
    from_x_below, from_x_above, from_z_below, from_z_above = received

    def place(partner_face, arrived, slot_list, weight_mask):
        values = (arrived * weight_mask[None, :]).reshape(fields, 16, slot_count)
        return partner_face.at[:, :, slot_list].add(values)
    partners[0] = place(partners[0], from_x_below, sector_slots[0], mask_low)
    partners[1] = place(partners[1], from_x_above, sector_slots[1], mask_high)
    ones_mask = jnp.ones((slot_count,), jnp.float32)
    partners[4] = place(partners[4], from_z_below, axial_slots[0], ones_mask)
    partners[5] = place(partners[5], from_z_above, axial_slots[1], ones_mask)
    partner_all = jnp.stack(partners)
    surface = jnp.einsum('fch,fhme->fcme', face_own, traces, precision=PRECISE) + jnp.einsum('fch,fhme->fcme', face_nbr, partner_all, precision=PRECISE)
    field_mask = jnp.array([0.0, 1.0, 1.0, 1.0, 0.0], dtype=jnp.float32)
    damping = field_mask[:, None, None] * drag[None, None, :]
    tendency = volume_term(adjoint, flux_jac, derivative) + lift_faces(surface) - damping * adjoint
    adjoint_next = adjoint + 0.1 * tendency
    velocity_f = velocity.astype(jnp.float32)
    elem_grad = drag * lax.optimization_barrier(jnp.sum(adjoint[1:4] * velocity_f * node_weight[None, :, None], axis=(0, 1)))
    return (adjoint_next, elem_grad)

def reference(adjoint, velocity, drag, block_weight, flux_jac, face_own, face_nbr, nbr_local, sector_slots, axial_slots, sector_live, elem_block):
    fields = adjoint.shape[0]
    devices = SECTORS * SLABS
    node_cube = adjoint.reshape(fields, 4, 4, 4, ELEMENTS)
    base_index = (jnp.arange(devices, dtype=jnp.int32) * E_DEV)[:, None]

    def edge(tile, slot_row):
        gathered = (base_index + slot_row.reshape(devices, FACES).astype(jnp.int32)).reshape(-1)
        picked = jnp.take(tile.reshape(fields * 16, ELEMENTS), gathered, axis=1)
        return picked.reshape(fields * 16, SECTORS, SLABS, FACES)
    low_x = edge(node_cube[:, 0], sector_slots[0])
    high_x = edge(node_cube[:, 3], sector_slots[1])
    low_z = edge(node_cube[:, :, :, 0], axial_slots[0])
    high_z = edge(node_cube[:, :, :, 3], axial_slots[1])
    from_x_below = jnp.roll(high_x, 1, axis=1)
    from_x_above = jnp.roll(low_x, -1, axis=1)
    zero_slab = jnp.zeros_like(high_z[:, :, :1])
    from_z_below = jnp.concatenate([zero_slab, high_z[:, :, :-1]], axis=2)
    from_z_above = jnp.concatenate([low_z[:, :, 1:], zero_slab], axis=2)
    recv_all = [stacked_arr.reshape(fields * 16, devices, FACES) for stacked_arr in (from_x_below, from_x_above, from_z_below, from_z_above)]
    live_all = sector_live.reshape(devices, 2)
    nbr_all = nbr_local.reshape(6, devices, E_DEV)
    sector_all = sector_slots.reshape(2, devices, FACES)
    axial_all = axial_slots.reshape(2, devices, FACES)

    def visit_device(device_q, carry):
        result, elem_grads = carry
        first_col = device_q * E_DEV

        def select_device(stacked_arr):
            return lax.dynamic_index_in_dim(stacked_arr, device_q, 1, False)
        own_state = lax.dynamic_slice_in_dim(adjoint, first_col, E_DEV, 2)
        own_velocity = lax.dynamic_slice_in_dim(velocity, first_col, E_DEV, 2)
        own_drag = lax.dynamic_slice_in_dim(drag, first_col, E_DEV, 0)
        received = tuple((select_device(stacked_arr) for stacked_arr in recv_all))
        live_counts = lax.dynamic_index_in_dim(live_all, device_q, 0, False)
        state_next, grad_part = finish_update(own_state, own_velocity, own_drag, select_device(nbr_all), select_device(sector_all), select_device(axial_all), live_counts, received, flux_jac, face_own, face_nbr)
        result = lax.dynamic_update_slice_in_dim(result, state_next, first_col, 2)
        elem_grads = lax.dynamic_update_slice_in_dim(elem_grads, grad_part, first_col, 0)
        return (result, elem_grads)
    adjoint_next, elem_grads = lax.fori_loop(0, devices, visit_device, (jnp.zeros_like(adjoint), jnp.zeros((ELEMENTS,), jnp.float32)))
    block_grad = jax.ops.segment_sum(block_weight * elem_grads, elem_block, num_segments=BLOCKS)
    return (adjoint_next, block_grad)
```

```python
import functools

import jax
import jax.numpy as jnp
import numpy as np
from jax import lax
from jax.experimental import pallas as pl
from jax.experimental.pallas import tpu as pltpu
from jax.sharding import PartitionSpec as P

BLOCKS = 4096
BF = jnp.bfloat16
F32 = jnp.float32
MESH = pl.DeviceIdType.MESH
INPUTS = 13
SIDES = (0, 1, 4, 5)


def lobatto_tables():
    points = np.array([-1.0, -1.0 / np.sqrt(5.0), 1.0 / np.sqrt(5.0), 1.0])
    weights = np.array([1.0, 5.0, 5.0, 1.0]) / 6.0
    scales = np.array(
        [np.prod([points[i] - points[k] for k in range(4) if k != i]) for i in range(4)]
    )
    derivative = np.zeros((4, 4))
    for i in range(4):
        for p in range(4):
            if i != p:
                derivative[i, p] = scales[i] / scales[p] / (points[i] - points[p])
            else:
                derivative[i, p] = sum((1.0 / (points[i] - points[k]) for k in range(4) if k != i))
    node_weight = (
        weights[:, None, None] * weights[None, :, None] * weights[None, None, :]
    ).reshape(64) / 8.0
    return (derivative, node_weight)


def constant_tables():
    derivative, node_weight = lobatto_tables()
    eye = np.eye(4)
    step = derivative.T
    mats = [
        np.kron(np.kron(step, eye), eye),
        np.kron(np.kron(eye, step), eye),
        np.kron(np.kron(eye, eye), step),
    ]
    nodes = np.arange(64).reshape(4, 4, 4)
    faces = [nodes[0], nodes[3], nodes[:, 0], nodes[:, 3], nodes[:, :, 0], nodes[:, :, 3]]
    for ids in faces:
        diag = np.zeros((64, 64))
        diag[ids.reshape(16), ids.reshape(16)] = 1.0
        mats.append(diag)
    mats = [0.1 * np.concatenate([m, m], axis=1) for m in mats]
    mats.append(np.repeat(node_weight[:, None], 128, axis=1))
    return jnp.asarray(np.stack(mats), F32)


def split2(x):
    hi = x.astype(BF)
    return hi, (x - hi.astype(F32)).astype(BF)


def dot(a, b):
    return jnp.dot(a, b, preferred_element_type=F32)


def dot_nt(a, b):
    return lax.dot_general(a, b, (((1,), (1,)), ((), ())), preferred_element_type=F32)


def one_hot(mask):
    return jnp.where(mask, 1.0, 0.0).astype(BF)


def add_face(ref, tile, face, part):
    low = lax.broadcasted_iota(jnp.int32, (8, 128), 0) < 4
    for c in range(5):
        rows = part[16 * c : 16 * c + 16]
        if face < 2:
            ids = pl.ds(48 * face, 16)
            ref[tile, c, ids, :] = ref[tile, c, ids, :] + rows
        elif face >= 4:
            ids = pl.ds(3 * (face - 4), 16, stride=4)
            ref[tile, c, ids, :] = ref[tile, c, ids, :] + rows
        else:
            for v in range(2):
                both = rows[8 * v : 8 * v + 8]
                turned = pltpu.roll(both, 4, 0)
                for k in range(2):
                    ids = pl.ds(32 * v + 16 * k + 8 * (face - 2), 8)
                    value = both if k == face - 2 else turned
                    mask = low if face == 2 else jnp.logical_not(low)
                    ref[tile, c, ids, :] = ref[tile, c, ids, :] + jnp.where(mask, value, 0.0)


def face_rows(ref, tile, c, face):
    if face < 2:
        return ref[tile, c, 48 * face : 48 * face + 16, :]
    if face >= 4:
        return ref[tile, c, pl.ds(3 * (face - 4), 16, stride=4), :]
    low = lax.broadcasted_iota(jnp.int32, (8, 128), 0) < 4
    out = []
    for v in range(2):
        first = ref[tile, c, 32 * v + 8 * (face - 2) : 32 * v + 8 * (face - 2) + 8, :]
        second = ref[tile, c, 32 * v + 16 + 8 * (face - 2) : 32 * v + 24 + 8 * (face - 2), :]
        if face == 2:
            out.append(jnp.where(low, first, pltpu.roll(second, 4, 0)))
        else:
            out.append(jnp.where(low, pltpu.roll(first, 4, 0), second))
    return jnp.concatenate(out, axis=0)


def exchange(sectors, slabs, owned, *refs):
    hbm_refs = refs[:INPUTS]
    acc_ref, recv_ref, oh_ref, grad_ref = refs[INPUTS : INPUTS + 4]
    x_ref = refs[INPUTS + 4]
    vmem_refs = (None,) + refs[INPUTS + 5 : 2 * INPUTS + 4]
    (
        _,
        vel_ref,
        drag_ref,
        bw_ref,
        jac_ref,
        own_ref,
        nbrmat_ref,
        nbr_ref,
        sslots_ref,
        aslots_ref,
        live_ref,
        eb_ref,
        mats_ref,
    ) = vmem_refs
    (
        xs_ref,
        tr_ref,
        send_ref,
        a_ref,
        b_ref,
        bsend_ref,
        brecv_ref,
        send_sem,
        recv_sem,
        load_sem,
        x_sem,
    ) = refs[2 * INPUTS + 4 :]
    tiles = x_ref.shape[0]
    elems = tiles * 128
    slots = sslots_ref.shape[1]
    width = bsend_ref.shape[2]
    count = sectors * slabs

    loads = {
        k: pltpu.make_async_copy(hbm_refs[k], vmem_refs[k], load_sem.at[k])
        for k in range(1, INPUTS)
    }
    fields = {
        (t, h): pltpu.make_async_copy(
            hbm_refs[0].at[h, :, pl.ds(128 * t, 128)], x_ref.at[t, h], x_sem.at[5 * t + h]
        )
        for t in range(tiles)
        for h in range(5)
    }
    for k in (8, 9, 10, 6):
        loads[k].start()
    for key in fields:
        fields[key].start()
    for k in (1, 2, 3, 11, 12, 4, 5, 7):
        loads[k].start()

    sec = lax.axis_index("sector")
    axi = lax.axis_index("axial")
    joint = sec * slabs + axi
    prev = lax.rem(joint + count - 1, count)
    nxt = lax.rem(joint + 1, count)
    dev_prev = (prev // slabs, lax.rem(prev, slabs))
    dev_next = (nxt // slabs, lax.rem(nxt, slabs))
    dev_low = (lax.rem(sec + sectors - 1, sectors), axi)
    dev_high = (lax.rem(sec + 1, sectors), axi)

    barrier = pltpu.get_barrier_semaphore()
    for device in (dev_prev, dev_next, dev_low, dev_high):
        pl.semaphore_signal(barrier, inc=1, device_id=device, device_id_type=MESH)

    for k in (8, 9, 10, 6):
        loads[k].wait()
    slot_ids = lax.broadcasted_iota(jnp.int32, (1, slots), 1)
    rows_slots = lax.broadcasted_iota(jnp.int32, (elems, slots), 0)
    for i in range(4):
        row = i % 2
        ids = (sslots_ref if i < 2 else aslots_ref)[row : row + 1, :]
        if i < 2:
            ids = jnp.where(slot_ids < live_ref[:, row : row + 1], ids, -1)
        oh_ref[i] = one_hot(rows_slots == ids)

    lane = lax.broadcasted_iota(jnp.int32, (6, 256), 1)
    field = lane % 80 // 16
    diagonal = lax.broadcasted_iota(jnp.int32, (16, 256), 1)
    diagonal = diagonal % 16 == lax.broadcasted_iota(jnp.int32, (16, 256), 0)
    for c in range(5):
        value = jnp.where(field == 0, nbrmat_ref[c][:, 0:1], 0.0)
        for h in range(1, 5):
            value = jnp.where(field == h, nbrmat_ref[c][:, h : h + 1], value)
        value = 0.1 * value
        hi = value.astype(BF).astype(F32)
        value = jnp.where(lane < 160, hi, value - hi)
        for f in range(6):
            b_ref[f, 16 * c : 16 * c + 16, :] = jnp.where(
                diagonal, value[f : f + 1, :], 0.0
            ).astype(BF)

    def take_trace(t, face):
        lanes = slice(128 * t, 128 * t + 128)
        for c in range(5):
            hi, lo = split2(face_rows(x_ref, t, c, face))
            tr_ref[face, 16 * c : 16 * c + 16, lanes] = hi
            tr_ref[face, 80 + 16 * c : 96 + 16 * c, lanes] = lo

    for t in range(tiles):
        for h in range(5):
            fields[t, h].wait()
        for face in SIDES:
            take_trace(t, face)

    def through(face, both):
        hi, lo = both[:80].astype(BF), both[80:].astype(BF)
        return dot(b_ref[face, :, 0:240], jnp.concatenate([hi, lo, hi], axis=0))

    for i, face in enumerate(SIDES):
        send_ref[i] = through(face + 1 - 2 * (face % 2), dot(tr_ref[face], oh_ref[i]))

    pl.semaphore_wait(barrier, 4)

    def remote(src, dst, k, device):
        return pltpu.make_async_remote_copy(
            src_ref=src,
            dst_ref=dst,
            send_sem=send_sem.at[k],
            recv_sem=recv_sem.at[k],
            device_id=device,
            device_id_type=MESH,
        )

    up_x = remote(send_ref.at[1], recv_ref.at[0], 0, dev_high)
    down_x = remote(send_ref.at[0], recv_ref.at[1], 1, dev_low)
    up_z = remote(send_ref.at[3], recv_ref.at[2], 2, dev_next)
    down_z = remote(send_ref.at[2], recv_ref.at[3], 3, dev_prev)
    up_b = remote(bsend_ref.at[2], brecv_ref.at[0], 4, dev_next)
    down_b = remote(bsend_ref.at[0], brecv_ref.at[1], 5, dev_prev)
    has_low = axi > 0
    has_high = axi < slabs - 1
    up_x.start()
    down_x.start()

    @pl.when(has_high)
    def _():
        up_z.start()

    @pl.when(has_low)
    def _():
        down_z.start()

    @pl.when(jnp.logical_not(has_low))
    def _():
        recv_ref[2] = jnp.zeros((80, slots), F32)

    @pl.when(jnp.logical_not(has_high))
    def _():
        recv_ref[3] = jnp.zeros((80, slots), F32)

    for k in (1, 2, 3, 11, 12):
        loads[k].wait()
    parts = []
    for t in range(tiles):
        lanes = slice(128 * t, 128 * t + 128)
        total = x_ref[t, 1] * vel_ref[0, :, lanes].astype(F32)
        total += x_ref[t, 2] * vel_ref[1, :, lanes].astype(F32)
        total += x_ref[t, 3] * vel_ref[2, :, lanes].astype(F32)
        parts.append(jnp.sum(total * mats_ref[9], axis=0, keepdims=True))
    elem_grad = drag_ref[...] * jnp.concatenate(parts, axis=1)
    weighted = bw_ref[...] * elem_grad
    w1 = weighted.astype(BF)
    rest = weighted - w1.astype(F32)
    w2 = rest.astype(BF)
    w3 = (rest - w2.astype(F32)).astype(BF).astype(F32)
    row16 = lax.broadcasted_iota(jnp.int32, (16, elems), 0)
    stack = jnp.where(row16 == 0, w1.astype(F32), 0.0)
    stack = jnp.where(row16 == 1, w2.astype(F32), stack)
    stack = jnp.where(row16 == 2, w3, stack).astype(BF)
    rel = eb_ref[...] - (joint - 1) * owned
    rel = jnp.where(rel < 0, rel + BLOCKS, rel)
    rel = jnp.where(rel >= BLOCKS, rel - BLOCKS, rel)
    rows_blk = lax.broadcasted_iota(jnp.int32, (width, elems), 0)
    for j in range(3):
        sums = dot_nt(stack, one_hot(rows_blk == rel - j * owned))
        total = jnp.sum(sums, axis=0, keepdims=True)
        bsend_ref[j] = jnp.broadcast_to(total, (8, width))
    up_b.start()
    down_b.start()

    for k in (4, 5):
        loads[k].wait()
    spread = jnp.minimum(lax.broadcasted_iota(jnp.int32, (5, 384), 1) // 64, 4)
    spread = jnp.where(spread == lax.broadcasted_iota(jnp.int32, (5, 384), 0), 1.0, 0.0)
    for c in range(5):
        rows = slice(64 * c, 64 * c + 64)
        jac = jac_ref[0][:, c : c + 1] * spread[0:1, :]
        face = own_ref[c][:, 0:1] * spread[0:1, :]
        for h in range(1, 5):
            jac += jac_ref[h][:, c : c + 1] * spread[h : h + 1, :]
            face += own_ref[c][:, h : h + 1] * spread[h : h + 1, :]
        for t in range(3):
            lanes = slice(128 * t, 128 * t + 128)
            total = mats_ref[0] * jac[0:1, lanes]
            for j in range(1, 9):
                row = jac[j : j + 1, lanes] if j < 3 else face[j - 3 : j - 2, lanes]
                total += mats_ref[j] * row
            hi, lo = split2(total)
            places = ((768, hi), (896, lo)) if t == 2 else ((0, hi), (256, hi), (512, lo))
            for base, part in places:
                base += 128 * t if t < 2 else 0
                a_ref[rows, base : base + 128] = part

    for t in range(tiles):
        lanes = slice(128 * t, 128 * t + 128)
        for h in range(5):
            hi, lo = split2(x_ref[t, h])
            places = ((768, hi), (832, lo), (896, hi))
            if h < 4:
                places = ((64 * h, hi), (256 + 64 * h, lo), (512 + 64 * h, hi))
            for base, part in places:
                xs_ref[base : base + 64, lanes] = part
        for face in (2, 3):
            take_trace(t, face)

    own = dot(a_ref[:, 0:960], xs_ref[...])
    keep = 1.0 - 0.1 * drag_ref[...]
    for t in range(tiles):
        lanes = slice(128 * t, 128 * t + 128)
        for c in range(5):
            x = x_ref[t, c]
            scaled = x * keep[:, lanes] if 1 <= c <= 3 else x
            acc_ref[t, c] = scaled + own[64 * c : 64 * c + 64, lanes]

    loads[7].wait()
    chunk = 256
    rows_src = lax.broadcasted_iota(jnp.int32, (chunk, elems), 0)
    for f in range(6):
        ids = nbr_ref[f : f + 1, :]
        g = f + 1 - 2 * (f % 2)
        both = jnp.zeros((160, elems), F32)
        for k in range(elems // chunk):
            hot = one_hot(rows_src == ids - k * chunk)
            both += dot(tr_ref[g, :, k * chunk : (k + 1) * chunk], hot)
        part = through(f, both)
        for t in range(tiles):
            add_face(acc_ref, t, f, part[:, 128 * t : 128 * t + 128])

    up_b.wait()
    down_b.wait()
    grad_ref[...] = bsend_ref[1] + brecv_ref[0] + brecv_ref[1]

    up_x.wait()
    down_x.wait()

    @pl.when(has_high)
    def _():
        up_z.wait_send()
        down_z.wait_recv()

    @pl.when(has_low)
    def _():
        down_z.wait_send()
        up_z.wait_recv()


def finish(acc_ref, recv_ref, oh_ref, sums_ref, out_ref, grad_ref, o_ref, g_ref, sem):
    tiles = acc_ref.shape[0]
    g_ref[...] = sums_ref[0, : g_ref.shape[0]]
    grad_copy = pltpu.make_async_copy(g_ref, grad_ref, sem.at[tiles])
    grad_copy.start()
    copies = []
    halves = [jnp.concatenate(split2(recv_ref[i]), axis=0) for i in range(4)]
    for first in range(0, tiles, 2):
        for t in (first, first + 1):
            o_ref[t] = acc_ref[t]
        for i, face in enumerate(SIDES):
            both = dot_nt(halves[i], oh_ref[i, 128 * first : 128 * first + 256, :])
            part = both[:80] + both[80:]
            for k in range(2):
                add_face(o_ref, first + k, face, part[:, 128 * k : 128 * k + 128])
        for t in (first, first + 1):
            copy = pltpu.make_async_copy(
                o_ref.at[t], out_ref.at[:, :, pl.ds(128 * t, 128)], sem.at[t]
            )
            copy.start()
            copies.append(copy)
    for copy in copies:
        copy.wait()
    grad_copy.wait()


def on_device(
    sectors,
    slabs,
    adjoint,
    velocity,
    drag,
    block_weight,
    flux_jac,
    face_own,
    face_nbr,
    nbr_local,
    sector_slots,
    axial_slots,
    sector_live,
    elem_block,
):
    elems = adjoint.shape[2]
    tiles = elems // 128
    slots = sector_slots.shape[1]
    owned = BLOCKS // (sectors * slabs)
    width = -(-owned // 128) * 128
    operands = (
        adjoint,
        velocity,
        drag.reshape(1, elems),
        block_weight.reshape(1, elems),
        jnp.transpose(flux_jac, (1, 0, 2)),
        jnp.transpose(face_own, (1, 0, 2)),
        jnp.transpose(face_nbr, (1, 0, 2)),
        nbr_local,
        sector_slots,
        axial_slots,
        sector_live.reshape(1, 2),
        elem_block.reshape(1, elems),
        constant_tables(),
    )
    vmem = pl.BlockSpec(memory_space=pltpu.VMEM)
    hbm = pl.BlockSpec(memory_space=pltpu.HBM)
    handed = pl.pallas_call(
        functools.partial(exchange, sectors, slabs, owned),
        out_shape=(
            pltpu.VMEM((tiles, 5, 64, 128), F32),
            pltpu.VMEM((4, 80, slots), F32),
            pltpu.VMEM((4, elems, slots), BF),
            pltpu.VMEM((8, width), F32),
        ),
        in_specs=[hbm] * INPUTS,
        out_specs=(vmem,) * 4,
        scratch_shapes=[pltpu.VMEM((tiles, 5, 64, 128), F32)]
        + [pltpu.VMEM(a.shape, a.dtype) for a in operands[1:]]
        + [
            pltpu.VMEM((960, elems), BF),
            pltpu.VMEM((6, 160, elems), BF),
            pltpu.VMEM((4, 80, slots), F32),
            pltpu.VMEM((320, 1024), BF),
            pltpu.VMEM((6, 80, 256), BF),
            pltpu.VMEM((3, 8, width), F32),
            pltpu.VMEM((2, 8, width), F32),
            pltpu.SemaphoreType.DMA((6,)),
            pltpu.SemaphoreType.DMA((6,)),
            pltpu.SemaphoreType.DMA((INPUTS,)),
            pltpu.SemaphoreType.DMA((5 * tiles,)),
        ],
        compiler_params=pltpu.CompilerParams(
            collective_id=0, has_side_effects=True, vmem_limit_bytes=60 * 1024 * 1024
        ),
    )(*operands)
    return pl.pallas_call(
        finish,
        out_shape=(
            jax.ShapeDtypeStruct(adjoint.shape, F32),
            jax.ShapeDtypeStruct((owned,), F32),
        ),
        in_specs=[vmem] * 4,
        out_specs=(hbm, hbm),
        scratch_shapes=[
            pltpu.VMEM((tiles, 5, 64, 128), F32),
            pltpu.VMEM((owned,), F32),
            pltpu.SemaphoreType.DMA((tiles + 1,)),
        ],
        compiler_params=pltpu.CompilerParams(vmem_limit_bytes=40 * 1024 * 1024),
    )(*handed)


def solution(mesh):
    placed = (
        P(None, None, ("sector", "axial")),
        P(None, None, ("sector", "axial")),
        P(("sector", "axial")),
        P(("sector", "axial")),
        P(),
        P(),
        P(),
        P(None, ("sector", "axial")),
        P(None, ("sector", "axial")),
        P(None, ("sector", "axial")),
        P("sector", "axial", None),
        P(("sector", "axial")),
    )
    return jax.shard_map(
        functools.partial(on_device, mesh.shape["sector"], mesh.shape["axial"]),
        mesh=mesh,
        in_specs=placed,
        out_specs=(P(None, None, ("sector", "axial")), P(("sector", "axial"))),
        check_vma=False,
    )
```

```python
import functools

import jax
import jax.numpy as jnp
import numpy as np
from jax import lax
from jax.experimental import pallas as pl
from jax.experimental.pallas import tpu as pltpu
from jax.sharding import PartitionSpec as P

BLOCKS = 4096
BF = jnp.bfloat16
F32 = jnp.float32
MESH = pl.DeviceIdType.MESH
INPUTS = 13
SIDES = (0, 1, 4, 5)


def lobatto_tables():
    points = np.array([-1.0, -1.0 / np.sqrt(5.0), 1.0 / np.sqrt(5.0), 1.0])
    weights = np.array([1.0, 5.0, 5.0, 1.0]) / 6.0
    scales = np.array(
        [np.prod([points[i] - points[k] for k in range(4) if k != i]) for i in range(4)]
    )
    derivative = np.zeros((4, 4))
    for i in range(4):
        for p in range(4):
            if i != p:
                derivative[i, p] = scales[i] / scales[p] / (points[i] - points[p])
            else:
                derivative[i, p] = sum((1.0 / (points[i] - points[k]) for k in range(4) if k != i))
    node_weight = (
        weights[:, None, None] * weights[None, :, None] * weights[None, None, :]
    ).reshape(64) / 8.0
    return (derivative, node_weight)


def constant_tables():
    derivative, node_weight = lobatto_tables()
    eye = np.eye(4)
    step = derivative.T
    mats = [
        np.kron(np.kron(step, eye), eye),
        np.kron(np.kron(eye, step), eye),
        np.kron(np.kron(eye, eye), step),
    ]
    nodes = np.arange(64).reshape(4, 4, 4)
    faces = [nodes[0], nodes[3], nodes[:, 0], nodes[:, 3], nodes[:, :, 0], nodes[:, :, 3]]
    for ids in faces:
        diag = np.zeros((64, 64))
        diag[ids.reshape(16), ids.reshape(16)] = 1.0
        mats.append(diag)
    mats = [0.1 * np.concatenate([m, m], axis=1) for m in mats]
    mats.append(np.repeat(node_weight[:, None], 128, axis=1))
    return jnp.asarray(np.stack(mats), F32)


def split2(x):
    hi = x.astype(BF)
    return hi, (x - hi.astype(F32)).astype(BF)


def dot(a, b):
    return jnp.dot(a, b, preferred_element_type=F32)


def dot_nt(a, b):
    return lax.dot_general(a, b, (((1,), (1,)), ((), ())), preferred_element_type=F32)


def one_hot(mask):
    return jnp.where(mask, jnp.ones((), BF), jnp.zeros((), BF))


def add_face(ref, tile, face, part):
    low = lax.broadcasted_iota(jnp.int32, (8, 128), 0) < 4
    for c in range(5):
        rows = part[c]
        if face < 2:
            ids = pl.ds(48 * face, 16)
            ref[tile, c, ids, :] = ref[tile, c, ids, :] + rows
        elif face >= 4:
            ids = pl.ds(3 * (face - 4), 16, stride=4)
            ref[tile, c, ids, :] = ref[tile, c, ids, :] + rows
        else:
            for v in range(2):
                both = rows[8 * v : 8 * v + 8]
                turned = pltpu.roll(both, 4, 0)
                for k in range(2):
                    ids = pl.ds(32 * v + 16 * k + 8 * (face - 2), 8)
                    value = both if k == face - 2 else turned
                    mask = low if face == 2 else jnp.logical_not(low)
                    ref[tile, c, ids, :] = ref[tile, c, ids, :] + jnp.where(mask, value, 0.0)


def mixed(coef_ref, face, c, parts):
    total = coef_ref[5 * c, face : face + 1, :] * parts[0]
    for h in range(1, 5):
        total += coef_ref[5 * c + h, face : face + 1, :] * parts[h]
    return total


def face_rows(ref, tile, c, face):
    if face < 2:
        return ref[tile, c, 48 * face : 48 * face + 16, :]
    if face >= 4:
        return ref[tile, c, pl.ds(3 * (face - 4), 16, stride=4), :]
    low = lax.broadcasted_iota(jnp.int32, (8, 128), 0) < 4
    out = []
    for v in range(2):
        first = ref[tile, c, 32 * v + 8 * (face - 2) : 32 * v + 8 * (face - 2) + 8, :]
        second = ref[tile, c, 32 * v + 16 + 8 * (face - 2) : 32 * v + 24 + 8 * (face - 2), :]
        if face == 2:
            out.append(jnp.where(low, first, pltpu.roll(second, 4, 0)))
        else:
            out.append(jnp.where(low, pltpu.roll(first, 4, 0), second))
    return jnp.concatenate(out, axis=0)


def exchange(sectors, slabs, owned, *refs):
    hbm_refs = refs[:INPUTS]
    acc_ref, recv_ref, oh_ref, grad_ref = refs[INPUTS : INPUTS + 4]
    x_ref = refs[INPUTS + 4]
    vmem_refs = (None,) + refs[INPUTS + 5 : 2 * INPUTS + 4]
    (
        _,
        vel_ref,
        drag_ref,
        bw_ref,
        jac_ref,
        own_ref,
        nbrmat_ref,
        nbr_ref,
        sslots_ref,
        aslots_ref,
        live_ref,
        eb_ref,
        mats_ref,
    ) = vmem_refs
    (
        xs_ref,
        tr_ref,
        send_ref,
        a_ref,
        coef_ref,
        bsend_ref,
        brecv_ref,
        send_sem,
        recv_sem,
        load_sem,
        x_sem,
    ) = refs[2 * INPUTS + 4 :]
    tiles = x_ref.shape[0]
    elems = tiles * 128
    slots = sslots_ref.shape[1]
    width = bsend_ref.shape[2]
    count = sectors * slabs

    loads = {
        k: pltpu.make_async_copy(hbm_refs[k], vmem_refs[k], load_sem.at[k])
        for k in range(1, INPUTS)
    }
    fields = {
        (t, h): pltpu.make_async_copy(
            hbm_refs[0].at[h, :, pl.ds(128 * t, 128)], x_ref.at[t, h], x_sem.at[5 * t + h]
        )
        for t in range(tiles)
        for h in range(5)
    }
    for k in (8, 9, 10, 6):
        loads[k].start()
    for key in fields:
        fields[key].start()
    for k in (1, 2, 3, 11, 12, 4, 5, 7):
        loads[k].start()

    sec = lax.axis_index("sector")
    axi = lax.axis_index("axial")
    joint = sec * slabs + axi
    prev = lax.rem(joint + count - 1, count)
    nxt = lax.rem(joint + 1, count)
    dev_prev = (prev // slabs, lax.rem(prev, slabs))
    dev_next = (nxt // slabs, lax.rem(nxt, slabs))
    dev_low = (lax.rem(sec + sectors - 1, sectors), axi)
    dev_high = (lax.rem(sec + 1, sectors), axi)

    barrier = pltpu.get_barrier_semaphore()
    for device in (dev_prev, dev_next, dev_low, dev_high):
        pl.semaphore_signal(barrier, inc=1, device_id=device, device_id_type=MESH)

    for k in (8, 9, 10, 6):
        loads[k].wait()
    slot_ids = lax.broadcasted_iota(jnp.int32, (1, slots), 1)
    rows_slots = lax.broadcasted_iota(jnp.int32, (elems, slots), 0).astype(jnp.int16)
    for i in range(4):
        row = i % 2
        ids = (sslots_ref if i < 2 else aslots_ref)[row : row + 1, :]
        if i < 2:
            ids = jnp.where(slot_ids < live_ref[:, row : row + 1], ids, -1)
        ids = jnp.broadcast_to(ids, (elems, slots)).astype(jnp.int16)
        oh_ref[i] = one_hot(rows_slots == ids)

    for c in range(5):
        for h in range(5):
            coef_ref[5 * c + h] = jnp.broadcast_to(0.1 * nbrmat_ref[c][:, h : h + 1], (6, 128))

    def take_trace(t, face):
        lanes = slice(128 * t, 128 * t + 128)
        for c in range(5):
            hi, lo = split2(face_rows(x_ref, t, c, face))
            tr_ref[face, 16 * c : 16 * c + 16, lanes] = hi
            tr_ref[face, 80 + 16 * c : 96 + 16 * c, lanes] = lo

    for key in fields:
        fields[key].wait()
    for t in range(tiles):
        for face in SIDES:
            take_trace(t, face)

    for i, face in enumerate(SIDES):
        both = dot(tr_ref[face], oh_ref[i])
        both = both[:80] + both[80:]
        for n in range(0, slots, 128):
            parts = [both[16 * h : 16 * h + 16, n : n + 128] for h in range(5)]
            for c in range(5):
                value = mixed(coef_ref, face + 1 - 2 * (face % 2), c, parts)
                send_ref[i, 16 * c : 16 * c + 16, n : n + 128] = value

    pl.semaphore_wait(barrier, 4)

    def remote(src, dst, k, device):
        return pltpu.make_async_remote_copy(
            src_ref=src,
            dst_ref=dst,
            send_sem=send_sem.at[k],
            recv_sem=recv_sem.at[k],
            device_id=device,
            device_id_type=MESH,
        )

    up_x = remote(send_ref.at[1], recv_ref.at[0], 0, dev_high)
    down_x = remote(send_ref.at[0], recv_ref.at[1], 1, dev_low)
    up_z = remote(send_ref.at[3], recv_ref.at[2], 2, dev_next)
    down_z = remote(send_ref.at[2], recv_ref.at[3], 3, dev_prev)
    up_b = remote(bsend_ref.at[2], brecv_ref.at[0], 4, dev_next)
    down_b = remote(bsend_ref.at[0], brecv_ref.at[1], 5, dev_prev)
    has_low = axi > 0
    has_high = axi < slabs - 1
    up_x.start()
    down_x.start()

    @pl.when(has_high)
    def _():
        up_z.start()

    @pl.when(has_low)
    def _():
        down_z.start()

    @pl.when(jnp.logical_not(has_low))
    def _():
        recv_ref[2] = jnp.zeros((80, slots), F32)

    @pl.when(jnp.logical_not(has_high))
    def _():
        recv_ref[3] = jnp.zeros((80, slots), F32)

    for k in (1, 2, 3, 11, 12):
        loads[k].wait()
    parts = []
    for t in range(tiles):
        lanes = slice(128 * t, 128 * t + 128)
        total = x_ref[t, 1] * vel_ref[0, :, lanes].astype(F32)
        total += x_ref[t, 2] * vel_ref[1, :, lanes].astype(F32)
        total += x_ref[t, 3] * vel_ref[2, :, lanes].astype(F32)
        parts.append(jnp.sum(total * mats_ref[9], axis=0, keepdims=True))
    elem_grad = drag_ref[...] * jnp.concatenate(parts, axis=1)
    weighted = bw_ref[...] * elem_grad
    w1 = weighted.astype(BF)
    rest = weighted - w1.astype(F32)
    w2 = rest.astype(BF)
    w3 = (rest - w2.astype(F32)).astype(BF).astype(F32)
    row16 = lax.broadcasted_iota(jnp.int32, (16, elems), 0)
    stack = jnp.where(row16 == 0, w1.astype(F32), 0.0)
    stack = jnp.where(row16 == 1, w2.astype(F32), stack)
    stack = jnp.where(row16 == 2, w3, stack).astype(BF)
    rel = eb_ref[...] - (joint - 1) * owned
    rel = jnp.where(rel < 0, rel + BLOCKS, rel)
    rel = jnp.where(rel >= BLOCKS, rel - BLOCKS, rel)
    rows_blk = lax.broadcasted_iota(jnp.int32, (width, elems), 0).astype(jnp.int16)
    for j in range(3):
        ids = jnp.broadcast_to(rel - j * owned, (width, elems)).astype(jnp.int16)
        sums = dot_nt(stack, one_hot(rows_blk == ids))
        total = jnp.sum(sums, axis=0, keepdims=True)
        bsend_ref[j] = jnp.broadcast_to(total, (8, width))
    up_b.start()
    down_b.start()

    for k in (4, 5):
        loads[k].wait()
    spread = jnp.minimum(lax.broadcasted_iota(jnp.int32, (5, 384), 1) // 64, 4)
    spread = jnp.where(spread == lax.broadcasted_iota(jnp.int32, (5, 384), 0), 1.0, 0.0)
    for c in range(5):
        rows = slice(64 * c, 64 * c + 64)
        jac = jac_ref[0][:, c : c + 1] * spread[0:1, :]
        face = own_ref[c][:, 0:1] * spread[0:1, :]
        for h in range(1, 5):
            jac += jac_ref[h][:, c : c + 1] * spread[h : h + 1, :]
            face += own_ref[c][:, h : h + 1] * spread[h : h + 1, :]
        for t in range(3):
            lanes = slice(128 * t, 128 * t + 128)
            total = mats_ref[0] * jac[0:1, lanes]
            for j in range(1, 9):
                row = jac[j : j + 1, lanes] if j < 3 else face[j - 3 : j - 2, lanes]
                total += mats_ref[j] * row
            hi, lo = split2(total)
            places = ((768, hi), (896, lo)) if t == 2 else ((0, hi), (256, hi), (512, lo))
            for base, part in places:
                base += 128 * t if t < 2 else 0
                a_ref[rows, base : base + 128] = part

    for t in range(tiles):
        lanes = slice(128 * t, 128 * t + 128)
        for h in range(5):
            hi, lo = split2(x_ref[t, h])
            places = ((768, hi), (832, lo), (896, hi))
            if h < 4:
                places = ((64 * h, hi), (256 + 64 * h, lo), (512 + 64 * h, hi))
            for base, part in places:
                xs_ref[base : base + 64, lanes] = part
        for face in (2, 3):
            take_trace(t, face)

    own = dot(a_ref[:, 0:960], xs_ref[...])
    keep = 1.0 - 0.1 * drag_ref[...]
    for t in range(tiles):
        lanes = slice(128 * t, 128 * t + 128)
        for c in range(5):
            x = x_ref[t, c]
            scaled = x * keep[:, lanes] if 1 <= c <= 3 else x
            acc_ref[t, c] = scaled + own[64 * c : 64 * c + 64, lanes]

    loads[7].wait()
    rows_src = lax.broadcasted_iota(jnp.int32, (elems, elems), 0).astype(jnp.int16)
    for f in range(6):
        g = f + 1 - 2 * (f % 2)
        ids = jnp.broadcast_to(nbr_ref[f : f + 1, :], (elems, elems)).astype(jnp.int16)
        both = dot(tr_ref[g], one_hot(rows_src == ids))
        both = both[:80] + both[80:]
        for t in range(tiles):
            parts = [both[16 * h : 16 * h + 16, 128 * t : 128 * t + 128] for h in range(5)]
            add_face(acc_ref, t, f, [mixed(coef_ref, f, c, parts) for c in range(5)])

    up_b.wait()
    down_b.wait()
    grad_ref[...] = bsend_ref[1] + brecv_ref[0] + brecv_ref[1]

    up_x.wait()
    down_x.wait()

    @pl.when(has_high)
    def _():
        up_z.wait_send()
        down_z.wait_recv()

    @pl.when(has_low)
    def _():
        down_z.wait_send()
        up_z.wait_recv()


def finish(acc_ref, recv_ref, oh_ref, sums_ref, out_ref, grad_ref, o_ref, g_ref, sem):
    tiles = acc_ref.shape[0]
    g_ref[...] = sums_ref[0, : g_ref.shape[0]]
    grad_copy = pltpu.make_async_copy(g_ref, grad_ref, sem.at[tiles])
    grad_copy.start()
    copies = []
    halves = [jnp.concatenate(split2(recv_ref[i]), axis=0) for i in range(4)]
    for first in range(0, tiles, 2):
        for t in (first, first + 1):
            o_ref[t] = acc_ref[t]
        for i, face in enumerate(SIDES):
            both = dot_nt(halves[i], oh_ref[i, 128 * first : 128 * first + 256, :])
            part = both[:80] + both[80:]
            for k in range(2):
                lanes = slice(128 * k, 128 * k + 128)
                rows = [part[16 * c : 16 * c + 16, lanes] for c in range(5)]
                add_face(o_ref, first + k, face, rows)
        for t in (first, first + 1):
            copy = pltpu.make_async_copy(
                o_ref.at[t], out_ref.at[:, :, pl.ds(128 * t, 128)], sem.at[t]
            )
            copy.start()
            copies.append(copy)
    for copy in copies:
        copy.wait()
    grad_copy.wait()


def on_device(
    sectors,
    slabs,
    adjoint,
    velocity,
    drag,
    block_weight,
    flux_jac,
    face_own,
    face_nbr,
    nbr_local,
    sector_slots,
    axial_slots,
    sector_live,
    elem_block,
):
    elems = adjoint.shape[2]
    tiles = elems // 128
    slots = sector_slots.shape[1]
    owned = BLOCKS // (sectors * slabs)
    width = -(-owned // 128) * 128
    operands = (
        adjoint,
        velocity,
        drag.reshape(1, elems),
        block_weight.reshape(1, elems),
        jnp.transpose(flux_jac, (1, 0, 2)),
        jnp.transpose(face_own, (1, 0, 2)),
        jnp.transpose(face_nbr, (1, 0, 2)),
        nbr_local,
        sector_slots,
        axial_slots,
        sector_live.reshape(1, 2),
        elem_block.reshape(1, elems),
        constant_tables(),
    )
    vmem = pl.BlockSpec(memory_space=pltpu.VMEM)
    hbm = pl.BlockSpec(memory_space=pltpu.HBM)
    handed = pl.pallas_call(
        functools.partial(exchange, sectors, slabs, owned),
        out_shape=(
            pltpu.VMEM((tiles, 5, 64, 128), F32),
            pltpu.VMEM((4, 80, slots), F32),
            pltpu.VMEM((4, elems, slots), BF),
            pltpu.VMEM((8, width), F32),
        ),
        in_specs=[hbm] * INPUTS,
        out_specs=(vmem,) * 4,
        scratch_shapes=[pltpu.VMEM((tiles, 5, 64, 128), F32)]
        + [pltpu.VMEM(a.shape, a.dtype) for a in operands[1:]]
        + [
            pltpu.VMEM((960, elems), BF),
            pltpu.VMEM((6, 160, elems), BF),
            pltpu.VMEM((4, 80, slots), F32),
            pltpu.VMEM((320, 1024), BF),
            pltpu.VMEM((25, 6, 128), F32),
            pltpu.VMEM((3, 8, width), F32),
            pltpu.VMEM((2, 8, width), F32),
            pltpu.SemaphoreType.DMA((6,)),
            pltpu.SemaphoreType.DMA((6,)),
            pltpu.SemaphoreType.DMA((INPUTS,)),
            pltpu.SemaphoreType.DMA((5 * tiles,)),
        ],
        compiler_params=pltpu.CompilerParams(
            collective_id=0, has_side_effects=True, vmem_limit_bytes=60 * 1024 * 1024
        ),
    )(*operands)
    return pl.pallas_call(
        finish,
        out_shape=(
            jax.ShapeDtypeStruct(adjoint.shape, F32),
            jax.ShapeDtypeStruct((owned,), F32),
        ),
        in_specs=[vmem] * 4,
        out_specs=(hbm, hbm),
        scratch_shapes=[
            pltpu.VMEM((tiles, 5, 64, 128), F32),
            pltpu.VMEM((owned,), F32),
            pltpu.SemaphoreType.DMA((tiles + 1,)),
        ],
        compiler_params=pltpu.CompilerParams(vmem_limit_bytes=40 * 1024 * 1024),
    )(*handed)


def solution(mesh):
    placed = (
        P(None, None, ("sector", "axial")),
        P(None, None, ("sector", "axial")),
        P(("sector", "axial")),
        P(("sector", "axial")),
        P(),
        P(),
        P(),
        P(None, ("sector", "axial")),
        P(None, ("sector", "axial")),
        P(None, ("sector", "axial")),
        P("sector", "axial", None),
        P(("sector", "axial")),
    )
    return jax.shard_map(
        functools.partial(on_device, mesh.shape["sector"], mesh.shape["axial"]),
        mesh=mesh,
        in_specs=placed,
        out_specs=(P(None, None, ("sector", "axial")), P(("sector", "axial"))),
        check_vma=False,
    )
```

```python
import functools

import jax
import jax.numpy as jnp
import numpy as np
from jax import lax
from jax.experimental import pallas as pl
from jax.experimental.pallas import tpu as pltpu
from jax.sharding import PartitionSpec as P

BLOCKS = 4096
BF = jnp.bfloat16
F32 = jnp.float32
MESH = pl.DeviceIdType.MESH
INPUTS = 14
SIDES = (0, 1, 4, 5)


def lobatto_tables():
    points = np.array([-1.0, -1.0 / np.sqrt(5.0), 1.0 / np.sqrt(5.0), 1.0])
    weights = np.array([1.0, 5.0, 5.0, 1.0]) / 6.0
    scales = np.array(
        [np.prod([points[i] - points[k] for k in range(4) if k != i]) for i in range(4)]
    )
    derivative = np.zeros((4, 4))
    for i in range(4):
        for p in range(4):
            if i != p:
                derivative[i, p] = scales[i] / scales[p] / (points[i] - points[p])
            else:
                derivative[i, p] = sum((1.0 / (points[i] - points[k]) for k in range(4) if k != i))
    node_weight = (
        weights[:, None, None] * weights[None, :, None] * weights[None, None, :]
    ).reshape(64) / 8.0
    return (derivative, node_weight)


def constant_tables():
    derivative, node_weight = lobatto_tables()
    eye = np.eye(4)
    step = derivative.T
    mats = [
        np.kron(np.kron(step, eye), eye),
        np.kron(np.kron(eye, step), eye),
        np.kron(np.kron(eye, eye), step),
    ]
    nodes = np.arange(64).reshape(4, 4, 4)
    faces = [nodes[0], nodes[3], nodes[:, 0], nodes[:, 3], nodes[:, :, 0], nodes[:, :, 3]]
    for ids in faces:
        diag = np.zeros((64, 64))
        diag[ids.reshape(16), ids.reshape(16)] = 1.0
        mats.append(diag)
    mats = [0.1 * np.concatenate([m, m], axis=1) for m in mats]
    weights = np.repeat(node_weight[:, None], 128, axis=1)
    return jnp.asarray(np.stack(mats), F32), jnp.asarray(weights, F32)


def split2(x):
    hi = x.astype(BF)
    return hi, (x - hi.astype(F32)).astype(BF)


def dot(a, b):
    return jnp.dot(a, b, preferred_element_type=F32)


def dot_nt(a, b):
    return lax.dot_general(a, b, (((1,), (1,)), ((), ())), preferred_element_type=F32)


def one_hot(mask):
    return jnp.where(mask, jnp.ones((), BF), jnp.zeros((), BF))


def add_face(ref, tile, face, part):
    low = lax.broadcasted_iota(jnp.int32, (8, 128), 0) < 4
    for c in range(5):
        rows = part[c]
        if face < 2:
            ids = pl.ds(48 * face, 16)
            ref[tile, c, ids, :] = ref[tile, c, ids, :] + rows
        elif face >= 4:
            ids = pl.ds(3 * (face - 4), 16, stride=4)
            ref[tile, c, ids, :] = ref[tile, c, ids, :] + rows
        else:
            for v in range(2):
                both = rows[8 * v : 8 * v + 8]
                turned = pltpu.roll(both, 4, 0)
                for k in range(2):
                    ids = pl.ds(32 * v + 16 * k + 8 * (face - 2), 8)
                    value = both if k == face - 2 else turned
                    mask = low if face == 2 else jnp.logical_not(low)
                    ref[tile, c, ids, :] = ref[tile, c, ids, :] + jnp.where(mask, value, 0.0)


def mixed(coef_ref, face, c, parts):
    total = coef_ref[5 * c, face : face + 1, :] * parts[0]
    for h in range(1, 5):
        total += coef_ref[5 * c + h, face : face + 1, :] * parts[h]
    return total


def face_rows(ref, tile, c, face):
    if face < 2:
        return ref[tile, c, 48 * face : 48 * face + 16, :]
    if face >= 4:
        return ref[tile, c, pl.ds(3 * (face - 4), 16, stride=4), :]
    low = lax.broadcasted_iota(jnp.int32, (8, 128), 0) < 4
    out = []
    for v in range(2):
        first = ref[tile, c, 32 * v + 8 * (face - 2) : 32 * v + 8 * (face - 2) + 8, :]
        second = ref[tile, c, 32 * v + 16 + 8 * (face - 2) : 32 * v + 24 + 8 * (face - 2), :]
        if face == 2:
            out.append(jnp.where(low, first, pltpu.roll(second, 4, 0)))
        else:
            out.append(jnp.where(low, pltpu.roll(first, 4, 0), second))
    return jnp.concatenate(out, axis=0)


def exchange(sectors, slabs, owned, *refs):
    hbm_refs = refs[:INPUTS]
    acc_ref, grad_ref = refs[INPUTS : INPUTS + 2]
    x_ref = refs[INPUTS + 2]
    vmem_refs = (None,) + refs[INPUTS + 3 : 2 * INPUTS + 2]
    (
        _,
        vel_ref,
        drag_ref,
        bw_ref,
        jac_ref,
        own_ref,
        nbrmat_ref,
        nbr_ref,
        sslots_ref,
        aslots_ref,
        live_ref,
        eb_ref,
        mats_ref,
        weight_ref,
    ) = vmem_refs
    (
        xs_ref,
        tr_ref,
        oh_ref,
        send_ref,
        recv_ref,
        a_ref,
        coef_ref,
        bsend_ref,
        brecv_ref,
        send_sem,
        recv_sem,
        far_sem,
        load_sem,
        x_sem,
    ) = refs[2 * INPUTS + 2 :]
    tiles = x_ref.shape[0]
    elems = tiles * 128
    slots = sslots_ref.shape[1]
    width = bsend_ref.shape[2]
    count = sectors * slabs

    loads = {
        k: pltpu.make_async_copy(hbm_refs[k], vmem_refs[k], load_sem.at[k])
        for k in range(1, INPUTS)
    }
    fields = {
        (t, h): pltpu.make_async_copy(
            hbm_refs[0].at[h, :, pl.ds(128 * t, 128)], x_ref.at[t, h], x_sem.at[5 * t + h]
        )
        for h in (1, 2, 3, 0, 4)
        for t in range(tiles)
    }
    for k in (1, 13, 2, 3, 11):
        loads[k].start()
    for key in fields:
        fields[key].start()
    for k in (8, 9, 10, 6, 7, 12, 4, 5):
        loads[k].start()

    sec = lax.axis_index("sector")
    axi = lax.axis_index("axial")
    joint = sec * slabs + axi
    prev = lax.rem(joint + count - 1, count)
    nxt = lax.rem(joint + 1, count)
    dev_prev = (prev // slabs, lax.rem(prev, slabs))
    dev_next = (nxt // slabs, lax.rem(nxt, slabs))
    dev_low = (lax.rem(sec + sectors - 1, sectors), axi)
    dev_high = (lax.rem(sec + 1, sectors), axi)

    has_low = axi > 0
    has_high = axi < slabs - 1

    barrier = pltpu.get_barrier_semaphore()

    def greet(device):
        pl.semaphore_signal(barrier, inc=1, device_id=device, device_id_type=MESH)

    greet(dev_low)
    greet(dev_high)

    @pl.when(has_low)
    def _():
        greet(dev_prev)

    @pl.when(has_high)
    def _():
        greet(dev_next)

    for k in (1, 13, 2, 3, 11):
        loads[k].wait()
    for h in (1, 2, 3):
        for t in range(tiles):
            fields[t, h].wait()
    parts = []
    for t in range(tiles):
        lanes = slice(128 * t, 128 * t + 128)
        total = x_ref[t, 1] * vel_ref[0, :, lanes].astype(F32)
        total += x_ref[t, 2] * vel_ref[1, :, lanes].astype(F32)
        total += x_ref[t, 3] * vel_ref[2, :, lanes].astype(F32)
        parts.append(jnp.sum(total * weight_ref[...], axis=0, keepdims=True))
    elem_grad = drag_ref[...] * jnp.concatenate(parts, axis=1)
    weighted = bw_ref[...] * elem_grad
    w1 = weighted.astype(BF)
    rest = weighted - w1.astype(F32)
    w2 = rest.astype(BF)
    w3 = (rest - w2.astype(F32)).astype(BF).astype(F32)
    row16 = lax.broadcasted_iota(jnp.int32, (16, elems), 0)
    stack = jnp.where(row16 == 0, w1.astype(F32), 0.0)
    stack = jnp.where(row16 == 1, w2.astype(F32), stack)
    stack = jnp.where(row16 == 2, w3, stack).astype(BF)
    rel = eb_ref[...] - (joint - 1) * owned
    rel = jnp.where(rel < 0, rel + BLOCKS, rel)
    rel = jnp.where(rel >= BLOCKS, rel - BLOCKS, rel)
    rows_blk = lax.broadcasted_iota(jnp.int32, (width, elems), 0).astype(jnp.int16)
    for j in range(3):
        ids = jnp.broadcast_to(rel - j * owned, (width, elems)).astype(jnp.int16)
        sums = dot_nt(stack, one_hot(rows_blk == ids))
        total = jnp.sum(sums, axis=0, keepdims=True)
        bsend_ref[j] = jnp.broadcast_to(total, (8, width))
    def remote(src, dst, k, device):
        return pltpu.make_async_remote_copy(
            src_ref=src,
            dst_ref=dst,
            send_sem=send_sem.at[k],
            recv_sem=recv_sem.at[k],
            device_id=device,
            device_id_type=MESH,
        )

    up_x = remote(send_ref.at[1], recv_ref.at[0], 0, dev_high)
    down_x = remote(send_ref.at[0], recv_ref.at[1], 1, dev_low)
    up_z = remote(send_ref.at[3], recv_ref.at[2], 2, dev_next)
    down_z = remote(send_ref.at[2], recv_ref.at[3], 3, dev_prev)
    up_b = remote(bsend_ref.at[2], brecv_ref.at[0], 4, dev_next)
    down_b = remote(bsend_ref.at[0], brecv_ref.at[1], 5, dev_prev)

    @pl.when(has_low)
    def _():
        pl.semaphore_wait(barrier, 4)
        down_b.start()

    @pl.when(jnp.logical_not(has_low))
    def _():
        pl.semaphore_wait(barrier, 3)
        greet(dev_prev)

    @pl.when(jnp.logical_not(has_high))
    def _():
        pl.semaphore_signal(far_sem, inc=1, device_id=dev_next, device_id_type=MESH)

    up_b.start()
    for k in (8, 9, 10, 6):
        loads[k].wait()
    slot_ids = lax.broadcasted_iota(jnp.int32, (1, slots), 1)
    rows_slots = lax.broadcasted_iota(jnp.int32, (elems, slots), 0).astype(jnp.int16)
    for i in range(4):
        row = i % 2
        ids = (sslots_ref if i < 2 else aslots_ref)[row : row + 1, :]
        if i < 2:
            ids = jnp.where(slot_ids < live_ref[:, row : row + 1], ids, -1)
        ids = jnp.broadcast_to(ids, (elems, slots)).astype(jnp.int16)
        oh_ref[i] = one_hot(rows_slots == ids)

    for c in range(5):
        for h in range(5):
            coef_ref[5 * c + h] = jnp.broadcast_to(0.1 * nbrmat_ref[c][:, h : h + 1], (6, 128))

    def take_trace(t, face):
        lanes = slice(128 * t, 128 * t + 128)
        for c in range(5):
            hi, lo = split2(face_rows(x_ref, t, c, face))
            tr_ref[face, 16 * c : 16 * c + 16, lanes] = hi
            tr_ref[face, 80 + 16 * c : 96 + 16 * c, lanes] = lo

    for h in (0, 4):
        for t in range(tiles):
            fields[t, h].wait()
    for t in range(tiles):
        for face in SIDES:
            take_trace(t, face)

    for i, face in enumerate(SIDES):
        both = dot(tr_ref[face], oh_ref[i])
        both = both[:80] + both[80:]
        for n in range(0, slots, 128):
            parts = [both[16 * h : 16 * h + 16, n : n + 128] for h in range(5)]
            for c in range(5):
                value = mixed(coef_ref, face + 1 - 2 * (face % 2), c, parts)
                send_ref[i, 16 * c : 16 * c + 16, n : n + 128] = value

    up_x.start()
    down_x.start()

    @pl.when(has_high)
    def _():
        up_z.start()

    @pl.when(has_low)
    def _():
        down_z.start()

    @pl.when(jnp.logical_not(has_low))
    def _():
        recv_ref[2] = jnp.zeros((80, slots), F32)

    @pl.when(jnp.logical_not(has_high))
    def _():
        recv_ref[3] = jnp.zeros((80, slots), F32)

    for k in (7, 12, 4, 5):
        loads[k].wait()

    spread = jnp.minimum(lax.broadcasted_iota(jnp.int32, (5, 384), 1) // 64, 4)
    spread = jnp.where(spread == lax.broadcasted_iota(jnp.int32, (5, 384), 0), 1.0, 0.0)
    for c in range(5):
        rows = slice(64 * c, 64 * c + 64)
        jac = jac_ref[0][:, c : c + 1] * spread[0:1, :]
        face = own_ref[c][:, 0:1] * spread[0:1, :]
        for h in range(1, 5):
            jac += jac_ref[h][:, c : c + 1] * spread[h : h + 1, :]
            face += own_ref[c][:, h : h + 1] * spread[h : h + 1, :]
        for t in range(3):
            lanes = slice(128 * t, 128 * t + 128)
            total = mats_ref[0] * jac[0:1, lanes]
            for j in range(1, 9):
                row = jac[j : j + 1, lanes] if j < 3 else face[j - 3 : j - 2, lanes]
                total += mats_ref[j] * row
            hi, lo = split2(total)
            places = ((768, hi), (896, lo)) if t == 2 else ((0, hi), (256, hi), (512, lo))
            for base, part in places:
                base += 128 * t if t < 2 else 0
                a_ref[rows, base : base + 128] = part

    for t in range(tiles):
        lanes = slice(128 * t, 128 * t + 128)
        for h in range(5):
            hi, lo = split2(x_ref[t, h])
            places = ((768, hi), (832, lo), (896, hi))
            if h < 4:
                places = ((64 * h, hi), (256 + 64 * h, lo), (512 + 64 * h, hi))
            for base, part in places:
                xs_ref[base : base + 64, lanes] = part
        for face in (2, 3):
            take_trace(t, face)

    own = dot(a_ref[:, 0:960], xs_ref[...])
    keep = 1.0 - 0.1 * drag_ref[...]
    for t in range(tiles):
        lanes = slice(128 * t, 128 * t + 128)
        for c in range(5):
            x = x_ref[t, c]
            scaled = x * keep[:, lanes] if 1 <= c <= 3 else x
            acc_ref[t, c] = scaled + own[64 * c : 64 * c + 64, lanes]

    rows_src = lax.broadcasted_iota(jnp.int32, (elems, elems), 0).astype(jnp.int16)
    for f in range(6):
        g = f + 1 - 2 * (f % 2)
        ids = jnp.broadcast_to(nbr_ref[f : f + 1, :], (elems, elems)).astype(jnp.int16)
        both = dot(tr_ref[g], one_hot(rows_src == ids))
        both = both[:80] + both[80:]
        for t in range(tiles):
            parts = [both[16 * h : 16 * h + 16, 128 * t : 128 * t + 128] for h in range(5)]
            add_face(acc_ref, t, f, [mixed(coef_ref, f, c, parts) for c in range(5)])

    @pl.when(jnp.logical_not(has_low))
    def _():
        pl.semaphore_wait(far_sem, 1)
        down_b.start()

    up_x.wait()
    down_x.wait()

    @pl.when(has_high)
    def _():
        up_z.wait_send()
        down_z.wait_recv()

    @pl.when(has_low)
    def _():
        down_z.wait_send()
        up_z.wait_recv()

    for i, face in enumerate(SIDES):
        both = dot_nt(jnp.concatenate(split2(recv_ref[i]), axis=0), oh_ref[i])
        both = both[:80] + both[80:]
        for t in range(tiles):
            lanes = slice(128 * t, 128 * t + 128)
            add_face(acc_ref, t, face, [both[16 * c : 16 * c + 16, lanes] for c in range(5)])

    up_b.wait()
    down_b.wait()
    sums = bsend_ref[1] + brecv_ref[0] + brecv_ref[1]
    grad_ref[...] = sums[0, :owned]


def finish(acc_ref, sums_ref, out_ref, grad_ref, sem):
    tiles = acc_ref.shape[0]
    copies = [pltpu.make_async_copy(sums_ref, grad_ref, sem.at[tiles])]
    for t in range(tiles):
        place = out_ref.at[:, :, pl.ds(128 * t, 128)]
        copies.append(pltpu.make_async_copy(acc_ref.at[t], place, sem.at[t]))
    for copy in copies:
        copy.start()
    for copy in copies:
        copy.wait()


def on_device(
    sectors,
    slabs,
    adjoint,
    velocity,
    drag,
    block_weight,
    flux_jac,
    face_own,
    face_nbr,
    nbr_local,
    sector_slots,
    axial_slots,
    sector_live,
    elem_block,
):
    elems = adjoint.shape[2]
    tiles = elems // 128
    slots = sector_slots.shape[1]
    owned = BLOCKS // (sectors * slabs)
    width = -(-owned // 128) * 128
    operands = (
        adjoint,
        velocity,
        drag.reshape(1, elems),
        block_weight.reshape(1, elems),
        jnp.transpose(flux_jac, (1, 0, 2)),
        jnp.transpose(face_own, (1, 0, 2)),
        jnp.transpose(face_nbr, (1, 0, 2)),
        nbr_local,
        sector_slots,
        axial_slots,
        sector_live.reshape(1, 2),
        elem_block.reshape(1, elems),
        *constant_tables(),
    )
    vmem = pl.BlockSpec(memory_space=pltpu.VMEM)
    hbm = pl.BlockSpec(memory_space=pltpu.HBM)
    handed = pl.pallas_call(
        functools.partial(exchange, sectors, slabs, owned),
        out_shape=(
            pltpu.VMEM((tiles, 5, 64, 128), F32),
            pltpu.VMEM((owned,), F32),
        ),
        in_specs=[hbm] * INPUTS,
        out_specs=(vmem,) * 2,
        scratch_shapes=[pltpu.VMEM((tiles, 5, 64, 128), F32)]
        + [pltpu.VMEM(a.shape, a.dtype) for a in operands[1:]]
        + [
            pltpu.VMEM((960, elems), BF),
            pltpu.VMEM((6, 160, elems), BF),
            pltpu.VMEM((4, elems, slots), BF),
            pltpu.VMEM((4, 80, slots), F32),
            pltpu.VMEM((4, 80, slots), F32),
            pltpu.VMEM((320, 1024), BF),
            pltpu.VMEM((25, 6, 128), F32),
            pltpu.VMEM((3, 8, width), F32),
            pltpu.VMEM((2, 8, width), F32),
            pltpu.SemaphoreType.DMA((6,)),
            pltpu.SemaphoreType.DMA((6,)),
            pltpu.SemaphoreType.REGULAR,
            pltpu.SemaphoreType.DMA((INPUTS,)),
            pltpu.SemaphoreType.DMA((5 * tiles,)),
        ],
        compiler_params=pltpu.CompilerParams(
            collective_id=0, has_side_effects=True, vmem_limit_bytes=60 * 1024 * 1024
        ),
    )(*operands)
    return pl.pallas_call(
        finish,
        out_shape=(
            jax.ShapeDtypeStruct(adjoint.shape, F32),
            jax.ShapeDtypeStruct((owned,), F32),
        ),
        in_specs=[vmem] * 2,
        out_specs=(hbm, hbm),
        scratch_shapes=[
            pltpu.SemaphoreType.DMA((tiles + 1,)),
        ],
        compiler_params=pltpu.CompilerParams(vmem_limit_bytes=40 * 1024 * 1024),
    )(*handed)


def solution(mesh):
    placed = (
        P(None, None, ("sector", "axial")),
        P(None, None, ("sector", "axial")),
        P(("sector", "axial")),
        P(("sector", "axial")),
        P(),
        P(),
        P(),
        P(None, ("sector", "axial")),
        P(None, ("sector", "axial")),
        P(None, ("sector", "axial")),
        P("sector", "axial", None),
        P(("sector", "axial")),
    )
    return jax.shard_map(
        functools.partial(on_device, mesh.shape["sector"], mesh.shape["axial"]),
        mesh=mesh,
        in_specs=placed,
        out_specs=(P(None, None, ("sector", "axial")), P(("sector", "axial"))),
        check_vma=False,
    )
```

```python
import functools

import jax
import jax.numpy as jnp
import numpy as np
from jax import lax
from jax.experimental import pallas as pl
from jax.experimental.pallas import tpu as pltpu
from jax.sharding import PartitionSpec as P

BLOCKS = 4096
BF = jnp.bfloat16
F32 = jnp.float32
MESH = pl.DeviceIdType.MESH
INPUTS = 14
SIDES = (0, 1, 4, 5)


def lobatto_tables():
    points = np.array([-1.0, -1.0 / np.sqrt(5.0), 1.0 / np.sqrt(5.0), 1.0])
    weights = np.array([1.0, 5.0, 5.0, 1.0]) / 6.0
    scales = np.array(
        [np.prod([points[i] - points[k] for k in range(4) if k != i]) for i in range(4)]
    )
    derivative = np.zeros((4, 4))
    for i in range(4):
        for p in range(4):
            if i != p:
                derivative[i, p] = scales[i] / scales[p] / (points[i] - points[p])
            else:
                derivative[i, p] = sum((1.0 / (points[i] - points[k]) for k in range(4) if k != i))
    node_weight = (
        weights[:, None, None] * weights[None, :, None] * weights[None, None, :]
    ).reshape(64) / 8.0
    return (derivative, node_weight)


def constant_tables():
    derivative, node_weight = lobatto_tables()
    eye = np.eye(4)
    step = derivative.T
    mats = [
        np.kron(np.kron(step, eye), eye),
        np.kron(np.kron(eye, step), eye),
        np.kron(np.kron(eye, eye), step),
    ]
    nodes = np.arange(64).reshape(4, 4, 4)
    faces = [nodes[0], nodes[3], nodes[:, 0], nodes[:, 3], nodes[:, :, 0], nodes[:, :, 3]]
    for ids in faces:
        diag = np.zeros((64, 64))
        diag[ids.reshape(16), ids.reshape(16)] = 1.0
        mats.append(diag)
    mats = [0.1 * np.concatenate([m, m], axis=1) for m in mats]
    weights = np.repeat(node_weight[:, None], 128, axis=1)
    return jnp.asarray(np.stack(mats), F32), jnp.asarray(weights, F32)


def split2(x):
    hi = x.astype(BF)
    return hi, (x - hi.astype(F32)).astype(BF)


def dot(a, b):
    return jnp.dot(a, b, preferred_element_type=F32)


def dot_nt(a, b):
    return lax.dot_general(a, b, (((1,), (1,)), ((), ())), preferred_element_type=F32)


def one_hot(mask):
    return jnp.where(mask, jnp.ones((), BF), jnp.zeros((), BF))


def add_face(ref, tile, face, part):
    low = lax.broadcasted_iota(jnp.int32, (8, 128), 0) < 4
    for c in range(5):
        rows = part[c]
        if face < 2:
            ids = pl.ds(48 * face, 16)
            ref[tile, c, ids, :] = ref[tile, c, ids, :] + rows
        elif face >= 4:
            ids = pl.ds(3 * (face - 4), 16, stride=4)
            ref[tile, c, ids, :] = ref[tile, c, ids, :] + rows
        else:
            for v in range(2):
                both = rows[8 * v : 8 * v + 8]
                turned = pltpu.roll(both, 4, 0)
                for k in range(2):
                    ids = pl.ds(32 * v + 16 * k + 8 * (face - 2), 8)
                    value = both if k == face - 2 else turned
                    mask = low if face == 2 else jnp.logical_not(low)
                    ref[tile, c, ids, :] = ref[tile, c, ids, :] + jnp.where(mask, value, 0.0)


def mixed(coef_ref, face, c, parts):
    total = coef_ref[5 * c, face : face + 1, :] * parts[0]
    for h in range(1, 5):
        total += coef_ref[5 * c + h, face : face + 1, :] * parts[h]
    return total


def face_rows(ref, tile, c, face):
    if face < 2:
        return ref[tile, c, 48 * face : 48 * face + 16, :]
    if face >= 4:
        return ref[tile, c, pl.ds(3 * (face - 4), 16, stride=4), :]
    low = lax.broadcasted_iota(jnp.int32, (8, 128), 0) < 4
    out = []
    for v in range(2):
        first = ref[tile, c, 32 * v + 8 * (face - 2) : 32 * v + 8 * (face - 2) + 8, :]
        second = ref[tile, c, 32 * v + 16 + 8 * (face - 2) : 32 * v + 24 + 8 * (face - 2), :]
        if face == 2:
            out.append(jnp.where(low, first, pltpu.roll(second, 4, 0)))
        else:
            out.append(jnp.where(low, pltpu.roll(first, 4, 0), second))
    return jnp.concatenate(out, axis=0)


def exchange(sectors, slabs, owned, *refs):
    hbm_refs = refs[:INPUTS]
    acc_ref, grad_ref = refs[INPUTS : INPUTS + 2]
    x_ref = refs[INPUTS + 2]
    vmem_refs = (None,) + refs[INPUTS + 3 : 2 * INPUTS + 2]
    (
        _,
        vel_ref,
        drag_ref,
        bw_ref,
        jac_ref,
        own_ref,
        nbrmat_ref,
        nbr_ref,
        sslots_ref,
        aslots_ref,
        live_ref,
        eb_ref,
        mats_ref,
        weight_ref,
    ) = vmem_refs
    (
        xs_ref,
        tr_ref,
        oh_ref,
        send_ref,
        recv_ref,
        a_ref,
        coef_ref,
        bsend_ref,
        brecv_ref,
        send_sem,
        recv_sem,
        far_sem,
        load_sem,
        x_sem,
    ) = refs[2 * INPUTS + 2 :]
    tiles = x_ref.shape[0]
    elems = tiles * 128
    slots = sslots_ref.shape[1]
    width = bsend_ref.shape[2]
    count = sectors * slabs

    loads = {
        k: pltpu.make_async_copy(hbm_refs[k], vmem_refs[k], load_sem.at[k])
        for k in range(1, INPUTS)
    }
    fields = {
        (t, h): pltpu.make_async_copy(
            hbm_refs[0].at[h, :, pl.ds(128 * t, 128)], x_ref.at[t, h], x_sem.at[5 * t + h]
        )
        for h in (1, 2, 3, 0, 4)
        for t in range(tiles)
    }
    for k in (9, 6):
        loads[k].start()
    for key in fields:
        fields[key].start()
    for k in (8, 10, 1, 13, 2, 3, 11, 7, 12, 4, 5):
        loads[k].start()

    sec = lax.axis_index("sector")
    axi = lax.axis_index("axial")
    joint = sec * slabs + axi
    prev = lax.rem(joint + count - 1, count)
    nxt = lax.rem(joint + 1, count)
    dev_prev = (prev // slabs, lax.rem(prev, slabs))
    dev_next = (nxt // slabs, lax.rem(nxt, slabs))
    dev_low = (lax.rem(sec + sectors - 1, sectors), axi)
    dev_high = (lax.rem(sec + 1, sectors), axi)

    has_low = axi > 0
    has_high = axi < slabs - 1

    barrier = pltpu.get_barrier_semaphore()

    def greet(device):
        pl.semaphore_signal(barrier, inc=1, device_id=device, device_id_type=MESH)

    greet(dev_low)
    greet(dev_high)

    @pl.when(has_low)
    def _():
        greet(dev_prev)

    @pl.when(has_high)
    def _():
        greet(dev_next)

    def remote(src, dst, k, device):
        return pltpu.make_async_remote_copy(
            src_ref=src,
            dst_ref=dst,
            send_sem=send_sem.at[k],
            recv_sem=recv_sem.at[k],
            device_id=device,
            device_id_type=MESH,
        )

    up_x = remote(send_ref.at[1], recv_ref.at[0], 0, dev_high)
    down_x = remote(send_ref.at[0], recv_ref.at[1], 1, dev_low)
    up_z = remote(send_ref.at[3], recv_ref.at[2], 2, dev_next)
    down_z = remote(send_ref.at[2], recv_ref.at[3], 3, dev_prev)
    up_b = remote(bsend_ref.at[2], brecv_ref.at[0], 4, dev_next)
    down_b = remote(bsend_ref.at[0], brecv_ref.at[1], 5, dev_prev)

    slot_ids = lax.broadcasted_iota(jnp.int32, (1, slots), 1)
    rows_slots = lax.broadcasted_iota(jnp.int32, (elems, slots), 0).astype(jnp.int16)

    def find_slots(i, ids):
        ids = jnp.broadcast_to(ids, (elems, slots)).astype(jnp.int16)
        oh_ref[i] = one_hot(rows_slots == ids)

    def take_trace(t, face):
        lanes = slice(128 * t, 128 * t + 128)
        for c in range(5):
            hi, lo = split2(face_rows(x_ref, t, c, face))
            tr_ref[face, 16 * c : 16 * c + 16, lanes] = hi
            tr_ref[face, 80 + 16 * c : 96 + 16 * c, lanes] = lo

    def fill_send(i):
        face = SIDES[i]
        for t in range(tiles):
            take_trace(t, face)
        both = dot(tr_ref[face], oh_ref[i])
        both = both[:80] + both[80:]
        for n in range(0, slots, 128):
            parts = [both[16 * h : 16 * h + 16, n : n + 128] for h in range(5)]
            for c in range(5):
                value = mixed(coef_ref, face + 1 - 2 * (face % 2), c, parts)
                send_ref[i, 16 * c : 16 * c + 16, n : n + 128] = value

    loads[9].wait()
    for i in (2, 3):
        find_slots(i, aslots_ref[i - 2 : i - 1, :])
    loads[6].wait()
    for c in range(5):
        for h in range(5):
            coef_ref[5 * c + h] = jnp.broadcast_to(0.1 * nbrmat_ref[c][:, h : h + 1], (6, 128))
    for key in fields:
        fields[key].wait()
    fill_send(2)
    fill_send(3)

    @pl.when(has_low)
    def _():
        pl.semaphore_wait(barrier, 4)

    @pl.when(jnp.logical_not(has_low))
    def _():
        pl.semaphore_wait(barrier, 3)
        greet(dev_prev)

    @pl.when(jnp.logical_not(has_high))
    def _():
        pl.semaphore_signal(far_sem, inc=1, device_id=dev_next, device_id_type=MESH)


    @pl.when(has_high)
    def _():
        up_z.start()

    @pl.when(has_low)
    def _():
        down_z.start()

    @pl.when(jnp.logical_not(has_low))
    def _():
        recv_ref[2] = jnp.zeros((80, slots), F32)

    @pl.when(jnp.logical_not(has_high))
    def _():
        recv_ref[3] = jnp.zeros((80, slots), F32)

    loads[8].wait()
    loads[10].wait()
    for i in (0, 1):
        live = slot_ids < live_ref[:, i : i + 1]
        find_slots(i, jnp.where(live, sslots_ref[i : i + 1, :], -1))
    fill_send(0)
    fill_send(1)
    up_x.start()
    down_x.start()

    for k in (1, 13, 2, 3, 11):
        loads[k].wait()
    parts = []
    for t in range(tiles):
        lanes = slice(128 * t, 128 * t + 128)
        total = x_ref[t, 1] * vel_ref[0, :, lanes].astype(F32)
        total += x_ref[t, 2] * vel_ref[1, :, lanes].astype(F32)
        total += x_ref[t, 3] * vel_ref[2, :, lanes].astype(F32)
        parts.append(jnp.sum(total * weight_ref[...], axis=0, keepdims=True))
    elem_grad = drag_ref[...] * jnp.concatenate(parts, axis=1)
    weighted = bw_ref[...] * elem_grad
    w1 = weighted.astype(BF)
    rest = weighted - w1.astype(F32)
    w2 = rest.astype(BF)
    w3 = (rest - w2.astype(F32)).astype(BF).astype(F32)
    row16 = lax.broadcasted_iota(jnp.int32, (16, elems), 0)
    stack = jnp.where(row16 == 0, w1.astype(F32), 0.0)
    stack = jnp.where(row16 == 1, w2.astype(F32), stack)
    stack = jnp.where(row16 == 2, w3, stack).astype(BF)
    rel = eb_ref[...] - (joint - 1) * owned
    rel = jnp.where(rel < 0, rel + BLOCKS, rel)
    rel = jnp.where(rel >= BLOCKS, rel - BLOCKS, rel)
    rows_blk = lax.broadcasted_iota(jnp.int32, (width, elems), 0).astype(jnp.int16)
    for j in range(3):
        ids = jnp.broadcast_to(rel - j * owned, (width, elems)).astype(jnp.int16)
        sums = dot_nt(stack, one_hot(rows_blk == ids))
        total = jnp.sum(sums, axis=0, keepdims=True)
        bsend_ref[j] = jnp.broadcast_to(total, (8, width))
    up_b.start()

    @pl.when(has_low)
    def _():
        down_b.start()

    for k in (7, 12, 4, 5):
        loads[k].wait()

    spread = jnp.minimum(lax.broadcasted_iota(jnp.int32, (5, 384), 1) // 64, 4)
    spread = jnp.where(spread == lax.broadcasted_iota(jnp.int32, (5, 384), 0), 1.0, 0.0)
    for c in range(5):
        rows = slice(64 * c, 64 * c + 64)
        jac = jac_ref[0][:, c : c + 1] * spread[0:1, :]
        face = own_ref[c][:, 0:1] * spread[0:1, :]
        for h in range(1, 5):
            jac += jac_ref[h][:, c : c + 1] * spread[h : h + 1, :]
            face += own_ref[c][:, h : h + 1] * spread[h : h + 1, :]
        for t in range(3):
            lanes = slice(128 * t, 128 * t + 128)
            total = mats_ref[0] * jac[0:1, lanes]
            for j in range(1, 9):
                row = jac[j : j + 1, lanes] if j < 3 else face[j - 3 : j - 2, lanes]
                total += mats_ref[j] * row
            hi, lo = split2(total)
            places = ((768, hi), (896, lo)) if t == 2 else ((0, hi), (256, hi), (512, lo))
            for base, part in places:
                base += 128 * t if t < 2 else 0
                a_ref[rows, base : base + 128] = part

    for t in range(tiles):
        lanes = slice(128 * t, 128 * t + 128)
        for h in range(5):
            hi, lo = split2(x_ref[t, h])
            places = ((768, hi), (832, lo), (896, hi))
            if h < 4:
                places = ((64 * h, hi), (256 + 64 * h, lo), (512 + 64 * h, hi))
            for base, part in places:
                xs_ref[base : base + 64, lanes] = part
        for face in (2, 3):
            take_trace(t, face)

    own = dot(a_ref[:, 0:960], xs_ref[...])
    keep = 1.0 - 0.1 * drag_ref[...]
    for t in range(tiles):
        lanes = slice(128 * t, 128 * t + 128)
        for c in range(5):
            x = x_ref[t, c]
            scaled = x * keep[:, lanes] if 1 <= c <= 3 else x
            acc_ref[t, c] = scaled + own[64 * c : 64 * c + 64, lanes]

    rows_src = lax.broadcasted_iota(jnp.int32, (elems, elems), 0).astype(jnp.int16)
    def gather(f):
        g = f + 1 - 2 * (f % 2)
        ids = jnp.broadcast_to(nbr_ref[f : f + 1, :], (elems, elems)).astype(jnp.int16)
        both = dot(tr_ref[g], one_hot(rows_src == ids))
        both = both[:80] + both[80:]
        for t in range(tiles):
            parts = [both[16 * h : 16 * h + 16, 128 * t : 128 * t + 128] for h in range(5)]
            add_face(acc_ref, t, f, [mixed(coef_ref, f, c, parts) for c in range(5)])

    for f in (0, 1, 2):
        gather(f)

    @pl.when(jnp.logical_not(has_low))
    def _():
        pl.semaphore_wait(far_sem, 1)
        down_b.start()

    for f in (3, 4, 5):
        gather(f)

    up_x.wait()
    down_x.wait()

    @pl.when(has_high)
    def _():
        up_z.wait_send()
        down_z.wait_recv()

    @pl.when(has_low)
    def _():
        down_z.wait_send()
        up_z.wait_recv()

    for i, face in enumerate(SIDES):
        both = dot_nt(jnp.concatenate(split2(recv_ref[i]), axis=0), oh_ref[i])
        both = both[:80] + both[80:]
        for t in range(tiles):
            lanes = slice(128 * t, 128 * t + 128)
            add_face(acc_ref, t, face, [both[16 * c : 16 * c + 16, lanes] for c in range(5)])

    up_b.wait()
    down_b.wait()
    sums = bsend_ref[1] + brecv_ref[0] + brecv_ref[1]
    grad_ref[...] = sums[0, :owned]


def finish(acc_ref, sums_ref, out_ref, grad_ref, sem):
    tiles = acc_ref.shape[0]
    copies = [pltpu.make_async_copy(sums_ref, grad_ref, sem.at[tiles])]
    for t in range(tiles):
        place = out_ref.at[:, :, pl.ds(128 * t, 128)]
        copies.append(pltpu.make_async_copy(acc_ref.at[t], place, sem.at[t]))
    for copy in copies:
        copy.start()
    for copy in copies:
        copy.wait()


def on_device(
    sectors,
    slabs,
    adjoint,
    velocity,
    drag,
    block_weight,
    flux_jac,
    face_own,
    face_nbr,
    nbr_local,
    sector_slots,
    axial_slots,
    sector_live,
    elem_block,
):
    elems = adjoint.shape[2]
    tiles = elems // 128
    slots = sector_slots.shape[1]
    owned = BLOCKS // (sectors * slabs)
    width = -(-owned // 128) * 128
    operands = (
        adjoint,
        velocity,
        drag.reshape(1, elems),
        block_weight.reshape(1, elems),
        jnp.transpose(flux_jac, (1, 0, 2)),
        jnp.transpose(face_own, (1, 0, 2)),
        jnp.transpose(face_nbr, (1, 0, 2)),
        nbr_local,
        sector_slots,
        axial_slots,
        sector_live.reshape(1, 2),
        elem_block.reshape(1, elems),
        *constant_tables(),
    )
    vmem = pl.BlockSpec(memory_space=pltpu.VMEM)
    hbm = pl.BlockSpec(memory_space=pltpu.HBM)
    handed = pl.pallas_call(
        functools.partial(exchange, sectors, slabs, owned),
        out_shape=(
            pltpu.VMEM((tiles, 5, 64, 128), F32),
            pltpu.VMEM((owned,), F32),
        ),
        in_specs=[hbm] * INPUTS,
        out_specs=(vmem,) * 2,
        scratch_shapes=[pltpu.VMEM((tiles, 5, 64, 128), F32)]
        + [pltpu.VMEM(a.shape, a.dtype) for a in operands[1:]]
        + [
            pltpu.VMEM((960, elems), BF),
            pltpu.VMEM((6, 160, elems), BF),
            pltpu.VMEM((4, elems, slots), BF),
            pltpu.VMEM((4, 80, slots), F32),
            pltpu.VMEM((4, 80, slots), F32),
            pltpu.VMEM((320, 1024), BF),
            pltpu.VMEM((25, 6, 128), F32),
            pltpu.VMEM((3, 8, width), F32),
            pltpu.VMEM((2, 8, width), F32),
            pltpu.SemaphoreType.DMA((6,)),
            pltpu.SemaphoreType.DMA((6,)),
            pltpu.SemaphoreType.REGULAR,
            pltpu.SemaphoreType.DMA((INPUTS,)),
            pltpu.SemaphoreType.DMA((5 * tiles,)),
        ],
        compiler_params=pltpu.CompilerParams(
            collective_id=0, has_side_effects=True, vmem_limit_bytes=60 * 1024 * 1024
        ),
    )(*operands)
    return pl.pallas_call(
        finish,
        out_shape=(
            jax.ShapeDtypeStruct(adjoint.shape, F32),
            jax.ShapeDtypeStruct((owned,), F32),
        ),
        in_specs=[vmem] * 2,
        out_specs=(hbm, hbm),
        scratch_shapes=[
            pltpu.SemaphoreType.DMA((tiles + 1,)),
        ],
        compiler_params=pltpu.CompilerParams(vmem_limit_bytes=40 * 1024 * 1024),
    )(*handed)


def solution(mesh):
    placed = (
        P(None, None, ("sector", "axial")),
        P(None, None, ("sector", "axial")),
        P(("sector", "axial")),
        P(("sector", "axial")),
        P(),
        P(),
        P(),
        P(None, ("sector", "axial")),
        P(None, ("sector", "axial")),
        P(None, ("sector", "axial")),
        P("sector", "axial", None),
        P(("sector", "axial")),
    )
    return jax.shard_map(
        functools.partial(on_device, mesh.shape["sector"], mesh.shape["axial"]),
        mesh=mesh,
        in_specs=placed,
        out_specs=(P(None, None, ("sector", "axial")), P(("sector", "axial"))),
        check_vma=False,
    )
```

```python
import functools

import jax
import jax.numpy as jnp
import numpy as np
from jax import lax
from jax.experimental import pallas as pl
from jax.experimental.pallas import tpu as pltpu
from jax.sharding import PartitionSpec as P

BLOCKS = 4096
BF = jnp.bfloat16
F32 = jnp.float32
MESH = pl.DeviceIdType.MESH
INPUTS = 14
SIDES = (0, 1, 4, 5)


def lobatto_tables():
    points = np.array([-1.0, -1.0 / np.sqrt(5.0), 1.0 / np.sqrt(5.0), 1.0])
    weights = np.array([1.0, 5.0, 5.0, 1.0]) / 6.0
    scales = np.array(
        [np.prod([points[i] - points[k] for k in range(4) if k != i]) for i in range(4)]
    )
    derivative = np.zeros((4, 4))
    for i in range(4):
        for p in range(4):
            if i != p:
                derivative[i, p] = scales[i] / scales[p] / (points[i] - points[p])
            else:
                derivative[i, p] = sum((1.0 / (points[i] - points[k]) for k in range(4) if k != i))
    node_weight = (
        weights[:, None, None] * weights[None, :, None] * weights[None, None, :]
    ).reshape(64) / 8.0
    return (derivative, node_weight)


def constant_tables():
    derivative, node_weight = lobatto_tables()
    eye = np.eye(4)
    step = derivative.T
    mats = [
        np.kron(np.kron(step, eye), eye),
        np.kron(np.kron(eye, step), eye),
        np.kron(np.kron(eye, eye), step),
    ]
    nodes = np.arange(64).reshape(4, 4, 4)
    faces = [nodes[0], nodes[3], nodes[:, 0], nodes[:, 3], nodes[:, :, 0], nodes[:, :, 3]]
    for ids in faces:
        diag = np.zeros((64, 64))
        diag[ids.reshape(16), ids.reshape(16)] = 1.0
        mats.append(diag)
    mats = [0.1 * np.concatenate([m, m], axis=1) for m in mats]
    weights = np.repeat(node_weight[:, None], 128, axis=1)
    return jnp.asarray(np.stack(mats), F32), jnp.asarray(weights, F32)


def split2(x):
    hi = x.astype(BF)
    return hi, (x - hi.astype(F32)).astype(BF)


def dot(a, b):
    return jnp.dot(a, b, preferred_element_type=F32)


def dot_nt(a, b):
    return lax.dot_general(a, b, (((1,), (1,)), ((), ())), preferred_element_type=F32)


def one_hot(mask):
    return jnp.where(mask, jnp.ones((), BF), jnp.zeros((), BF))


def add_face(ref, tile, face, part):
    low = lax.broadcasted_iota(jnp.int32, (8, 128), 0) < 4
    for c in range(5):
        rows = part[c]
        if face < 2:
            ids = pl.ds(48 * face, 16)
            ref[tile, c, ids, :] = ref[tile, c, ids, :] + rows
        elif face >= 4:
            ids = pl.ds(3 * (face - 4), 16, stride=4)
            ref[tile, c, ids, :] = ref[tile, c, ids, :] + rows
        else:
            for v in range(2):
                both = rows[8 * v : 8 * v + 8]
                turned = pltpu.roll(both, 4, 0)
                for k in range(2):
                    ids = pl.ds(32 * v + 16 * k + 8 * (face - 2), 8)
                    value = both if k == face - 2 else turned
                    mask = low if face == 2 else jnp.logical_not(low)
                    ref[tile, c, ids, :] = ref[tile, c, ids, :] + jnp.where(mask, value, 0.0)


def mixed(coef_ref, face, c, parts):
    total = coef_ref[5 * c, face : face + 1, :] * parts[0]
    for h in range(1, 5):
        total += coef_ref[5 * c + h, face : face + 1, :] * parts[h]
    return total


def face_rows(ref, tile, c, face):
    if face < 2:
        return ref[tile, c, 48 * face : 48 * face + 16, :]
    if face >= 4:
        return ref[tile, c, pl.ds(3 * (face - 4), 16, stride=4), :]
    low = lax.broadcasted_iota(jnp.int32, (8, 128), 0) < 4
    out = []
    for v in range(2):
        first = ref[tile, c, 32 * v + 8 * (face - 2) : 32 * v + 8 * (face - 2) + 8, :]
        second = ref[tile, c, 32 * v + 16 + 8 * (face - 2) : 32 * v + 24 + 8 * (face - 2), :]
        if face == 2:
            out.append(jnp.where(low, first, pltpu.roll(second, 4, 0)))
        else:
            out.append(jnp.where(low, pltpu.roll(first, 4, 0), second))
    return jnp.concatenate(out, axis=0)


def exchange(sectors, slabs, owned, *refs):
    hbm_refs = refs[:INPUTS]
    acc_ref, grad_ref = refs[INPUTS : INPUTS + 2]
    x_ref = refs[INPUTS + 2]
    vmem_refs = (None,) + refs[INPUTS + 3 : 2 * INPUTS + 2]
    (
        _,
        vel_ref,
        drag_ref,
        bw_ref,
        jac_ref,
        own_ref,
        nbrmat_ref,
        nbr_ref,
        sslots_ref,
        aslots_ref,
        live_ref,
        eb_ref,
        mats_ref,
        weight_ref,
    ) = vmem_refs
    (
        xs_ref,
        tr_ref,
        oh_ref,
        send_ref,
        recv_ref,
        a_ref,
        coef_ref,
        bsend_ref,
        brecv_ref,
        send_sem,
        recv_sem,
        far_sem,
        load_sem,
        x_sem,
    ) = refs[2 * INPUTS + 2 :]
    tiles = x_ref.shape[0]
    elems = tiles * 128
    slots = sslots_ref.shape[1]
    width = bsend_ref.shape[2]
    count = sectors * slabs

    loads = {
        k: pltpu.make_async_copy(hbm_refs[k], vmem_refs[k], load_sem.at[k])
        for k in range(1, INPUTS)
    }
    fields = {
        (t, h): pltpu.make_async_copy(
            hbm_refs[0].at[h, :, pl.ds(128 * t, 128)], x_ref.at[t, h], x_sem.at[5 * t + h]
        )
        for h in (1, 2, 3, 0, 4)
        for t in range(tiles)
    }
    for k in (9, 6):
        loads[k].start()
    for key in fields:
        fields[key].start()
    for k in (8, 10, 1, 13, 2, 3, 11, 7, 12, 4, 5):
        loads[k].start()

    sec = lax.axis_index("sector")
    axi = lax.axis_index("axial")
    joint = sec * slabs + axi
    prev = lax.rem(joint + count - 1, count)
    nxt = lax.rem(joint + 1, count)
    dev_prev = (prev // slabs, lax.rem(prev, slabs))
    dev_next = (nxt // slabs, lax.rem(nxt, slabs))
    dev_low = (lax.rem(sec + sectors - 1, sectors), axi)
    dev_high = (lax.rem(sec + 1, sectors), axi)

    has_low = axi > 0
    has_high = axi < slabs - 1

    barrier = pltpu.get_barrier_semaphore()

    def greet(device):
        pl.semaphore_signal(barrier, inc=1, device_id=device, device_id_type=MESH)

    greet(dev_low)
    greet(dev_high)
    greet(dev_prev)

    @pl.when(has_high)
    def _():
        greet(dev_next)

    def remote(src, dst, k, device):
        return pltpu.make_async_remote_copy(
            src_ref=src,
            dst_ref=dst,
            send_sem=send_sem.at[k],
            recv_sem=recv_sem.at[k],
            device_id=device,
            device_id_type=MESH,
        )

    up_x = remote(send_ref.at[1], recv_ref.at[0], 0, dev_high)
    down_x = remote(send_ref.at[0], recv_ref.at[1], 1, dev_low)
    up_z = remote(send_ref.at[3], recv_ref.at[2], 2, dev_next)
    down_z = remote(send_ref.at[2], recv_ref.at[3], 3, dev_prev)
    up_b = remote(bsend_ref.at[2], brecv_ref.at[0], 4, dev_next)
    down_b = remote(bsend_ref.at[0], brecv_ref.at[1], 5, dev_prev)

    slot_ids = lax.broadcasted_iota(jnp.int32, (1, slots), 1)
    rows_slots = lax.broadcasted_iota(jnp.int32, (elems, slots), 0).astype(jnp.int16)

    def find_slots(i, ids):
        ids = jnp.broadcast_to(ids, (elems, slots)).astype(jnp.int16)
        oh_ref[i] = one_hot(rows_slots == ids)

    def take_trace(t, face):
        lanes = slice(128 * t, 128 * t + 128)
        for c in range(5):
            hi, lo = split2(face_rows(x_ref, t, c, face))
            tr_ref[face, 16 * c : 16 * c + 16, lanes] = hi
            tr_ref[face, 80 + 16 * c : 96 + 16 * c, lanes] = lo

    def fill_send(i):
        face = SIDES[i]
        for t in range(tiles):
            take_trace(t, face)
        both = dot(tr_ref[face], oh_ref[i])
        both = both[:80] + both[80:]
        for n in range(0, slots, 128):
            parts = [both[16 * h : 16 * h + 16, n : n + 128] for h in range(5)]
            for c in range(5):
                value = mixed(coef_ref, face + 1 - 2 * (face % 2), c, parts)
                send_ref[i, 16 * c : 16 * c + 16, n : n + 128] = value

    loads[9].wait()
    for i in (2, 3):
        find_slots(i, aslots_ref[i - 2 : i - 1, :])
    loads[6].wait()
    for c in range(5):
        for h in range(5):
            coef_ref[5 * c + h] = jnp.broadcast_to(0.1 * nbrmat_ref[c][:, h : h + 1], (6, 128))
    for key in fields:
        fields[key].wait()
    fill_send(2)
    fill_send(3)

    @pl.when(has_low)
    def _():
        pl.semaphore_wait(barrier, 4)

    @pl.when(jnp.logical_not(has_low))
    def _():
        pl.semaphore_wait(barrier, 3)

    @pl.when(jnp.logical_not(has_high))
    def _():
        pl.semaphore_signal(far_sem, inc=1, device_id=dev_next, device_id_type=MESH)

    @pl.when(has_high)
    def _():
        up_z.start()

    @pl.when(has_low)
    def _():
        down_z.start()

    @pl.when(jnp.logical_not(has_low))
    def _():
        recv_ref[2] = jnp.zeros((80, slots), F32)

    @pl.when(jnp.logical_not(has_high))
    def _():
        recv_ref[3] = jnp.zeros((80, slots), F32)

    loads[8].wait()
    loads[10].wait()
    for i in (0, 1):
        live = slot_ids < live_ref[:, i : i + 1]
        find_slots(i, jnp.where(live, sslots_ref[i : i + 1, :], -1))
    fill_send(0)
    fill_send(1)
    up_x.start()
    down_x.start()

    for k in (1, 13, 2, 3, 11):
        loads[k].wait()
    parts = []
    for t in range(tiles):
        lanes = slice(128 * t, 128 * t + 128)
        total = x_ref[t, 1] * vel_ref[0, :, lanes].astype(F32)
        total += x_ref[t, 2] * vel_ref[1, :, lanes].astype(F32)
        total += x_ref[t, 3] * vel_ref[2, :, lanes].astype(F32)
        parts.append(jnp.sum(total * weight_ref[...], axis=0, keepdims=True))
    elem_grad = drag_ref[...] * jnp.concatenate(parts, axis=1)
    weighted = bw_ref[...] * elem_grad
    w1 = weighted.astype(BF)
    rest = weighted - w1.astype(F32)
    w2 = rest.astype(BF)
    w3 = (rest - w2.astype(F32)).astype(BF).astype(F32)
    row16 = lax.broadcasted_iota(jnp.int32, (16, elems), 0)
    stack = jnp.where(row16 == 0, w1.astype(F32), 0.0)
    stack = jnp.where(row16 == 1, w2.astype(F32), stack)
    stack = jnp.where(row16 == 2, w3, stack).astype(BF)
    rel = eb_ref[...] - (joint - 1) * owned
    rel = jnp.where(rel < 0, rel + BLOCKS, rel)
    rel = jnp.where(rel >= BLOCKS, rel - BLOCKS, rel)
    rows_blk = lax.broadcasted_iota(jnp.int32, (width, elems), 0).astype(jnp.int16)
    for j in range(3):
        ids = jnp.broadcast_to(rel - j * owned, (width, elems)).astype(jnp.int16)
        sums = dot_nt(stack, one_hot(rows_blk == ids))
        total = jnp.sum(sums, axis=0, keepdims=True)
        bsend_ref[j] = jnp.broadcast_to(total, (8, width))
    up_b.start()

    @pl.when(has_low)
    def _():
        down_b.start()

    for k in (7, 12, 4, 5):
        loads[k].wait()

    spread = jnp.minimum(lax.broadcasted_iota(jnp.int32, (5, 384), 1) // 64, 4)
    spread = jnp.where(spread == lax.broadcasted_iota(jnp.int32, (5, 384), 0), 1.0, 0.0)
    for c in range(5):
        rows = slice(64 * c, 64 * c + 64)
        jac = jac_ref[0][:, c : c + 1] * spread[0:1, :]
        face = own_ref[c][:, 0:1] * spread[0:1, :]
        for h in range(1, 5):
            jac += jac_ref[h][:, c : c + 1] * spread[h : h + 1, :]
            face += own_ref[c][:, h : h + 1] * spread[h : h + 1, :]
        for t in range(3):
            lanes = slice(128 * t, 128 * t + 128)
            total = mats_ref[0] * jac[0:1, lanes]
            for j in range(1, 9):
                row = jac[j : j + 1, lanes] if j < 3 else face[j - 3 : j - 2, lanes]
                total += mats_ref[j] * row
            hi, lo = split2(total)
            places = ((768, hi), (896, lo)) if t == 2 else ((0, hi), (256, hi), (512, lo))
            for base, part in places:
                base += 128 * t if t < 2 else 0
                a_ref[rows, base : base + 128] = part

    for t in range(tiles):
        lanes = slice(128 * t, 128 * t + 128)
        for h in range(5):
            hi, lo = split2(x_ref[t, h])
            places = ((768, hi), (832, lo), (896, hi))
            if h < 4:
                places = ((64 * h, hi), (256 + 64 * h, lo), (512 + 64 * h, hi))
            for base, part in places:
                xs_ref[base : base + 64, lanes] = part
        for face in (2, 3):
            take_trace(t, face)

    own = dot(a_ref[:, 0:960], xs_ref[...])
    keep = 1.0 - 0.1 * drag_ref[...]
    for t in range(tiles):
        lanes = slice(128 * t, 128 * t + 128)
        for c in range(5):
            x = x_ref[t, c]
            scaled = x * keep[:, lanes] if 1 <= c <= 3 else x
            acc_ref[t, c] = scaled + own[64 * c : 64 * c + 64, lanes]

    rows_src = lax.broadcasted_iota(jnp.int32, (elems, elems), 0).astype(jnp.int16)
    def gather(f):
        g = f + 1 - 2 * (f % 2)
        ids = jnp.broadcast_to(nbr_ref[f : f + 1, :], (elems, elems)).astype(jnp.int16)
        both = dot(tr_ref[g], one_hot(rows_src == ids))
        both = both[:80] + both[80:]
        for t in range(tiles):
            parts = [both[16 * h : 16 * h + 16, 128 * t : 128 * t + 128] for h in range(5)]
            add_face(acc_ref, t, f, [mixed(coef_ref, f, c, parts) for c in range(5)])

    for f in (0, 1, 2):
        gather(f)

    @pl.when(jnp.logical_not(has_low))
    def _():
        pl.semaphore_wait(far_sem, 1)
        down_b.start()

    for f in (3, 4, 5):
        gather(f)

    up_x.wait()
    down_x.wait()

    @pl.when(has_high)
    def _():
        up_z.wait_send()
        down_z.wait_recv()

    @pl.when(has_low)
    def _():
        down_z.wait_send()
        up_z.wait_recv()

    for i, face in enumerate(SIDES):
        both = dot_nt(jnp.concatenate(split2(recv_ref[i]), axis=0), oh_ref[i])
        both = both[:80] + both[80:]
        for t in range(tiles):
            lanes = slice(128 * t, 128 * t + 128)
            add_face(acc_ref, t, face, [both[16 * c : 16 * c + 16, lanes] for c in range(5)])

    up_b.wait()
    down_b.wait()
    sums = bsend_ref[1] + brecv_ref[0] + brecv_ref[1]
    grad_ref[...] = sums[0, :owned]


def finish(acc_ref, sums_ref, out_ref, grad_ref, sem):
    tiles = acc_ref.shape[0]
    copies = [pltpu.make_async_copy(sums_ref, grad_ref, sem.at[tiles])]
    for t in range(tiles):
        place = out_ref.at[:, :, pl.ds(128 * t, 128)]
        copies.append(pltpu.make_async_copy(acc_ref.at[t], place, sem.at[t]))
    for copy in copies:
        copy.start()
    for copy in copies:
        copy.wait()


def on_device(
    sectors,
    slabs,
    adjoint,
    velocity,
    drag,
    block_weight,
    flux_jac,
    face_own,
    face_nbr,
    nbr_local,
    sector_slots,
    axial_slots,
    sector_live,
    elem_block,
):
    elems = adjoint.shape[2]
    tiles = elems // 128
    slots = sector_slots.shape[1]
    owned = BLOCKS // (sectors * slabs)
    width = -(-owned // 128) * 128
    operands = (
        adjoint,
        velocity,
        drag.reshape(1, elems),
        block_weight.reshape(1, elems),
        jnp.transpose(flux_jac, (1, 0, 2)),
        jnp.transpose(face_own, (1, 0, 2)),
        jnp.transpose(face_nbr, (1, 0, 2)),
        nbr_local,
        sector_slots,
        axial_slots,
        sector_live.reshape(1, 2),
        elem_block.reshape(1, elems),
        *constant_tables(),
    )
    vmem = pl.BlockSpec(memory_space=pltpu.VMEM)
    hbm = pl.BlockSpec(memory_space=pltpu.HBM)
    handed = pl.pallas_call(
        functools.partial(exchange, sectors, slabs, owned),
        out_shape=(
            pltpu.VMEM((tiles, 5, 64, 128), F32),
            pltpu.VMEM((owned,), F32),
        ),
        in_specs=[hbm] * INPUTS,
        out_specs=(vmem,) * 2,
        scratch_shapes=[pltpu.VMEM((tiles, 5, 64, 128), F32)]
        + [pltpu.VMEM(a.shape, a.dtype) for a in operands[1:]]
        + [
            pltpu.VMEM((960, elems), BF),
            pltpu.VMEM((6, 160, elems), BF),
            pltpu.VMEM((4, elems, slots), BF),
            pltpu.VMEM((4, 80, slots), F32),
            pltpu.VMEM((4, 80, slots), F32),
            pltpu.VMEM((320, 1024), BF),
            pltpu.VMEM((25, 6, 128), F32),
            pltpu.VMEM((3, 8, width), F32),
            pltpu.VMEM((2, 8, width), F32),
            pltpu.SemaphoreType.DMA((6,)),
            pltpu.SemaphoreType.DMA((6,)),
            pltpu.SemaphoreType.REGULAR,
            pltpu.SemaphoreType.DMA((INPUTS,)),
            pltpu.SemaphoreType.DMA((5 * tiles,)),
        ],
        compiler_params=pltpu.CompilerParams(
            collective_id=0, has_side_effects=True, vmem_limit_bytes=60 * 1024 * 1024
        ),
    )(*operands)
    return pl.pallas_call(
        finish,
        out_shape=(
            jax.ShapeDtypeStruct(adjoint.shape, F32),
            jax.ShapeDtypeStruct((owned,), F32),
        ),
        in_specs=[vmem] * 2,
        out_specs=(hbm, hbm),
        scratch_shapes=[
            pltpu.SemaphoreType.DMA((tiles + 1,)),
        ],
        compiler_params=pltpu.CompilerParams(vmem_limit_bytes=40 * 1024 * 1024),
    )(*handed)


def solution(mesh):
    placed = (
        P(None, None, ("sector", "axial")),
        P(None, None, ("sector", "axial")),
        P(("sector", "axial")),
        P(("sector", "axial")),
        P(),
        P(),
        P(),
        P(None, ("sector", "axial")),
        P(None, ("sector", "axial")),
        P(None, ("sector", "axial")),
        P("sector", "axial", None),
        P(("sector", "axial")),
    )
    return jax.shard_map(
        functools.partial(on_device, mesh.shape["sector"], mesh.shape["axial"]),
        mesh=mesh,
        in_specs=placed,
        out_specs=(P(None, None, ("sector", "axial")), P(("sector", "axial"))),
        check_vma=False,
    )
```

```python
import functools

import jax
import jax.numpy as jnp
import numpy as np
from jax import lax
from jax.experimental import pallas as pl
from jax.experimental.pallas import tpu as pltpu
from jax.sharding import PartitionSpec as P

BLOCKS = 4096
BF = jnp.bfloat16
F32 = jnp.float32
MESH = pl.DeviceIdType.MESH
INPUTS = 14
SIDES = (0, 1, 4, 5)


def lobatto_tables():
    points = np.array([-1.0, -1.0 / np.sqrt(5.0), 1.0 / np.sqrt(5.0), 1.0])
    weights = np.array([1.0, 5.0, 5.0, 1.0]) / 6.0
    scales = np.array(
        [np.prod([points[i] - points[k] for k in range(4) if k != i]) for i in range(4)]
    )
    derivative = np.zeros((4, 4))
    for i in range(4):
        for p in range(4):
            if i != p:
                derivative[i, p] = scales[i] / scales[p] / (points[i] - points[p])
            else:
                derivative[i, p] = sum((1.0 / (points[i] - points[k]) for k in range(4) if k != i))
    node_weight = (
        weights[:, None, None] * weights[None, :, None] * weights[None, None, :]
    ).reshape(64) / 8.0
    return (derivative, node_weight)


def constant_tables():
    derivative, node_weight = lobatto_tables()
    eye = np.eye(4)
    step = derivative.T
    mats = [
        np.kron(np.kron(step, eye), eye),
        np.kron(np.kron(eye, step), eye),
        np.kron(np.kron(eye, eye), step),
    ]
    nodes = np.arange(64).reshape(4, 4, 4)
    faces = [nodes[0], nodes[3], nodes[:, 0], nodes[:, 3], nodes[:, :, 0], nodes[:, :, 3]]
    for ids in faces:
        diag = np.zeros((64, 64))
        diag[ids.reshape(16), ids.reshape(16)] = 1.0
        mats.append(diag)
    mats = [0.1 * np.concatenate([m, m], axis=1) for m in mats]
    weights = np.repeat(node_weight[:, None], 128, axis=1)
    return jnp.asarray(np.stack(mats), F32), jnp.asarray(weights, F32)


def split2(x):
    hi = x.astype(BF)
    return hi, (x - hi.astype(F32)).astype(BF)


def dot(a, b):
    return jnp.dot(a, b, preferred_element_type=F32)


def dot_nt(a, b):
    return lax.dot_general(a, b, (((1,), (1,)), ((), ())), preferred_element_type=F32)


def one_hot(mask):
    return jnp.where(mask, jnp.ones((), BF), jnp.zeros((), BF))


def add_face(ref, tile, face, part):
    low = lax.broadcasted_iota(jnp.int32, (8, 128), 0) < 4
    for c in range(5):
        rows = part[c]
        if face < 2:
            ids = pl.ds(48 * face, 16)
            ref[tile, c, ids, :] = ref[tile, c, ids, :] + rows
        elif face >= 4:
            ids = pl.ds(3 * (face - 4), 16, stride=4)
            ref[tile, c, ids, :] = ref[tile, c, ids, :] + rows
        else:
            for v in range(2):
                both = rows[8 * v : 8 * v + 8]
                turned = pltpu.roll(both, 4, 0)
                for k in range(2):
                    ids = pl.ds(32 * v + 16 * k + 8 * (face - 2), 8)
                    value = both if k == face - 2 else turned
                    mask = low if face == 2 else jnp.logical_not(low)
                    ref[tile, c, ids, :] = ref[tile, c, ids, :] + jnp.where(mask, value, 0.0)


def mixed(coef_ref, face, c, parts):
    total = coef_ref[5 * c, face : face + 1, :] * parts[0]
    for h in range(1, 5):
        total += coef_ref[5 * c + h, face : face + 1, :] * parts[h]
    return total


def face_rows(ref, tile, c, face):
    if face < 2:
        return ref[tile, c, 48 * face : 48 * face + 16, :]
    if face >= 4:
        return ref[tile, c, pl.ds(3 * (face - 4), 16, stride=4), :]
    low = lax.broadcasted_iota(jnp.int32, (8, 128), 0) < 4
    out = []
    for v in range(2):
        first = ref[tile, c, 32 * v + 8 * (face - 2) : 32 * v + 8 * (face - 2) + 8, :]
        second = ref[tile, c, 32 * v + 16 + 8 * (face - 2) : 32 * v + 24 + 8 * (face - 2), :]
        if face == 2:
            out.append(jnp.where(low, first, pltpu.roll(second, 4, 0)))
        else:
            out.append(jnp.where(low, pltpu.roll(first, 4, 0), second))
    return jnp.concatenate(out, axis=0)


def exchange(sectors, slabs, owned, *refs):
    hbm_refs = refs[:INPUTS]
    acc_ref, grad_ref = refs[INPUTS : INPUTS + 2]
    x_ref = refs[INPUTS + 2]
    vmem_refs = (None,) + refs[INPUTS + 3 : 2 * INPUTS + 2]
    (
        _,
        vel_ref,
        drag_ref,
        bw_ref,
        jac_ref,
        own_ref,
        nbrmat_ref,
        nbr_ref,
        sslots_ref,
        aslots_ref,
        live_ref,
        eb_ref,
        mats_ref,
        weight_ref,
    ) = vmem_refs
    (
        xs_ref,
        tr_ref,
        oh_ref,
        send_ref,
        recv_ref,
        a_ref,
        coef_ref,
        bsend_ref,
        brecv_ref,
        send_sem,
        recv_sem,
        far_sem,
        load_sem,
        x_sem,
    ) = refs[2 * INPUTS + 2 :]
    tiles = x_ref.shape[0]
    elems = tiles * 128
    slots = sslots_ref.shape[1]
    width = bsend_ref.shape[2]
    count = sectors * slabs

    loads = {
        k: pltpu.make_async_copy(hbm_refs[k], vmem_refs[k], load_sem.at[k])
        for k in range(1, INPUTS)
    }
    fields = {
        (t, h): pltpu.make_async_copy(
            hbm_refs[0].at[h, :, pl.ds(128 * t, 128)], x_ref.at[t, h], x_sem.at[5 * t + h]
        )
        for h in (1, 2, 3, 0, 4)
        for t in range(tiles)
    }
    for k in (9, 6):
        loads[k].start()
    for key in fields:
        fields[key].start()
    for k in (8, 10, 1, 13, 2, 3, 11, 7, 12, 4, 5):
        loads[k].start()

    sec = lax.axis_index("sector")
    axi = lax.axis_index("axial")
    joint = sec * slabs + axi
    prev = lax.rem(joint + count - 1, count)
    nxt = lax.rem(joint + 1, count)
    dev_prev = (prev // slabs, lax.rem(prev, slabs))
    dev_next = (nxt // slabs, lax.rem(nxt, slabs))
    dev_low = (lax.rem(sec + sectors - 1, sectors), axi)
    dev_high = (lax.rem(sec + 1, sectors), axi)

    has_low = axi > 0
    has_high = axi < slabs - 1

    barrier = pltpu.get_barrier_semaphore()

    def greet(device):
        pl.semaphore_signal(barrier, inc=1, device_id=device, device_id_type=MESH)

    greet(dev_low)
    greet(dev_high)
    greet(dev_prev)

    @pl.when(has_high)
    def _():
        greet(dev_next)

    def remote(src, dst, k, device):
        return pltpu.make_async_remote_copy(
            src_ref=src,
            dst_ref=dst,
            send_sem=send_sem.at[k],
            recv_sem=recv_sem.at[k],
            device_id=device,
            device_id_type=MESH,
        )

    up_x = remote(send_ref.at[1], recv_ref.at[0], 0, dev_high)
    down_x = remote(send_ref.at[0], recv_ref.at[1], 1, dev_low)
    up_z = remote(send_ref.at[3], recv_ref.at[2], 2, dev_next)
    down_z = remote(send_ref.at[2], recv_ref.at[3], 3, dev_prev)
    up_b = remote(bsend_ref.at[2], brecv_ref.at[0], 4, dev_next)
    down_b = remote(bsend_ref.at[0], brecv_ref.at[1], 5, dev_prev)

    slot_ids = lax.broadcasted_iota(jnp.int32, (1, slots), 1)
    rows_slots = lax.broadcasted_iota(jnp.int32, (elems, slots), 0).astype(jnp.int16)

    def find_slots(i, ids):
        ids = jnp.broadcast_to(ids, (elems, slots)).astype(jnp.int16)
        oh_ref[i] = one_hot(rows_slots == ids)

    def take_trace(t, face):
        lanes = slice(128 * t, 128 * t + 128)
        for c in range(5):
            hi, lo = split2(face_rows(x_ref, t, c, face))
            tr_ref[face, 16 * c : 16 * c + 16, lanes] = hi
            tr_ref[face, 80 + 16 * c : 96 + 16 * c, lanes] = lo

    def fill_send(i):
        face = SIDES[i]
        for t in range(tiles):
            take_trace(t, face)
        both = dot(tr_ref[face], oh_ref[i])
        both = both[:80] + both[80:]
        for n in range(0, slots, 128):
            parts = [both[16 * h : 16 * h + 16, n : n + 128] for h in range(5)]
            for c in range(5):
                value = mixed(coef_ref, face + 1 - 2 * (face % 2), c, parts)
                send_ref[i, 16 * c : 16 * c + 16, n : n + 128] = value

    loads[9].wait()
    for i in (2, 3):
        find_slots(i, aslots_ref[i - 2 : i - 1, :])
    loads[6].wait()
    for c in range(5):
        for h in range(5):
            coef_ref[5 * c + h] = jnp.broadcast_to(0.1 * nbrmat_ref[c][:, h : h + 1], (6, 128))
    for key in fields:
        fields[key].wait()
    def sum_blocks():
        for k in (1, 13, 2, 3, 11):
            loads[k].wait()
        parts = []
        for t in range(tiles):
            lanes = slice(128 * t, 128 * t + 128)
            total = x_ref[t, 1] * vel_ref[0, :, lanes].astype(F32)
            total += x_ref[t, 2] * vel_ref[1, :, lanes].astype(F32)
            total += x_ref[t, 3] * vel_ref[2, :, lanes].astype(F32)
            parts.append(jnp.sum(total * weight_ref[...], axis=0, keepdims=True))
        elem_grad = drag_ref[...] * jnp.concatenate(parts, axis=1)
        weighted = bw_ref[...] * elem_grad
        w1 = weighted.astype(BF)
        rest = weighted - w1.astype(F32)
        w2 = rest.astype(BF)
        w3 = (rest - w2.astype(F32)).astype(BF).astype(F32)
        row16 = lax.broadcasted_iota(jnp.int32, (16, elems), 0)
        stack = jnp.where(row16 == 0, w1.astype(F32), 0.0)
        stack = jnp.where(row16 == 1, w2.astype(F32), stack)
        stack = jnp.where(row16 == 2, w3, stack).astype(BF)
        rel = eb_ref[...] - (joint - 1) * owned
        rel = jnp.where(rel < 0, rel + BLOCKS, rel)
        rel = jnp.where(rel >= BLOCKS, rel - BLOCKS, rel)
        rows_blk = lax.broadcasted_iota(jnp.int32, (width, elems), 0).astype(jnp.int16)
        for j in range(3):
            ids = jnp.broadcast_to(rel - j * owned, (width, elems)).astype(jnp.int16)
            sums = dot_nt(stack, one_hot(rows_blk == ids))
            total = jnp.sum(sums, axis=0, keepdims=True)
            bsend_ref[j] = jnp.broadcast_to(total, (8, width))

    @pl.when(jnp.logical_not(has_high))
    def _():
        sum_blocks()
        pl.semaphore_wait(barrier, 4)
        pl.semaphore_signal(far_sem, inc=1, device_id=dev_next, device_id_type=MESH)
        up_b.start()
        down_b.start()

    fill_send(2)
    fill_send(3)

    @pl.when(jnp.logical_and(has_low, has_high))
    def _():
        pl.semaphore_wait(barrier, 4)

    @pl.when(jnp.logical_not(has_low))
    def _():
        pl.semaphore_wait(barrier, 3)

    @pl.when(has_high)
    def _():
        up_z.start()

    @pl.when(has_low)
    def _():
        down_z.start()

    @pl.when(jnp.logical_not(has_low))
    def _():
        recv_ref[2] = jnp.zeros((80, slots), F32)

    @pl.when(jnp.logical_not(has_high))
    def _():
        recv_ref[3] = jnp.zeros((80, slots), F32)

    loads[8].wait()
    loads[10].wait()
    for i in (0, 1):
        live = slot_ids < live_ref[:, i : i + 1]
        find_slots(i, jnp.where(live, sslots_ref[i : i + 1, :], -1))
    fill_send(0)
    fill_send(1)
    up_x.start()
    down_x.start()

    @pl.when(has_high)
    def _():
        sum_blocks()
        up_b.start()

    @pl.when(jnp.logical_and(has_low, has_high))
    def _():
        down_b.start()

    for k in (7, 12, 4, 5):
        loads[k].wait()

    spread = jnp.minimum(lax.broadcasted_iota(jnp.int32, (5, 384), 1) // 64, 4)
    spread = jnp.where(spread == lax.broadcasted_iota(jnp.int32, (5, 384), 0), 1.0, 0.0)
    for c in range(5):
        rows = slice(64 * c, 64 * c + 64)
        jac = jac_ref[0][:, c : c + 1] * spread[0:1, :]
        face = own_ref[c][:, 0:1] * spread[0:1, :]
        for h in range(1, 5):
            jac += jac_ref[h][:, c : c + 1] * spread[h : h + 1, :]
            face += own_ref[c][:, h : h + 1] * spread[h : h + 1, :]
        for t in range(3):
            lanes = slice(128 * t, 128 * t + 128)
            total = mats_ref[0] * jac[0:1, lanes]
            for j in range(1, 9):
                row = jac[j : j + 1, lanes] if j < 3 else face[j - 3 : j - 2, lanes]
                total += mats_ref[j] * row
            hi, lo = split2(total)
            places = ((768, hi), (896, lo)) if t == 2 else ((0, hi), (256, hi), (512, lo))
            for base, part in places:
                base += 128 * t if t < 2 else 0
                a_ref[rows, base : base + 128] = part

    for t in range(tiles):
        lanes = slice(128 * t, 128 * t + 128)
        for h in range(5):
            hi, lo = split2(x_ref[t, h])
            places = ((768, hi), (832, lo), (896, hi))
            if h < 4:
                places = ((64 * h, hi), (256 + 64 * h, lo), (512 + 64 * h, hi))
            for base, part in places:
                xs_ref[base : base + 64, lanes] = part
        for face in (2, 3):
            take_trace(t, face)

    own = dot(a_ref[:, 0:960], xs_ref[...])
    keep = 1.0 - 0.1 * drag_ref[...]
    for t in range(tiles):
        lanes = slice(128 * t, 128 * t + 128)
        for c in range(5):
            x = x_ref[t, c]
            scaled = x * keep[:, lanes] if 1 <= c <= 3 else x
            acc_ref[t, c] = scaled + own[64 * c : 64 * c + 64, lanes]

    rows_src = lax.broadcasted_iota(jnp.int32, (elems, elems), 0).astype(jnp.int16)
    def gather(f):
        g = f + 1 - 2 * (f % 2)
        ids = jnp.broadcast_to(nbr_ref[f : f + 1, :], (elems, elems)).astype(jnp.int16)
        both = dot(tr_ref[g], one_hot(rows_src == ids))
        both = both[:80] + both[80:]
        for t in range(tiles):
            parts = [both[16 * h : 16 * h + 16, 128 * t : 128 * t + 128] for h in range(5)]
            add_face(acc_ref, t, f, [mixed(coef_ref, f, c, parts) for c in range(5)])

    for f in (0, 1, 2):
        gather(f)

    @pl.when(jnp.logical_not(has_low))
    def _():
        pl.semaphore_wait(far_sem, 1)
        down_b.start()

    for f in (3, 4, 5):
        gather(f)

    up_x.wait()
    down_x.wait()

    @pl.when(has_high)
    def _():
        up_z.wait_send()
        down_z.wait_recv()

    @pl.when(has_low)
    def _():
        down_z.wait_send()
        up_z.wait_recv()

    for i, face in enumerate(SIDES):
        both = dot_nt(jnp.concatenate(split2(recv_ref[i]), axis=0), oh_ref[i])
        both = both[:80] + both[80:]
        for t in range(tiles):
            lanes = slice(128 * t, 128 * t + 128)
            add_face(acc_ref, t, face, [both[16 * c : 16 * c + 16, lanes] for c in range(5)])

    up_b.wait()
    down_b.wait()
    sums = bsend_ref[1] + brecv_ref[0] + brecv_ref[1]
    grad_ref[...] = sums[0, :owned]


def finish(acc_ref, sums_ref, out_ref, grad_ref, sem):
    tiles = acc_ref.shape[0]
    copies = [pltpu.make_async_copy(sums_ref, grad_ref, sem.at[tiles])]
    for t in range(tiles):
        place = out_ref.at[:, :, pl.ds(128 * t, 128)]
        copies.append(pltpu.make_async_copy(acc_ref.at[t], place, sem.at[t]))
    for copy in copies:
        copy.start()
    for copy in copies:
        copy.wait()


def on_device(
    sectors,
    slabs,
    adjoint,
    velocity,
    drag,
    block_weight,
    flux_jac,
    face_own,
    face_nbr,
    nbr_local,
    sector_slots,
    axial_slots,
    sector_live,
    elem_block,
):
    elems = adjoint.shape[2]
    tiles = elems // 128
    slots = sector_slots.shape[1]
    owned = BLOCKS // (sectors * slabs)
    width = -(-owned // 128) * 128
    operands = (
        adjoint,
        velocity,
        drag.reshape(1, elems),
        block_weight.reshape(1, elems),
        jnp.transpose(flux_jac, (1, 0, 2)),
        jnp.transpose(face_own, (1, 0, 2)),
        jnp.transpose(face_nbr, (1, 0, 2)),
        nbr_local,
        sector_slots,
        axial_slots,
        sector_live.reshape(1, 2),
        elem_block.reshape(1, elems),
        *constant_tables(),
    )
    vmem = pl.BlockSpec(memory_space=pltpu.VMEM)
    hbm = pl.BlockSpec(memory_space=pltpu.HBM)
    handed = pl.pallas_call(
        functools.partial(exchange, sectors, slabs, owned),
        out_shape=(
            pltpu.VMEM((tiles, 5, 64, 128), F32),
            pltpu.VMEM((owned,), F32),
        ),
        in_specs=[hbm] * INPUTS,
        out_specs=(vmem,) * 2,
        scratch_shapes=[pltpu.VMEM((tiles, 5, 64, 128), F32)]
        + [pltpu.VMEM(a.shape, a.dtype) for a in operands[1:]]
        + [
            pltpu.VMEM((960, elems), BF),
            pltpu.VMEM((6, 160, elems), BF),
            pltpu.VMEM((4, elems, slots), BF),
            pltpu.VMEM((4, 80, slots), F32),
            pltpu.VMEM((4, 80, slots), F32),
            pltpu.VMEM((320, 1024), BF),
            pltpu.VMEM((25, 6, 128), F32),
            pltpu.VMEM((3, 8, width), F32),
            pltpu.VMEM((2, 8, width), F32),
            pltpu.SemaphoreType.DMA((6,)),
            pltpu.SemaphoreType.DMA((6,)),
            pltpu.SemaphoreType.REGULAR,
            pltpu.SemaphoreType.DMA((INPUTS,)),
            pltpu.SemaphoreType.DMA((5 * tiles,)),
        ],
        compiler_params=pltpu.CompilerParams(
            collective_id=0, has_side_effects=True, vmem_limit_bytes=60 * 1024 * 1024
        ),
    )(*operands)
    return pl.pallas_call(
        finish,
        out_shape=(
            jax.ShapeDtypeStruct(adjoint.shape, F32),
            jax.ShapeDtypeStruct((owned,), F32),
        ),
        in_specs=[vmem] * 2,
        out_specs=(hbm, hbm),
        scratch_shapes=[
            pltpu.SemaphoreType.DMA((tiles + 1,)),
        ],
        compiler_params=pltpu.CompilerParams(vmem_limit_bytes=40 * 1024 * 1024),
    )(*handed)


def solution(mesh):
    placed = (
        P(None, None, ("sector", "axial")),
        P(None, None, ("sector", "axial")),
        P(("sector", "axial")),
        P(("sector", "axial")),
        P(),
        P(),
        P(),
        P(None, ("sector", "axial")),
        P(None, ("sector", "axial")),
        P(None, ("sector", "axial")),
        P("sector", "axial", None),
        P(("sector", "axial")),
    )
    return jax.shard_map(
        functools.partial(on_device, mesh.shape["sector"], mesh.shape["axial"]),
        mesh=mesh,
        in_specs=placed,
        out_specs=(P(None, None, ("sector", "axial")), P(("sector", "axial"))),
        check_vma=False,
    )
```

```python
import functools

import jax
import jax.numpy as jnp
import numpy as np
from jax import lax
from jax.experimental import pallas as pl
from jax.experimental.pallas import tpu as pltpu
from jax.sharding import PartitionSpec as P

BLOCKS = 4096
BF = jnp.bfloat16
F32 = jnp.float32
MESH = pl.DeviceIdType.MESH
INPUTS = 14
SIDES = (0, 1, 4, 5)


def lobatto_tables():
    points = np.array([-1.0, -1.0 / np.sqrt(5.0), 1.0 / np.sqrt(5.0), 1.0])
    weights = np.array([1.0, 5.0, 5.0, 1.0]) / 6.0
    scales = np.array(
        [np.prod([points[i] - points[k] for k in range(4) if k != i]) for i in range(4)]
    )
    derivative = np.zeros((4, 4))
    for i in range(4):
        for p in range(4):
            if i != p:
                derivative[i, p] = scales[i] / scales[p] / (points[i] - points[p])
            else:
                derivative[i, p] = sum((1.0 / (points[i] - points[k]) for k in range(4) if k != i))
    node_weight = (
        weights[:, None, None] * weights[None, :, None] * weights[None, None, :]
    ).reshape(64) / 8.0
    return (derivative, node_weight)


def constant_tables():
    derivative, node_weight = lobatto_tables()
    eye = np.eye(4)
    step = derivative.T
    mats = [
        np.kron(np.kron(step, eye), eye),
        np.kron(np.kron(eye, step), eye),
        np.kron(np.kron(eye, eye), step),
    ]
    nodes = np.arange(64).reshape(4, 4, 4)
    faces = [nodes[0], nodes[3], nodes[:, 0], nodes[:, 3], nodes[:, :, 0], nodes[:, :, 3]]
    for ids in faces:
        diag = np.zeros((64, 64))
        diag[ids.reshape(16), ids.reshape(16)] = 1.0
        mats.append(diag)
    mats = [0.1 * np.concatenate([m, m], axis=1) for m in mats]
    weights = np.repeat(node_weight[:, None], 128, axis=1)
    return jnp.asarray(np.stack(mats), F32), jnp.asarray(weights, F32)


def split2(x):
    hi = x.astype(BF)
    return hi, (x - hi.astype(F32)).astype(BF)


def dot(a, b):
    return jnp.dot(a, b, preferred_element_type=F32)


def dot_nt(a, b):
    return lax.dot_general(a, b, (((1,), (1,)), ((), ())), preferred_element_type=F32)


def one_hot(mask):
    return jnp.where(mask, jnp.ones((), BF), jnp.zeros((), BF))


def add_face(ref, tile, face, part):
    low = lax.broadcasted_iota(jnp.int32, (8, 128), 0) < 4
    for c in range(5):
        rows = part[c]
        if face < 2:
            ids = pl.ds(48 * face, 16)
            ref[tile, c, ids, :] = ref[tile, c, ids, :] + rows
        elif face >= 4:
            ids = pl.ds(3 * (face - 4), 16, stride=4)
            ref[tile, c, ids, :] = ref[tile, c, ids, :] + rows
        else:
            for v in range(2):
                both = rows[8 * v : 8 * v + 8]
                turned = pltpu.roll(both, 4, 0)
                for k in range(2):
                    ids = pl.ds(32 * v + 16 * k + 8 * (face - 2), 8)
                    value = both if k == face - 2 else turned
                    mask = low if face == 2 else jnp.logical_not(low)
                    ref[tile, c, ids, :] = ref[tile, c, ids, :] + jnp.where(mask, value, 0.0)


def mixed(coef_ref, face, c, parts):
    total = coef_ref[5 * c, face : face + 1, :] * parts[0]
    for h in range(1, 5):
        total += coef_ref[5 * c + h, face : face + 1, :] * parts[h]
    return total


def face_rows(ref, tile, c, face):
    if face < 2:
        return ref[tile, c, 48 * face : 48 * face + 16, :]
    if face >= 4:
        return ref[tile, c, pl.ds(3 * (face - 4), 16, stride=4), :]
    low = lax.broadcasted_iota(jnp.int32, (8, 128), 0) < 4
    out = []
    for v in range(2):
        first = ref[tile, c, 32 * v + 8 * (face - 2) : 32 * v + 8 * (face - 2) + 8, :]
        second = ref[tile, c, 32 * v + 16 + 8 * (face - 2) : 32 * v + 24 + 8 * (face - 2), :]
        if face == 2:
            out.append(jnp.where(low, first, pltpu.roll(second, 4, 0)))
        else:
            out.append(jnp.where(low, pltpu.roll(first, 4, 0), second))
    return jnp.concatenate(out, axis=0)


def exchange(sectors, slabs, owned, *refs):
    hbm_refs = refs[:INPUTS]
    acc_ref, grad_ref = refs[INPUTS : INPUTS + 2]
    x_ref = refs[INPUTS + 2]
    vmem_refs = (None,) + refs[INPUTS + 3 : 2 * INPUTS + 2]
    (
        _,
        vel_ref,
        drag_ref,
        bw_ref,
        jac_ref,
        own_ref,
        nbrmat_ref,
        nbr_ref,
        sslots_ref,
        aslots_ref,
        live_ref,
        eb_ref,
        mats_ref,
        weight_ref,
    ) = vmem_refs
    (
        xs_ref,
        tr_ref,
        oh_ref,
        place_ref,
        send_ref,
        recv_ref,
        a_ref,
        coef_ref,
        bsend_ref,
        brecv_ref,
        send_sem,
        recv_sem,
        far_sem,
        load_sem,
        x_sem,
    ) = refs[2 * INPUTS + 2 :]
    tiles = x_ref.shape[0]
    elems = tiles * 128
    slots = sslots_ref.shape[1]
    width = bsend_ref.shape[2]
    count = sectors * slabs

    loads = {
        k: pltpu.make_async_copy(hbm_refs[k], vmem_refs[k], load_sem.at[k])
        for k in range(1, INPUTS)
    }
    fields = {
        (t, h): pltpu.make_async_copy(
            hbm_refs[0].at[h, :, pl.ds(128 * t, 128)], x_ref.at[t, h], x_sem.at[5 * t + h]
        )
        for h in (1, 2, 3, 0, 4)
        for t in range(tiles)
    }
    for k in (9, 8, 10):
        loads[k].start()
    for key in fields:
        fields[key].start()
    for k in (6, 1, 13, 2, 3, 11, 7, 12, 4, 5):
        loads[k].start()

    sec = lax.axis_index("sector")
    axi = lax.axis_index("axial")
    joint = sec * slabs + axi
    prev = lax.rem(joint + count - 1, count)
    nxt = lax.rem(joint + 1, count)
    dev_prev = (prev // slabs, lax.rem(prev, slabs))
    dev_next = (nxt // slabs, lax.rem(nxt, slabs))
    dev_low = (lax.rem(sec + sectors - 1, sectors), axi)
    dev_high = (lax.rem(sec + 1, sectors), axi)

    has_low = axi > 0
    has_high = axi < slabs - 1

    barrier = pltpu.get_barrier_semaphore()

    def greet(device):
        pl.semaphore_signal(barrier, inc=1, device_id=device, device_id_type=MESH)

    greet(dev_low)
    greet(dev_high)
    greet(dev_prev)

    @pl.when(has_high)
    def _():
        greet(dev_next)

    def remote(src, dst, k, device):
        return pltpu.make_async_remote_copy(
            src_ref=src,
            dst_ref=dst,
            send_sem=send_sem.at[k],
            recv_sem=recv_sem.at[k],
            device_id=device,
            device_id_type=MESH,
        )

    up_x = remote(send_ref.at[1], recv_ref.at[0], 0, dev_high)
    down_x = remote(send_ref.at[0], recv_ref.at[1], 1, dev_low)
    up_z = remote(send_ref.at[3], recv_ref.at[2], 2, dev_next)
    down_z = remote(send_ref.at[2], recv_ref.at[3], 3, dev_prev)
    up_b = remote(bsend_ref.at[2], brecv_ref.at[0], 4, dev_next)
    down_b = remote(bsend_ref.at[0], brecv_ref.at[1], 5, dev_prev)

    slot_ids = lax.broadcasted_iota(jnp.int32, (1, slots), 1)
    rows_slots = lax.broadcasted_iota(jnp.int32, (elems, slots), 0).astype(jnp.int16)

    columns = lax.broadcasted_iota(jnp.int32, (slots, elems), 1).astype(jnp.int16)

    def slot_row(i):
        if i >= 2:
            return aslots_ref[i - 2 : i - 1, :]
        return jnp.where(slot_ids < live_ref[:, i : i + 1], sslots_ref[i : i + 1, :], -1)

    def find_slots(i):
        ids = jnp.broadcast_to(slot_row(i), (elems, slots)).astype(jnp.int16)
        oh_ref[i] = one_hot(rows_slots == ids)

    def find_places(i):
        ids = jnp.broadcast_to(slot_row(i), (128, slots)).T
        ids = jnp.concatenate([ids] * tiles, axis=1).astype(jnp.int16)
        place_ref[i] = one_hot(columns == ids)

    def take_trace(t, face):
        lanes = slice(128 * t, 128 * t + 128)
        for c in range(5):
            hi, lo = split2(face_rows(x_ref, t, c, face))
            tr_ref[face, 16 * c : 16 * c + 16, lanes] = hi
            tr_ref[face, 80 + 16 * c : 96 + 16 * c, lanes] = lo

    def fill_send(i):
        face = SIDES[i]
        for t in range(tiles):
            take_trace(t, face)
        both = dot(tr_ref[face], oh_ref[i])
        send_ref[i] = both[:80] + both[80:]

    for k in (9, 8, 10):
        loads[k].wait()
    for i in range(4):
        find_slots(i)
    for key in fields:
        fields[key].wait()
    def sum_blocks():
        for k in (1, 13, 2, 3, 11):
            loads[k].wait()
        parts = []
        for t in range(tiles):
            lanes = slice(128 * t, 128 * t + 128)
            total = x_ref[t, 1] * vel_ref[0, :, lanes].astype(F32)
            total += x_ref[t, 2] * vel_ref[1, :, lanes].astype(F32)
            total += x_ref[t, 3] * vel_ref[2, :, lanes].astype(F32)
            parts.append(jnp.sum(total * weight_ref[...], axis=0, keepdims=True))
        elem_grad = drag_ref[...] * jnp.concatenate(parts, axis=1)
        weighted = bw_ref[...] * elem_grad
        w1 = weighted.astype(BF)
        rest = weighted - w1.astype(F32)
        w2 = rest.astype(BF)
        w3 = (rest - w2.astype(F32)).astype(BF).astype(F32)
        row16 = lax.broadcasted_iota(jnp.int32, (16, elems), 0)
        stack = jnp.where(row16 == 0, w1.astype(F32), 0.0)
        stack = jnp.where(row16 == 1, w2.astype(F32), stack)
        stack = jnp.where(row16 == 2, w3, stack).astype(BF)
        rel = eb_ref[...] - (joint - 1) * owned
        rel = jnp.where(rel < 0, rel + BLOCKS, rel)
        rel = jnp.where(rel >= BLOCKS, rel - BLOCKS, rel)
        rows_blk = lax.broadcasted_iota(jnp.int32, (width, elems), 0).astype(jnp.int16)
        for j in range(3):
            ids = jnp.broadcast_to(rel - j * owned, (width, elems)).astype(jnp.int16)
            sums = dot_nt(stack, one_hot(rows_blk == ids))
            total = jnp.sum(sums, axis=0, keepdims=True)
            bsend_ref[j] = jnp.broadcast_to(total, (8, width))

    @pl.when(jnp.logical_not(has_high))
    def _():
        sum_blocks()
        pl.semaphore_wait(barrier, 4)
        pl.semaphore_signal(far_sem, inc=1, device_id=dev_next, device_id_type=MESH)
        up_b.start()
        down_b.start()

    fill_send(2)
    fill_send(3)

    @pl.when(jnp.logical_and(has_low, has_high))
    def _():
        pl.semaphore_wait(barrier, 4)

    @pl.when(jnp.logical_not(has_low))
    def _():
        pl.semaphore_wait(barrier, 3)

    even = axi % 2 == 0

    @pl.when(jnp.logical_and(has_high, even))
    def _():
        up_z.start()

    @pl.when(jnp.logical_and(has_low, jnp.logical_not(even)))
    def _():
        down_z.start()

    @pl.when(jnp.logical_not(has_low))
    def _():
        recv_ref[2] = jnp.zeros((80, slots), F32)

    @pl.when(jnp.logical_not(has_high))
    def _():
        recv_ref[3] = jnp.zeros((80, slots), F32)

    fill_send(0)
    fill_send(1)
    up_x.start()
    down_x.start()

    @pl.when(jnp.logical_and(has_high, jnp.logical_not(even)))
    def _():
        up_z.start()

    @pl.when(jnp.logical_and(has_low, even))
    def _():
        down_z.start()

    @pl.when(has_high)
    def _():
        sum_blocks()
        up_b.start()

    @pl.when(jnp.logical_and(has_low, has_high))
    def _():
        down_b.start()

    for k in (7, 12, 4, 5, 6):
        loads[k].wait()
    for c in range(5):
        for h in range(5):
            coef_ref[5 * c + h] = jnp.broadcast_to(0.1 * nbrmat_ref[c][:, h : h + 1], (6, 128))
    for i in range(4):
        find_places(i)

    spread = jnp.minimum(lax.broadcasted_iota(jnp.int32, (5, 384), 1) // 64, 4)
    spread = jnp.where(spread == lax.broadcasted_iota(jnp.int32, (5, 384), 0), 1.0, 0.0)
    for c in range(5):
        rows = slice(64 * c, 64 * c + 64)
        jac = jac_ref[0][:, c : c + 1] * spread[0:1, :]
        face = own_ref[c][:, 0:1] * spread[0:1, :]
        for h in range(1, 5):
            jac += jac_ref[h][:, c : c + 1] * spread[h : h + 1, :]
            face += own_ref[c][:, h : h + 1] * spread[h : h + 1, :]
        for t in range(3):
            lanes = slice(128 * t, 128 * t + 128)
            total = mats_ref[0] * jac[0:1, lanes]
            for j in range(1, 9):
                row = jac[j : j + 1, lanes] if j < 3 else face[j - 3 : j - 2, lanes]
                total += mats_ref[j] * row
            hi, lo = split2(total)
            places = ((768, hi), (896, lo)) if t == 2 else ((0, hi), (256, hi), (512, lo))
            for base, part in places:
                base += 128 * t if t < 2 else 0
                a_ref[rows, base : base + 128] = part

    for t in range(tiles):
        lanes = slice(128 * t, 128 * t + 128)
        for h in range(5):
            hi, lo = split2(x_ref[t, h])
            for base, part in ((0, hi), (256, lo)) if h < 4 else ((256, hi), (320, lo)):
                xs_ref[64 * h + base : 64 * h + base + 64, lanes] = part
        for face in (2, 3):
            take_trace(t, face)

    xs = [xs_ref[rows, :] for rows in (slice(0, 512), slice(0, 256), slice(512, 640), slice(512, 576))]
    own = dot(a_ref[:, 0:960], jnp.concatenate(xs, axis=0))
    keep = 1.0 - 0.1 * drag_ref[...]
    for t in range(tiles):
        lanes = slice(128 * t, 128 * t + 128)
        for c in range(5):
            x = x_ref[t, c]
            scaled = x * keep[:, lanes] if 1 <= c <= 3 else x
            acc_ref[t, c] = scaled + own[64 * c : 64 * c + 64, lanes]

    rows_src = lax.broadcasted_iota(jnp.int32, (elems, elems), 0).astype(jnp.int16)
    def gather(f, i=None):
        g = f + 1 - 2 * (f % 2)
        ids = jnp.broadcast_to(nbr_ref[f : f + 1, :], (elems, elems)).astype(jnp.int16)
        sources, places = tr_ref[g], one_hot(rows_src == ids)
        if i is not None:
            got = jnp.concatenate(split2(recv_ref[i]), axis=0)
            sources = jnp.concatenate([sources, got], axis=1)
            places = jnp.concatenate([places, place_ref[i]], axis=0)
        both = dot(sources, places)
        both = both[:80] + both[80:]
        for t in range(tiles):
            parts = [both[16 * h : 16 * h + 16, 128 * t : 128 * t + 128] for h in range(5)]
            add_face(acc_ref, t, f, [mixed(coef_ref, f, c, parts) for c in range(5)])

    gather(2)
    gather(3)

    @pl.when(jnp.logical_not(has_low))
    def _():
        pl.semaphore_wait(far_sem, 1)
        down_b.start()

    up_x.wait()
    down_x.wait()
    gather(0, 0)
    gather(1, 1)

    @pl.when(has_high)
    def _():
        up_z.wait_send()
        down_z.wait_recv()

    @pl.when(has_low)
    def _():
        down_z.wait_send()
        up_z.wait_recv()

    gather(4, 2)
    gather(5, 3)

    up_b.wait()
    down_b.wait()
    sums = bsend_ref[1] + brecv_ref[0] + brecv_ref[1]
    grad_ref[...] = sums[0, :owned]


def finish(acc_ref, sums_ref, out_ref, grad_ref, sem):
    tiles = acc_ref.shape[0]
    copies = [pltpu.make_async_copy(sums_ref, grad_ref, sem.at[tiles])]
    for t in range(tiles):
        place = out_ref.at[:, :, pl.ds(128 * t, 128)]
        copies.append(pltpu.make_async_copy(acc_ref.at[t], place, sem.at[t]))
    for copy in copies:
        copy.start()
    for copy in copies:
        copy.wait()


def on_device(
    sectors,
    slabs,
    adjoint,
    velocity,
    drag,
    block_weight,
    flux_jac,
    face_own,
    face_nbr,
    nbr_local,
    sector_slots,
    axial_slots,
    sector_live,
    elem_block,
):
    elems = adjoint.shape[2]
    tiles = elems // 128
    slots = sector_slots.shape[1]
    owned = BLOCKS // (sectors * slabs)
    width = -(-owned // 128) * 128
    operands = (
        adjoint,
        velocity,
        drag.reshape(1, elems),
        block_weight.reshape(1, elems),
        jnp.transpose(flux_jac, (1, 0, 2)),
        jnp.transpose(face_own, (1, 0, 2)),
        jnp.transpose(face_nbr, (1, 0, 2)),
        nbr_local,
        sector_slots,
        axial_slots,
        sector_live.reshape(1, 2),
        elem_block.reshape(1, elems),
        *constant_tables(),
    )
    vmem = pl.BlockSpec(memory_space=pltpu.VMEM)
    hbm = pl.BlockSpec(memory_space=pltpu.HBM)
    handed = pl.pallas_call(
        functools.partial(exchange, sectors, slabs, owned),
        out_shape=(
            pltpu.VMEM((tiles, 5, 64, 128), F32),
            pltpu.VMEM((owned,), F32),
        ),
        in_specs=[hbm] * INPUTS,
        out_specs=(vmem,) * 2,
        scratch_shapes=[pltpu.VMEM((tiles, 5, 64, 128), F32)]
        + [pltpu.VMEM(a.shape, a.dtype) for a in operands[1:]]
        + [
            pltpu.VMEM((640, elems), BF),
            pltpu.VMEM((6, 160, elems), BF),
            pltpu.VMEM((4, elems, slots), BF),
            pltpu.VMEM((4, slots, elems), BF),
            pltpu.VMEM((4, 80, slots), F32),
            pltpu.VMEM((4, 80, slots), F32),
            pltpu.VMEM((320, 1024), BF),
            pltpu.VMEM((25, 6, 128), F32),
            pltpu.VMEM((3, 8, width), F32),
            pltpu.VMEM((2, 8, width), F32),
            pltpu.SemaphoreType.DMA((6,)),
            pltpu.SemaphoreType.DMA((6,)),
            pltpu.SemaphoreType.REGULAR,
            pltpu.SemaphoreType.DMA((INPUTS,)),
            pltpu.SemaphoreType.DMA((5 * tiles,)),
        ],
        compiler_params=pltpu.CompilerParams(
            collective_id=0, has_side_effects=True, vmem_limit_bytes=60 * 1024 * 1024
        ),
    )(*operands)
    return pl.pallas_call(
        finish,
        out_shape=(
            jax.ShapeDtypeStruct(adjoint.shape, F32),
            jax.ShapeDtypeStruct((owned,), F32),
        ),
        in_specs=[vmem] * 2,
        out_specs=(hbm, hbm),
        scratch_shapes=[
            pltpu.SemaphoreType.DMA((tiles + 1,)),
        ],
        compiler_params=pltpu.CompilerParams(vmem_limit_bytes=40 * 1024 * 1024),
    )(*handed)


def solution(mesh):
    placed = (
        P(None, None, ("sector", "axial")),
        P(None, None, ("sector", "axial")),
        P(("sector", "axial")),
        P(("sector", "axial")),
        P(),
        P(),
        P(),
        P(None, ("sector", "axial")),
        P(None, ("sector", "axial")),
        P(None, ("sector", "axial")),
        P("sector", "axial", None),
        P(("sector", "axial")),
    )
    return jax.shard_map(
        functools.partial(on_device, mesh.shape["sector"], mesh.shape["axial"]),
        mesh=mesh,
        in_specs=placed,
        out_specs=(P(None, None, ("sector", "axial")), P(("sector", "axial"))),
        check_vma=False,
    )
```

```python
import functools

import jax
import jax.numpy as jnp
import numpy as np
from jax import lax
from jax.experimental import pallas as pl
from jax.experimental.pallas import tpu as pltpu
from jax.sharding import PartitionSpec as P

BLOCKS = 4096
BF = jnp.bfloat16
F32 = jnp.float32
MESH = pl.DeviceIdType.MESH
INPUTS = 14
SIDES = (0, 1, 4, 5)


def lobatto_tables():
    points = np.array([-1.0, -1.0 / np.sqrt(5.0), 1.0 / np.sqrt(5.0), 1.0])
    weights = np.array([1.0, 5.0, 5.0, 1.0]) / 6.0
    scales = np.array(
        [np.prod([points[i] - points[k] for k in range(4) if k != i]) for i in range(4)]
    )
    derivative = np.zeros((4, 4))
    for i in range(4):
        for p in range(4):
            if i != p:
                derivative[i, p] = scales[i] / scales[p] / (points[i] - points[p])
            else:
                derivative[i, p] = sum((1.0 / (points[i] - points[k]) for k in range(4) if k != i))
    node_weight = (
        weights[:, None, None] * weights[None, :, None] * weights[None, None, :]
    ).reshape(64) / 8.0
    return (derivative, node_weight)


def constant_tables():
    derivative, node_weight = lobatto_tables()
    eye = np.eye(4)
    step = derivative.T
    mats = [
        np.kron(np.kron(step, eye), eye),
        np.kron(np.kron(eye, step), eye),
        np.kron(np.kron(eye, eye), step),
    ]
    nodes = np.arange(64).reshape(4, 4, 4)
    faces = [nodes[0], nodes[3], nodes[:, 0], nodes[:, 3], nodes[:, :, 0], nodes[:, :, 3]]
    for ids in faces:
        diag = np.zeros((64, 64))
        diag[ids.reshape(16), ids.reshape(16)] = 1.0
        mats.append(diag)
    mats = [0.1 * np.concatenate([m, m], axis=1) for m in mats]
    weights = np.repeat(node_weight[:, None], 128, axis=1)
    return jnp.asarray(np.stack(mats), F32), jnp.asarray(weights, F32)


def split2(x):
    hi = x.astype(BF)
    return hi, (x - hi.astype(F32)).astype(BF)


def dot(a, b):
    return jnp.dot(a, b, preferred_element_type=F32)


def dot_nt(a, b):
    return lax.dot_general(a, b, (((1,), (1,)), ((), ())), preferred_element_type=F32)


def one_hot(mask):
    return jnp.where(mask, jnp.ones((), BF), jnp.zeros((), BF))


def add_face(ref, tile, face, part, axial):
    low = lax.broadcasted_iota(jnp.int32, (8, 128), 0) < 4
    for c in range(5):
        rows = part[c]
        if axial:
            ids = pl.ds(3 * (face - 4), 16, stride=4)
            ref[tile, c, ids, :] = ref[tile, c, ids, :] + rows
        elif face < 2:
            ids = pl.ds(48 * face, 16)
            ref[tile, c, ids, :] = ref[tile, c, ids, :] + rows
        else:
            for v in range(2):
                both = rows[8 * v : 8 * v + 8]
                turned = pltpu.roll(both, 4, 0)
                for k in range(2):
                    ids = pl.ds(32 * v + 16 * k + 8 * (face - 2), 8)
                    value = both if k == face - 2 else turned
                    mask = low if face == 2 else jnp.logical_not(low)
                    ref[tile, c, ids, :] = ref[tile, c, ids, :] + jnp.where(mask, value, 0.0)


def mixed(coef_ref, face, c, parts):
    total = coef_ref[5 * c, pl.ds(face, 1), :] * parts[0]
    for h in range(1, 5):
        total += coef_ref[5 * c + h, pl.ds(face, 1), :] * parts[h]
    return total


def face_rows(ref, tile, c, face, axial):
    if not axial and face < 2:
        return ref[tile, c, 48 * face : 48 * face + 16, :]
    if axial:
        return ref[tile, c, pl.ds(3 * (face - 4), 16, stride=4), :]
    low = lax.broadcasted_iota(jnp.int32, (8, 128), 0) < 4
    out = []
    for v in range(2):
        first = ref[tile, c, 32 * v + 8 * (face - 2) : 32 * v + 8 * (face - 2) + 8, :]
        second = ref[tile, c, 32 * v + 16 + 8 * (face - 2) : 32 * v + 24 + 8 * (face - 2), :]
        if face == 2:
            out.append(jnp.where(low, first, pltpu.roll(second, 4, 0)))
        else:
            out.append(jnp.where(low, pltpu.roll(first, 4, 0), second))
    return jnp.concatenate(out, axis=0)


def exchange(sectors, slabs, owned, *refs):
    hbm_refs = refs[:INPUTS]
    acc_ref, grad_ref = refs[INPUTS : INPUTS + 2]
    x_ref = refs[INPUTS + 2]
    vmem_refs = (None,) + refs[INPUTS + 3 : 2 * INPUTS + 2]
    (
        _,
        vel_ref,
        drag_ref,
        bw_ref,
        jac_ref,
        own_ref,
        nbrmat_ref,
        nbr_ref,
        sslots_ref,
        aslots_ref,
        live_ref,
        eb_ref,
        mats_ref,
        weight_ref,
    ) = vmem_refs
    (
        xs_ref,
        tr_ref,
        oh_ref,
        place_ref,
        send_ref,
        recv_ref,
        a_ref,
        coef_ref,
        bsend_ref,
        brecv_ref,
        send_sem,
        recv_sem,
        far_sem,
        load_sem,
        x_sem,
    ) = refs[2 * INPUTS + 2 :]
    tiles = x_ref.shape[0]
    elems = tiles * 128
    slots = sslots_ref.shape[1]
    width = bsend_ref.shape[2]
    count = sectors * slabs

    loads = {
        k: pltpu.make_async_copy(hbm_refs[k], vmem_refs[k], load_sem.at[k])
        for k in range(1, INPUTS)
    }
    fields = {
        (t, h): pltpu.make_async_copy(
            hbm_refs[0].at[h, :, pl.ds(128 * t, 128)], x_ref.at[t, h], x_sem.at[5 * t + h]
        )
        for h in (1, 2, 3, 0, 4)
        for t in range(tiles)
    }
    for k in (9, 8, 10):
        loads[k].start()
    for key in fields:
        fields[key].start()
    for k in (6, 1, 13, 2, 3, 11, 7, 12, 4, 5):
        loads[k].start()

    sec = lax.axis_index("sector")
    axi = lax.axis_index("axial")
    joint = sec * slabs + axi
    prev = lax.rem(joint + count - 1, count)
    nxt = lax.rem(joint + 1, count)
    dev_prev = (prev // slabs, lax.rem(prev, slabs))
    dev_next = (nxt // slabs, lax.rem(nxt, slabs))
    dev_low = (lax.rem(sec + sectors - 1, sectors), axi)
    dev_high = (lax.rem(sec + 1, sectors), axi)

    has_low = axi > 0
    has_high = axi < slabs - 1

    barrier = pltpu.get_barrier_semaphore()

    def greet(device):
        pl.semaphore_signal(barrier, inc=1, device_id=device, device_id_type=MESH)

    greet(dev_low)
    greet(dev_high)
    greet(dev_prev)

    @pl.when(has_high)
    def _():
        greet(dev_next)

    def remote(src, dst, k, device):
        return pltpu.make_async_remote_copy(
            src_ref=src,
            dst_ref=dst,
            send_sem=send_sem.at[k],
            recv_sem=recv_sem.at[k],
            device_id=device,
            device_id_type=MESH,
        )

    up_x = remote(send_ref.at[1], recv_ref.at[0], 0, dev_high)
    down_x = remote(send_ref.at[0], recv_ref.at[1], 1, dev_low)
    up_z = remote(send_ref.at[3], recv_ref.at[2], 2, dev_next)
    down_z = remote(send_ref.at[2], recv_ref.at[3], 3, dev_prev)
    up_b = remote(bsend_ref.at[2], brecv_ref.at[0], 4, dev_next)
    down_b = remote(bsend_ref.at[0], brecv_ref.at[1], 5, dev_prev)

    @pl.when(jnp.logical_not(has_high))
    def _():
        pl.semaphore_wait(barrier, 4)
        pl.semaphore_signal(far_sem, inc=1, device_id=dev_next, device_id_type=MESH)

    even = axi % 2 == 0
    first_face = 5 - axi % 2
    second_face = 4 + axi % 2
    slot_ids = lax.broadcasted_iota(jnp.int32, (1, slots), 1)
    rows_slots = lax.broadcasted_iota(jnp.int32, (elems, slots), 0).astype(jnp.int16)

    columns = lax.broadcasted_iota(jnp.int32, (slots, elems), 1).astype(jnp.int16)

    def slot_row(i):
        if i >= 2:
            return aslots_ref[i - 2 : i - 1, :]
        return jnp.where(slot_ids < live_ref[:, i : i + 1], sslots_ref[i : i + 1, :], -1)

    def find_slots(i):
        ids = jnp.broadcast_to(slot_row(i), (elems, slots)).astype(jnp.int16)
        oh_ref[i] = one_hot(rows_slots == ids)

    def find_places(i):
        ids = jnp.broadcast_to(slot_row(i), (128, slots)).T
        ids = jnp.concatenate([ids] * tiles, axis=1).astype(jnp.int16)
        place_ref[i] = one_hot(columns == ids)

    def take_trace(t, face, axial=False):
        lanes = slice(128 * t, 128 * t + 128)
        for c in range(5):
            hi, lo = split2(face_rows(x_ref, t, c, face, axial))
            tr_ref[face, 16 * c : 16 * c + 16, lanes] = hi
            tr_ref[face, 80 + 16 * c : 96 + 16 * c, lanes] = lo

    def fill_send(face, axial=False):
        i = face - 2 if axial else face
        for t in range(tiles):
            take_trace(t, face, axial)
        both = dot(tr_ref[face], oh_ref[i])
        send_ref[i] = both[:80] + both[80:]

    for k in (9, 8, 10):
        loads[k].wait()
    for i in range(4):
        find_slots(i)
    for key in fields:
        fields[key].wait()
    def sum_blocks():
        for k in (1, 13, 2, 3, 11):
            loads[k].wait()
        parts = []
        for t in range(tiles):
            lanes = slice(128 * t, 128 * t + 128)
            total = x_ref[t, 1] * vel_ref[0, :, lanes].astype(F32)
            total += x_ref[t, 2] * vel_ref[1, :, lanes].astype(F32)
            total += x_ref[t, 3] * vel_ref[2, :, lanes].astype(F32)
            parts.append(jnp.sum(total * weight_ref[...], axis=0, keepdims=True))
        elem_grad = drag_ref[...] * jnp.concatenate(parts, axis=1)
        weighted = bw_ref[...] * elem_grad
        w1 = weighted.astype(BF)
        rest = weighted - w1.astype(F32)
        w2 = rest.astype(BF)
        w3 = (rest - w2.astype(F32)).astype(BF).astype(F32)
        row16 = lax.broadcasted_iota(jnp.int32, (16, elems), 0)
        stack = jnp.where(row16 == 0, w1.astype(F32), 0.0)
        stack = jnp.where(row16 == 1, w2.astype(F32), stack)
        stack = jnp.where(row16 == 2, w3, stack).astype(BF)
        rel = eb_ref[...] - (joint - 1) * owned
        rel = jnp.where(rel < 0, rel + BLOCKS, rel)
        rel = jnp.where(rel >= BLOCKS, rel - BLOCKS, rel)
        rows_blk = lax.broadcasted_iota(jnp.int32, (width, elems), 0).astype(jnp.int16)
        for j in range(3):
            ids = jnp.broadcast_to(rel - j * owned, (width, elems)).astype(jnp.int16)
            sums = dot_nt(stack, one_hot(rows_blk == ids))
            total = jnp.sum(sums, axis=0, keepdims=True)
            bsend_ref[j] = jnp.broadcast_to(total, (8, width))

    @pl.when(jnp.logical_not(has_high))
    def _():
        sum_blocks()
        up_b.start()
        down_b.start()

    fill_send(first_face, True)

    @pl.when(jnp.logical_and(has_low, has_high))
    def _():
        pl.semaphore_wait(barrier, 4)

    @pl.when(jnp.logical_not(has_low))
    def _():
        pl.semaphore_wait(barrier, 3)

    @pl.when(jnp.logical_and(has_high, even))
    def _():
        up_z.start()

    @pl.when(jnp.logical_and(has_low, jnp.logical_not(even)))
    def _():
        down_z.start()

    fill_send(second_face, True)

    @pl.when(jnp.logical_and(has_high, jnp.logical_not(even)))
    def _():
        up_z.start()

    @pl.when(jnp.logical_and(has_low, even))
    def _():
        down_z.start()

    @pl.when(jnp.logical_not(has_low))
    def _():
        recv_ref[2] = jnp.zeros((80, slots), F32)

    @pl.when(jnp.logical_not(has_high))
    def _():
        recv_ref[3] = jnp.zeros((80, slots), F32)

    fill_send(0)
    fill_send(1)
    up_x.start()
    down_x.start()

    @pl.when(has_high)
    def _():
        sum_blocks()
        up_b.start()

    @pl.when(jnp.logical_and(has_low, has_high))
    def _():
        down_b.start()

    for k in (7, 12, 4, 5, 6):
        loads[k].wait()
    for c in range(5):
        for h in range(5):
            coef_ref[5 * c + h] = jnp.broadcast_to(0.1 * nbrmat_ref[c][:, h : h + 1], (6, 128))
    for i in range(4):
        find_places(i)

    spread = jnp.minimum(lax.broadcasted_iota(jnp.int32, (5, 384), 1) // 64, 4)
    spread = jnp.where(spread == lax.broadcasted_iota(jnp.int32, (5, 384), 0), 1.0, 0.0)
    for c in range(5):
        rows = slice(64 * c, 64 * c + 64)
        jac = jac_ref[0][:, c : c + 1] * spread[0:1, :]
        face = own_ref[c][:, 0:1] * spread[0:1, :]
        for h in range(1, 5):
            jac += jac_ref[h][:, c : c + 1] * spread[h : h + 1, :]
            face += own_ref[c][:, h : h + 1] * spread[h : h + 1, :]
        for t in range(3):
            lanes = slice(128 * t, 128 * t + 128)
            total = mats_ref[0] * jac[0:1, lanes]
            for j in range(1, 9):
                row = jac[j : j + 1, lanes] if j < 3 else face[j - 3 : j - 2, lanes]
                total += mats_ref[j] * row
            hi, lo = split2(total)
            places = ((768, hi), (896, lo)) if t == 2 else ((0, hi), (256, hi), (512, lo))
            for base, part in places:
                base += 128 * t if t < 2 else 0
                a_ref[rows, base : base + 128] = part

    for t in range(tiles):
        lanes = slice(128 * t, 128 * t + 128)
        for h in range(5):
            hi, lo = split2(x_ref[t, h])
            for base, part in ((0, hi), (256, lo)) if h < 4 else ((256, hi), (320, lo)):
                xs_ref[64 * h + base : 64 * h + base + 64, lanes] = part
        for face in (2, 3):
            take_trace(t, face)

    xs = [xs_ref[rows, :] for rows in (slice(0, 512), slice(0, 256), slice(512, 640), slice(512, 576))]
    own = dot(a_ref[:, 0:960], jnp.concatenate(xs, axis=0))
    keep = 1.0 - 0.1 * drag_ref[...]
    for t in range(tiles):
        lanes = slice(128 * t, 128 * t + 128)
        for c in range(5):
            x = x_ref[t, c]
            scaled = x * keep[:, lanes] if 1 <= c <= 3 else x
            acc_ref[t, c] = scaled + own[64 * c : 64 * c + 64, lanes]

    rows_src = lax.broadcasted_iota(jnp.int32, (elems, elems), 0).astype(jnp.int16)
    def gather(f, i=None, axial=False):
        g = 9 - f if axial else f + 1 - 2 * (f % 2)
        ids = jnp.broadcast_to(nbr_ref[pl.ds(f, 1), :], (elems, elems)).astype(jnp.int16)
        sources, places = tr_ref[g], one_hot(rows_src == ids)
        if i is not None:
            got = jnp.concatenate(split2(recv_ref[i]), axis=0)
            sources = jnp.concatenate([sources, got], axis=1)
            places = jnp.concatenate([places, place_ref[i]], axis=0)
        both = dot(sources, places)
        both = both[:80] + both[80:]
        for t in range(tiles):
            parts = [both[16 * h : 16 * h + 16, 128 * t : 128 * t + 128] for h in range(5)]
            add_face(acc_ref, t, f, [mixed(coef_ref, f, c, parts) for c in range(5)], axial)

    @pl.when(jnp.logical_not(has_low))
    def _():
        pl.semaphore_wait(far_sem, 1)
        down_b.start()

    gather(2)
    gather(3)
    up_x.wait()
    down_x.wait()
    gather(0, 0)
    gather(1, 1)

    @pl.when(jnp.logical_and(has_high, even))
    def _():
        down_z.wait_recv()

    @pl.when(jnp.logical_not(even))
    def _():
        up_z.wait_recv()

    gather(first_face, first_face - 2, True)

    @pl.when(jnp.logical_and(has_low, even))
    def _():
        up_z.wait_recv()

    @pl.when(jnp.logical_and(has_high, jnp.logical_not(even)))
    def _():
        down_z.wait_recv()

    gather(second_face, second_face - 2, True)

    @pl.when(has_high)
    def _():
        up_z.wait_send()

    @pl.when(has_low)
    def _():
        down_z.wait_send()

    up_b.wait()
    down_b.wait()
    sums = bsend_ref[1] + brecv_ref[0] + brecv_ref[1]
    grad_ref[...] = sums[0, :owned]


def finish(acc_ref, sums_ref, out_ref, grad_ref, sem):
    tiles = acc_ref.shape[0]
    copies = [pltpu.make_async_copy(sums_ref, grad_ref, sem.at[tiles])]
    for t in range(tiles):
        place = out_ref.at[:, :, pl.ds(128 * t, 128)]
        copies.append(pltpu.make_async_copy(acc_ref.at[t], place, sem.at[t]))
    for copy in copies:
        copy.start()
    for copy in copies:
        copy.wait()


def on_device(
    sectors,
    slabs,
    adjoint,
    velocity,
    drag,
    block_weight,
    flux_jac,
    face_own,
    face_nbr,
    nbr_local,
    sector_slots,
    axial_slots,
    sector_live,
    elem_block,
):
    elems = adjoint.shape[2]
    tiles = elems // 128
    slots = sector_slots.shape[1]
    owned = BLOCKS // (sectors * slabs)
    width = -(-owned // 128) * 128
    operands = (
        adjoint,
        velocity,
        drag.reshape(1, elems),
        block_weight.reshape(1, elems),
        jnp.transpose(flux_jac, (1, 0, 2)),
        jnp.transpose(face_own, (1, 0, 2)),
        jnp.transpose(face_nbr, (1, 0, 2)),
        nbr_local,
        sector_slots,
        axial_slots,
        sector_live.reshape(1, 2),
        elem_block.reshape(1, elems),
        *constant_tables(),
    )
    vmem = pl.BlockSpec(memory_space=pltpu.VMEM)
    hbm = pl.BlockSpec(memory_space=pltpu.HBM)
    handed = pl.pallas_call(
        functools.partial(exchange, sectors, slabs, owned),
        out_shape=(
            pltpu.VMEM((tiles, 5, 64, 128), F32),
            pltpu.VMEM((owned,), F32),
        ),
        in_specs=[hbm] * INPUTS,
        out_specs=(vmem,) * 2,
        scratch_shapes=[pltpu.VMEM((tiles, 5, 64, 128), F32)]
        + [pltpu.VMEM(a.shape, a.dtype) for a in operands[1:]]
        + [
            pltpu.VMEM((640, elems), BF),
            pltpu.VMEM((6, 160, elems), BF),
            pltpu.VMEM((4, elems, slots), BF),
            pltpu.VMEM((4, slots, elems), BF),
            pltpu.VMEM((4, 80, slots), F32),
            pltpu.VMEM((4, 80, slots), F32),
            pltpu.VMEM((320, 1024), BF),
            pltpu.VMEM((25, 6, 128), F32),
            pltpu.VMEM((3, 8, width), F32),
            pltpu.VMEM((2, 8, width), F32),
            pltpu.SemaphoreType.DMA((6,)),
            pltpu.SemaphoreType.DMA((6,)),
            pltpu.SemaphoreType.REGULAR,
            pltpu.SemaphoreType.DMA((INPUTS,)),
            pltpu.SemaphoreType.DMA((5 * tiles,)),
        ],
        compiler_params=pltpu.CompilerParams(
            collective_id=0, has_side_effects=True, vmem_limit_bytes=60 * 1024 * 1024
        ),
    )(*operands)
    return pl.pallas_call(
        finish,
        out_shape=(
            jax.ShapeDtypeStruct(adjoint.shape, F32),
            jax.ShapeDtypeStruct((owned,), F32),
        ),
        in_specs=[vmem] * 2,
        out_specs=(hbm, hbm),
        scratch_shapes=[
            pltpu.SemaphoreType.DMA((tiles + 1,)),
        ],
        compiler_params=pltpu.CompilerParams(vmem_limit_bytes=40 * 1024 * 1024),
    )(*handed)


def solution(mesh):
    placed = (
        P(None, None, ("sector", "axial")),
        P(None, None, ("sector", "axial")),
        P(("sector", "axial")),
        P(("sector", "axial")),
        P(),
        P(),
        P(),
        P(None, ("sector", "axial")),
        P(None, ("sector", "axial")),
        P(None, ("sector", "axial")),
        P("sector", "axial", None),
        P(("sector", "axial")),
    )
    return jax.shard_map(
        functools.partial(on_device, mesh.shape["sector"], mesh.shape["axial"]),
        mesh=mesh,
        in_specs=placed,
        out_specs=(P(None, None, ("sector", "axial")), P(("sector", "axial"))),
        check_vma=False,
    )
```

```python
import functools

import jax
import jax.numpy as jnp
import numpy as np
from jax import lax
from jax.experimental import pallas as pl
from jax.experimental.pallas import tpu as pltpu
from jax.sharding import PartitionSpec as P

BLOCKS = 4096
BF = jnp.bfloat16
F32 = jnp.float32
MESH = pl.DeviceIdType.MESH
INPUTS = 14
SIDES = (0, 1, 4, 5)


def lobatto_tables():
    points = np.array([-1.0, -1.0 / np.sqrt(5.0), 1.0 / np.sqrt(5.0), 1.0])
    weights = np.array([1.0, 5.0, 5.0, 1.0]) / 6.0
    scales = np.array(
        [np.prod([points[i] - points[k] for k in range(4) if k != i]) for i in range(4)]
    )
    derivative = np.zeros((4, 4))
    for i in range(4):
        for p in range(4):
            if i != p:
                derivative[i, p] = scales[i] / scales[p] / (points[i] - points[p])
            else:
                derivative[i, p] = sum((1.0 / (points[i] - points[k]) for k in range(4) if k != i))
    node_weight = (
        weights[:, None, None] * weights[None, :, None] * weights[None, None, :]
    ).reshape(64) / 8.0
    return (derivative, node_weight)


def constant_tables():
    derivative, node_weight = lobatto_tables()
    eye = np.eye(4)
    step = derivative.T
    mats = [
        np.kron(np.kron(step, eye), eye),
        np.kron(np.kron(eye, step), eye),
        np.kron(np.kron(eye, eye), step),
    ]
    nodes = np.arange(64).reshape(4, 4, 4)
    faces = [nodes[0], nodes[3], nodes[:, 0], nodes[:, 3], nodes[:, :, 0], nodes[:, :, 3]]
    for ids in faces:
        diag = np.zeros((64, 64))
        diag[ids.reshape(16), ids.reshape(16)] = 1.0
        mats.append(diag)
    mats = [0.1 * np.concatenate([m, m], axis=1) for m in mats]
    weights = np.repeat(node_weight[:, None], 128, axis=1)
    return jnp.asarray(np.stack(mats), F32), jnp.asarray(weights, F32)


def split2(x):
    hi = x.astype(BF)
    return hi, (x - hi.astype(F32)).astype(BF)


def dot(a, b):
    return jnp.dot(a, b, preferred_element_type=F32)


def dot_nt(a, b):
    return lax.dot_general(a, b, (((1,), (1,)), ((), ())), preferred_element_type=F32)


def one_hot(mask):
    return jnp.where(mask, jnp.ones((), BF), jnp.zeros((), BF))


def add_face(ref, tile, face, part):
    low = lax.broadcasted_iota(jnp.int32, (8, 128), 0) < 4
    for c in range(5):
        rows = part[c]
        if face < 2:
            ids = pl.ds(48 * face, 16)
            ref[tile, c, ids, :] = ref[tile, c, ids, :] + rows
        elif face >= 4:
            ids = pl.ds(3 * (face - 4), 16, stride=4)
            ref[tile, c, ids, :] = ref[tile, c, ids, :] + rows
        else:
            for v in range(2):
                both = rows[8 * v : 8 * v + 8]
                turned = pltpu.roll(both, 4, 0)
                for k in range(2):
                    ids = pl.ds(32 * v + 16 * k + 8 * (face - 2), 8)
                    value = both if k == face - 2 else turned
                    mask = low if face == 2 else jnp.logical_not(low)
                    ref[tile, c, ids, :] = ref[tile, c, ids, :] + jnp.where(mask, value, 0.0)


def mixed(coef_ref, face, c, parts):
    total = coef_ref[5 * c, face : face + 1, :] * parts[0]
    for h in range(1, 5):
        total += coef_ref[5 * c + h, face : face + 1, :] * parts[h]
    return total


def face_rows(ref, tile, c, face):
    if face < 2:
        return ref[tile, c, 48 * face : 48 * face + 16, :]
    if face >= 4:
        return ref[tile, c, pl.ds(3 * (face - 4), 16, stride=4), :]
    low = lax.broadcasted_iota(jnp.int32, (8, 128), 0) < 4
    out = []
    for v in range(2):
        first = ref[tile, c, 32 * v + 8 * (face - 2) : 32 * v + 8 * (face - 2) + 8, :]
        second = ref[tile, c, 32 * v + 16 + 8 * (face - 2) : 32 * v + 24 + 8 * (face - 2), :]
        if face == 2:
            out.append(jnp.where(low, first, pltpu.roll(second, 4, 0)))
        else:
            out.append(jnp.where(low, pltpu.roll(first, 4, 0), second))
    return jnp.concatenate(out, axis=0)


def exchange(sectors, slabs, owned, *refs):
    hbm_refs = refs[:INPUTS]
    acc_ref, grad_ref = refs[INPUTS : INPUTS + 2]
    x_ref = refs[INPUTS + 2]
    vmem_refs = (None,) + refs[INPUTS + 3 : 2 * INPUTS + 2]
    (
        _,
        vel_ref,
        drag_ref,
        bw_ref,
        jac_ref,
        own_ref,
        nbrmat_ref,
        nbr_ref,
        sslots_ref,
        aslots_ref,
        live_ref,
        eb_ref,
        mats_ref,
        weight_ref,
    ) = vmem_refs
    (
        xs_ref,
        tr_ref,
        oh_ref,
        place_ref,
        send_ref,
        recv_ref,
        a_ref,
        coef_ref,
        bsend_ref,
        brecv_ref,
        send_sem,
        recv_sem,
        far_sem,
        load_sem,
        x_sem,
    ) = refs[2 * INPUTS + 2 :]
    tiles = x_ref.shape[0]
    elems = tiles * 128
    slots = sslots_ref.shape[1]
    width = bsend_ref.shape[2]
    count = sectors * slabs

    loads = {
        k: pltpu.make_async_copy(hbm_refs[k], vmem_refs[k], load_sem.at[k])
        for k in range(1, INPUTS)
    }
    fields = {
        (t, h): pltpu.make_async_copy(
            hbm_refs[0].at[h, :, pl.ds(128 * t, 128)], x_ref.at[t, h], x_sem.at[5 * t + h]
        )
        for h in (1, 2, 3, 0, 4)
        for t in range(tiles)
    }
    for k in (9, 8, 10, 6):
        loads[k].start()
    for key in fields:
        fields[key].start()
    for k in (1, 13, 2, 3, 11, 7, 12, 4, 5):
        loads[k].start()

    sec = lax.axis_index("sector")
    axi = lax.axis_index("axial")
    joint = sec * slabs + axi
    prev = lax.rem(joint + count - 1, count)
    nxt = lax.rem(joint + 1, count)
    dev_prev = (prev // slabs, lax.rem(prev, slabs))
    dev_next = (nxt // slabs, lax.rem(nxt, slabs))
    dev_low = (lax.rem(sec + sectors - 1, sectors), axi)
    dev_high = (lax.rem(sec + 1, sectors), axi)

    has_low = axi > 0
    has_high = axi < slabs - 1

    barrier = pltpu.get_barrier_semaphore()

    def greet(device):
        pl.semaphore_signal(barrier, inc=1, device_id=device, device_id_type=MESH)

    greet(dev_low)
    greet(dev_high)
    greet(dev_prev)

    @pl.when(has_high)
    def _():
        greet(dev_next)

    def remote(src, dst, k, device):
        return pltpu.make_async_remote_copy(
            src_ref=src,
            dst_ref=dst,
            send_sem=send_sem.at[k],
            recv_sem=recv_sem.at[k],
            device_id=device,
            device_id_type=MESH,
        )

    up_x = remote(send_ref.at[1], recv_ref.at[0], 0, dev_high)
    down_x = remote(send_ref.at[0], recv_ref.at[1], 1, dev_low)
    up_z = remote(send_ref.at[3], recv_ref.at[2], 2, dev_next)
    down_z = remote(send_ref.at[2], recv_ref.at[3], 3, dev_prev)
    up_b = remote(bsend_ref.at[2], brecv_ref.at[0], 4, dev_next)
    down_b = remote(bsend_ref.at[0], brecv_ref.at[1], 5, dev_prev)

    @pl.when(jnp.logical_not(has_high))
    def _():
        pl.semaphore_wait(barrier, 4)
        pl.semaphore_signal(far_sem, inc=1, device_id=dev_next, device_id_type=MESH)

    slot_ids = lax.broadcasted_iota(jnp.int32, (1, slots), 1)
    rows_slots = lax.broadcasted_iota(jnp.int32, (elems, slots), 0).astype(jnp.int16)

    columns = lax.broadcasted_iota(jnp.int32, (slots, elems), 1).astype(jnp.int16)

    def slot_row(i):
        if i >= 2:
            return aslots_ref[i - 2 : i - 1, :]
        return jnp.where(slot_ids < live_ref[:, i : i + 1], sslots_ref[i : i + 1, :], -1)

    def find_slots(i):
        ids = jnp.broadcast_to(slot_row(i), (elems, slots)).astype(jnp.int16)
        oh_ref[i] = one_hot(rows_slots == ids)

    def find_places(i):
        ids = jnp.broadcast_to(slot_row(i), (128, slots)).T
        ids = jnp.concatenate([ids] * tiles, axis=1).astype(jnp.int16)
        place_ref[i] = one_hot(columns == ids)

    def take_trace(t, face):
        lanes = slice(128 * t, 128 * t + 128)
        for c in range(5):
            hi, lo = split2(face_rows(x_ref, t, c, face))
            tr_ref[face, 16 * c : 16 * c + 16, lanes] = hi
            tr_ref[face, 80 + 16 * c : 96 + 16 * c, lanes] = lo

    def fill_send(i):
        face = SIDES[i]
        for t in range(tiles):
            take_trace(t, face)
        both = dot(tr_ref[face], oh_ref[i])
        both = both[:80] + both[80:]
        if i < 2:
            send_ref[i] = both
            return
        for n in range(0, slots, 128):
            parts = [both[16 * h : 16 * h + 16, n : n + 128] for h in range(5)]
            for c in range(5):
                value = mixed(coef_ref, 9 - face, c, parts)
                send_ref[i, 16 * c : 16 * c + 16, n : n + 128] = value

    for k in (9, 8, 10):
        loads[k].wait()
    for i in range(4):
        find_slots(i)
    loads[6].wait()
    for c in range(5):
        for h in range(5):
            coef_ref[5 * c + h] = jnp.broadcast_to(0.1 * nbrmat_ref[c][:, h : h + 1], (6, 128))
    for key in fields:
        fields[key].wait()
    def sum_blocks():
        for k in (1, 13, 2, 3, 11):
            loads[k].wait()
        parts = []
        for t in range(tiles):
            lanes = slice(128 * t, 128 * t + 128)
            total = x_ref[t, 1] * vel_ref[0, :, lanes].astype(F32)
            total += x_ref[t, 2] * vel_ref[1, :, lanes].astype(F32)
            total += x_ref[t, 3] * vel_ref[2, :, lanes].astype(F32)
            parts.append(jnp.sum(total * weight_ref[...], axis=0, keepdims=True))
        elem_grad = drag_ref[...] * jnp.concatenate(parts, axis=1)
        weighted = bw_ref[...] * elem_grad
        w1 = weighted.astype(BF)
        rest = weighted - w1.astype(F32)
        w2 = rest.astype(BF)
        w3 = (rest - w2.astype(F32)).astype(BF).astype(F32)
        row16 = lax.broadcasted_iota(jnp.int32, (16, elems), 0)
        stack = jnp.where(row16 == 0, w1.astype(F32), 0.0)
        stack = jnp.where(row16 == 1, w2.astype(F32), stack)
        stack = jnp.where(row16 == 2, w3, stack).astype(BF)
        rel = eb_ref[...] - (joint - 1) * owned
        rel = jnp.where(rel < 0, rel + BLOCKS, rel)
        rel = jnp.where(rel >= BLOCKS, rel - BLOCKS, rel)
        rows_blk = lax.broadcasted_iota(jnp.int32, (width, elems), 0).astype(jnp.int16)
        for j in range(3):
            ids = jnp.broadcast_to(rel - j * owned, (width, elems)).astype(jnp.int16)
            sums = dot_nt(stack, one_hot(rows_blk == ids))
            total = jnp.sum(sums, axis=0, keepdims=True)
            bsend_ref[j] = jnp.broadcast_to(total, (8, width))

    @pl.when(jnp.logical_not(has_high))
    def _():
        sum_blocks()
        up_b.start()
        down_b.start()

    fill_send(2)
    fill_send(3)

    @pl.when(jnp.logical_and(has_low, has_high))
    def _():
        pl.semaphore_wait(barrier, 4)

    @pl.when(jnp.logical_not(has_low))
    def _():
        pl.semaphore_wait(barrier, 3)

    @pl.when(has_high)
    def _():
        up_z.start()

    @pl.when(has_low)
    def _():
        down_z.start()

    @pl.when(jnp.logical_not(has_low))
    def _():
        recv_ref[2] = jnp.zeros((80, slots), F32)

    @pl.when(jnp.logical_not(has_high))
    def _():
        recv_ref[3] = jnp.zeros((80, slots), F32)

    fill_send(0)
    fill_send(1)
    up_x.start()
    down_x.start()

    @pl.when(has_high)
    def _():
        sum_blocks()
        up_b.start()

    @pl.when(jnp.logical_and(has_low, has_high))
    def _():
        down_b.start()

    for k in (7, 12, 4, 5):
        loads[k].wait()
    for i in range(4):
        find_places(i)

    spread = jnp.minimum(lax.broadcasted_iota(jnp.int32, (5, 384), 1) // 64, 4)
    spread = jnp.where(spread == lax.broadcasted_iota(jnp.int32, (5, 384), 0), 1.0, 0.0)
    for c in range(5):
        rows = slice(64 * c, 64 * c + 64)
        jac = jac_ref[0][:, c : c + 1] * spread[0:1, :]
        face = own_ref[c][:, 0:1] * spread[0:1, :]
        for h in range(1, 5):
            jac += jac_ref[h][:, c : c + 1] * spread[h : h + 1, :]
            face += own_ref[c][:, h : h + 1] * spread[h : h + 1, :]
        for t in range(3):
            lanes = slice(128 * t, 128 * t + 128)
            total = mats_ref[0] * jac[0:1, lanes]
            for j in range(1, 9):
                row = jac[j : j + 1, lanes] if j < 3 else face[j - 3 : j - 2, lanes]
                total += mats_ref[j] * row
            hi, lo = split2(total)
            places = ((768, hi), (896, lo)) if t == 2 else ((0, hi), (256, hi), (512, lo))
            for base, part in places:
                base += 128 * t if t < 2 else 0
                a_ref[rows, base : base + 128] = part

    for t in range(tiles):
        lanes = slice(128 * t, 128 * t + 128)
        for h in range(5):
            hi, lo = split2(x_ref[t, h])
            for base, part in ((0, hi), (256, lo)) if h < 4 else ((256, hi), (320, lo)):
                xs_ref[64 * h + base : 64 * h + base + 64, lanes] = part
        for face in (2, 3):
            take_trace(t, face)

    xs = [xs_ref[rows, :] for rows in (slice(0, 512), slice(0, 256), slice(512, 640), slice(512, 576))]
    own = dot(a_ref[:, 0:960], jnp.concatenate(xs, axis=0))
    keep = 1.0 - 0.1 * drag_ref[...]
    for t in range(tiles):
        lanes = slice(128 * t, 128 * t + 128)
        for c in range(5):
            x = x_ref[t, c]
            scaled = x * keep[:, lanes] if 1 <= c <= 3 else x
            acc_ref[t, c] = scaled + own[64 * c : 64 * c + 64, lanes]

    rows_src = lax.broadcasted_iota(jnp.int32, (elems, elems), 0).astype(jnp.int16)
    def gather(f, i=None):
        g = f + 1 - 2 * (f % 2)
        ids = jnp.broadcast_to(nbr_ref[f : f + 1, :], (elems, elems)).astype(jnp.int16)
        sources, places = tr_ref[g], one_hot(rows_src == ids)
        if i is not None:
            got = jnp.concatenate(split2(recv_ref[i]), axis=0)
            sources = jnp.concatenate([sources, got], axis=1)
            places = jnp.concatenate([places, place_ref[i]], axis=0)
        both = dot(sources, places)
        both = both[:80] + both[80:]
        for t in range(tiles):
            parts = [both[16 * h : 16 * h + 16, 128 * t : 128 * t + 128] for h in range(5)]
            add_face(acc_ref, t, f, [mixed(coef_ref, f, c, parts) for c in range(5)])

    for f in (2, 3, 4, 5):
        gather(f)
    up_x.wait()
    down_x.wait()
    gather(0, 0)
    gather(1, 1)

    @pl.when(jnp.logical_not(has_low))
    def _():
        pl.semaphore_wait(far_sem, 1)
        down_b.start()

    @pl.when(has_high)
    def _():
        up_z.wait_send()
        down_z.wait_recv()

    @pl.when(has_low)
    def _():
        down_z.wait_send()
        up_z.wait_recv()

    for i in (2, 3):
        both = dot(jnp.concatenate(split2(recv_ref[i]), axis=0), place_ref[i])
        both = both[:80] + both[80:]
        for t in range(tiles):
            lanes = slice(128 * t, 128 * t + 128)
            rows = [both[16 * c : 16 * c + 16, lanes] for c in range(5)]
            add_face(acc_ref, t, SIDES[i], rows)

    up_b.wait()
    down_b.wait()
    sums = bsend_ref[1] + brecv_ref[0] + brecv_ref[1]
    grad_ref[...] = sums[0, :owned]


def finish(acc_ref, sums_ref, out_ref, grad_ref, sem):
    tiles = acc_ref.shape[0]
    copies = [pltpu.make_async_copy(sums_ref, grad_ref, sem.at[tiles])]
    for t in range(tiles):
        place = out_ref.at[:, :, pl.ds(128 * t, 128)]
        copies.append(pltpu.make_async_copy(acc_ref.at[t], place, sem.at[t]))
    for copy in copies:
        copy.start()
    for copy in copies:
        copy.wait()


def on_device(
    sectors,
    slabs,
    adjoint,
    velocity,
    drag,
    block_weight,
    flux_jac,
    face_own,
    face_nbr,
    nbr_local,
    sector_slots,
    axial_slots,
    sector_live,
    elem_block,
):
    elems = adjoint.shape[2]
    tiles = elems // 128
    slots = sector_slots.shape[1]
    owned = BLOCKS // (sectors * slabs)
    width = -(-owned // 128) * 128
    operands = (
        adjoint,
        velocity,
        drag.reshape(1, elems),
        block_weight.reshape(1, elems),
        jnp.transpose(flux_jac, (1, 0, 2)),
        jnp.transpose(face_own, (1, 0, 2)),
        jnp.transpose(face_nbr, (1, 0, 2)),
        nbr_local,
        sector_slots,
        axial_slots,
        sector_live.reshape(1, 2),
        elem_block.reshape(1, elems),
        *constant_tables(),
    )
    vmem = pl.BlockSpec(memory_space=pltpu.VMEM)
    hbm = pl.BlockSpec(memory_space=pltpu.HBM)
    handed = pl.pallas_call(
        functools.partial(exchange, sectors, slabs, owned),
        out_shape=(
            pltpu.VMEM((tiles, 5, 64, 128), F32),
            pltpu.VMEM((owned,), F32),
        ),
        in_specs=[hbm] * INPUTS,
        out_specs=(vmem,) * 2,
        scratch_shapes=[pltpu.VMEM((tiles, 5, 64, 128), F32)]
        + [pltpu.VMEM(a.shape, a.dtype) for a in operands[1:]]
        + [
            pltpu.VMEM((640, elems), BF),
            pltpu.VMEM((6, 160, elems), BF),
            pltpu.VMEM((4, elems, slots), BF),
            pltpu.VMEM((4, slots, elems), BF),
            pltpu.VMEM((4, 80, slots), F32),
            pltpu.VMEM((4, 80, slots), F32),
            pltpu.VMEM((320, 1024), BF),
            pltpu.VMEM((25, 6, 128), F32),
            pltpu.VMEM((3, 8, width), F32),
            pltpu.VMEM((2, 8, width), F32),
            pltpu.SemaphoreType.DMA((6,)),
            pltpu.SemaphoreType.DMA((6,)),
            pltpu.SemaphoreType.REGULAR,
            pltpu.SemaphoreType.DMA((INPUTS,)),
            pltpu.SemaphoreType.DMA((5 * tiles,)),
        ],
        compiler_params=pltpu.CompilerParams(
            collective_id=0, has_side_effects=True, vmem_limit_bytes=60 * 1024 * 1024
        ),
    )(*operands)
    return pl.pallas_call(
        finish,
        out_shape=(
            jax.ShapeDtypeStruct(adjoint.shape, F32),
            jax.ShapeDtypeStruct((owned,), F32),
        ),
        in_specs=[vmem] * 2,
        out_specs=(hbm, hbm),
        scratch_shapes=[
            pltpu.SemaphoreType.DMA((tiles + 1,)),
        ],
        compiler_params=pltpu.CompilerParams(vmem_limit_bytes=40 * 1024 * 1024),
    )(*handed)


def solution(mesh):
    placed = (
        P(None, None, ("sector", "axial")),
        P(None, None, ("sector", "axial")),
        P(("sector", "axial")),
        P(("sector", "axial")),
        P(),
        P(),
        P(),
        P(None, ("sector", "axial")),
        P(None, ("sector", "axial")),
        P(None, ("sector", "axial")),
        P("sector", "axial", None),
        P(("sector", "axial")),
    )
    return jax.shard_map(
        functools.partial(on_device, mesh.shape["sector"], mesh.shape["axial"]),
        mesh=mesh,
        in_specs=placed,
        out_specs=(P(None, None, ("sector", "axial")), P(("sector", "axial"))),
        check_vma=False,
    )
```

```python
import functools

import jax
import jax.numpy as jnp
import numpy as np
from jax import lax
from jax.experimental import pallas as pl
from jax.experimental.pallas import tpu as pltpu
from jax.sharding import PartitionSpec as P

BLOCKS = 4096
BF = jnp.bfloat16
F32 = jnp.float32
MESH = pl.DeviceIdType.MESH
INPUTS = 14
SIDES = (0, 1, 4, 5)


def lobatto_tables():
    points = np.array([-1.0, -1.0 / np.sqrt(5.0), 1.0 / np.sqrt(5.0), 1.0])
    weights = np.array([1.0, 5.0, 5.0, 1.0]) / 6.0
    scales = np.array(
        [np.prod([points[i] - points[k] for k in range(4) if k != i]) for i in range(4)]
    )
    derivative = np.zeros((4, 4))
    for i in range(4):
        for p in range(4):
            if i != p:
                derivative[i, p] = scales[i] / scales[p] / (points[i] - points[p])
            else:
                derivative[i, p] = sum((1.0 / (points[i] - points[k]) for k in range(4) if k != i))
    node_weight = (
        weights[:, None, None] * weights[None, :, None] * weights[None, None, :]
    ).reshape(64) / 8.0
    return (derivative, node_weight)


def constant_tables():
    derivative, node_weight = lobatto_tables()
    eye = np.eye(4)
    step = derivative.T
    mats = [
        np.kron(np.kron(step, eye), eye),
        np.kron(np.kron(eye, step), eye),
        np.kron(np.kron(eye, eye), step),
    ]
    nodes = np.arange(64).reshape(4, 4, 4)
    faces = [nodes[0], nodes[3], nodes[:, 0], nodes[:, 3], nodes[:, :, 0], nodes[:, :, 3]]
    for ids in faces:
        diag = np.zeros((64, 64))
        diag[ids.reshape(16), ids.reshape(16)] = 1.0
        mats.append(diag)
    mats = [0.1 * np.concatenate([m, m], axis=1) for m in mats]
    weights = np.repeat(node_weight[:, None], 128, axis=1)
    return jnp.asarray(np.stack(mats), F32), jnp.asarray(weights, F32)


def split2(x):
    hi = x.astype(BF)
    return hi, (x - hi.astype(F32)).astype(BF)


def dot(a, b):
    return jnp.dot(a, b, preferred_element_type=F32)


def dot_nt(a, b):
    return lax.dot_general(a, b, (((1,), (1,)), ((), ())), preferred_element_type=F32)


def one_hot(mask):
    return jnp.where(mask, jnp.ones((), BF), jnp.zeros((), BF))


def add_face(ref, tile, face, part):
    low = lax.broadcasted_iota(jnp.int32, (8, 128), 0) < 4
    for c in range(5):
        rows = part[c]
        if face < 2:
            ids = pl.ds(48 * face, 16)
            ref[tile, c, ids, :] = ref[tile, c, ids, :] + rows
        elif face >= 4:
            ids = pl.ds(3 * (face - 4), 16, stride=4)
            ref[tile, c, ids, :] = ref[tile, c, ids, :] + rows
        else:
            for v in range(2):
                both = rows[8 * v : 8 * v + 8]
                turned = pltpu.roll(both, 4, 0)
                for k in range(2):
                    ids = pl.ds(32 * v + 16 * k + 8 * (face - 2), 8)
                    value = both if k == face - 2 else turned
                    mask = low if face == 2 else jnp.logical_not(low)
                    ref[tile, c, ids, :] = ref[tile, c, ids, :] + jnp.where(mask, value, 0.0)


def mixed(coef_ref, face, c, parts):
    total = coef_ref[5 * c, face : face + 1, :] * parts[0]
    for h in range(1, 5):
        total += coef_ref[5 * c + h, face : face + 1, :] * parts[h]
    return total


def face_rows(ref, tile, c, face):
    if face < 2:
        return ref[tile, c, 48 * face : 48 * face + 16, :]
    if face >= 4:
        return ref[tile, c, pl.ds(3 * (face - 4), 16, stride=4), :]
    low = lax.broadcasted_iota(jnp.int32, (8, 128), 0) < 4
    out = []
    for v in range(2):
        first = ref[tile, c, 32 * v + 8 * (face - 2) : 32 * v + 8 * (face - 2) + 8, :]
        second = ref[tile, c, 32 * v + 16 + 8 * (face - 2) : 32 * v + 24 + 8 * (face - 2), :]
        if face == 2:
            out.append(jnp.where(low, first, pltpu.roll(second, 4, 0)))
        else:
            out.append(jnp.where(low, pltpu.roll(first, 4, 0), second))
    return jnp.concatenate(out, axis=0)


def exchange(sectors, slabs, owned, *refs):
    hbm_refs = refs[:INPUTS]
    acc_ref, grad_ref = refs[INPUTS : INPUTS + 2]
    x_ref = refs[INPUTS + 2]
    vmem_refs = (None,) + refs[INPUTS + 3 : 2 * INPUTS + 2]
    (
        _,
        vel_ref,
        drag_ref,
        bw_ref,
        jac_ref,
        own_ref,
        nbrmat_ref,
        nbr_ref,
        sslots_ref,
        aslots_ref,
        live_ref,
        eb_ref,
        mats_ref,
        weight_ref,
    ) = vmem_refs
    (
        xs_ref,
        tr_ref,
        oh_ref,
        place_ref,
        send_ref,
        recv_ref,
        a_ref,
        coef_ref,
        bsend_ref,
        brecv_ref,
        send_sem,
        recv_sem,
        far_sem,
        load_sem,
        x_sem,
    ) = refs[2 * INPUTS + 2 :]
    tiles = x_ref.shape[0]
    elems = tiles * 128
    slots = sslots_ref.shape[1]
    width = bsend_ref.shape[2]
    count = sectors * slabs

    loads = {
        k: pltpu.make_async_copy(hbm_refs[k], vmem_refs[k], load_sem.at[k])
        for k in range(1, INPUTS)
    }
    fields = {
        (t, h): pltpu.make_async_copy(
            hbm_refs[0].at[h, :, pl.ds(128 * t, 128)], x_ref.at[t, h], x_sem.at[5 * t + h]
        )
        for h in (1, 2, 3, 0, 4)
        for t in range(tiles)
    }
    sec = lax.axis_index("sector")
    axi = lax.axis_index("axial")
    joint = sec * slabs + axi
    prev = lax.rem(joint + count - 1, count)
    nxt = lax.rem(joint + 1, count)
    dev_prev = (prev // slabs, lax.rem(prev, slabs))
    dev_next = (nxt // slabs, lax.rem(nxt, slabs))
    dev_low = (lax.rem(sec + sectors - 1, sectors), axi)
    dev_high = (lax.rem(sec + 1, sectors), axi)

    has_low = axi > 0
    has_high = axi < slabs - 1

    def start_block_loads():
        for k in (1, 13, 2, 3, 11):
            loads[k].start()

    @pl.when(jnp.logical_not(has_high))
    def _():
        start_block_loads()

    for k in (9, 8, 10, 6):
        loads[k].start()
    for key in fields:
        fields[key].start()

    @pl.when(has_high)
    def _():
        start_block_loads()

    for k in (7, 12, 4, 5):
        loads[k].start()

    barrier = pltpu.get_barrier_semaphore()

    def greet(device):
        pl.semaphore_signal(barrier, inc=1, device_id=device, device_id_type=MESH)

    greet(dev_low)
    greet(dev_high)
    greet(dev_prev)

    @pl.when(has_high)
    def _():
        greet(dev_next)

    def remote(src, dst, k, device):
        return pltpu.make_async_remote_copy(
            src_ref=src,
            dst_ref=dst,
            send_sem=send_sem.at[k],
            recv_sem=recv_sem.at[k],
            device_id=device,
            device_id_type=MESH,
        )

    up_x = remote(send_ref.at[1], recv_ref.at[0], 0, dev_high)
    down_x = remote(send_ref.at[0], recv_ref.at[1], 1, dev_low)
    up_z = remote(send_ref.at[3], recv_ref.at[2], 2, dev_next)
    down_z = remote(send_ref.at[2], recv_ref.at[3], 3, dev_prev)
    up_b = remote(bsend_ref.at[2], brecv_ref.at[0], 4, dev_next)
    down_b = remote(bsend_ref.at[0], brecv_ref.at[1], 5, dev_prev)

    def sum_blocks():
        for k in (1, 13, 2, 3, 11):
            loads[k].wait()
        parts = []
        for t in range(tiles):
            lanes = slice(128 * t, 128 * t + 128)
            total = x_ref[t, 1] * vel_ref[0, :, lanes].astype(F32)
            total += x_ref[t, 2] * vel_ref[1, :, lanes].astype(F32)
            total += x_ref[t, 3] * vel_ref[2, :, lanes].astype(F32)
            parts.append(jnp.sum(total * weight_ref[...], axis=0, keepdims=True))
        elem_grad = drag_ref[...] * jnp.concatenate(parts, axis=1)
        weighted = bw_ref[...] * elem_grad
        w1 = weighted.astype(BF)
        rest = weighted - w1.astype(F32)
        w2 = rest.astype(BF)
        w3 = (rest - w2.astype(F32)).astype(BF).astype(F32)
        row16 = lax.broadcasted_iota(jnp.int32, (16, elems), 0)
        stack = jnp.where(row16 == 0, w1.astype(F32), 0.0)
        stack = jnp.where(row16 == 1, w2.astype(F32), stack)
        stack = jnp.where(row16 == 2, w3, stack).astype(BF)
        rel = eb_ref[...] - (joint - 1) * owned
        rel = jnp.where(rel < 0, rel + BLOCKS, rel)
        rel = jnp.where(rel >= BLOCKS, rel - BLOCKS, rel)
        for j in (1, 0):
            rel = jnp.where(rel >= owned * (j + 1), rel + (width - owned), rel)
        rows_blk = lax.broadcasted_iota(jnp.int32, (3 * width, elems), 0).astype(jnp.int16)
        ids = jnp.broadcast_to(rel, (3 * width, elems)).astype(jnp.int16)
        sums = dot_nt(stack, one_hot(rows_blk == ids))
        total = jnp.sum(sums, axis=0, keepdims=True)
        for j in range(3):
            part = total[:, j * width : (j + 1) * width]
            bsend_ref[j] = jnp.broadcast_to(part, (8, width))

    @pl.when(jnp.logical_not(has_high))
    def _():
        pl.semaphore_wait(barrier, 4)
        pl.semaphore_signal(far_sem, inc=1, device_id=dev_next, device_id_type=MESH)
        for h in (1, 2, 3):
            for t in range(tiles):
                fields[t, h].wait()
        sum_blocks()
        up_b.start()
        down_b.start()

    slot_ids = lax.broadcasted_iota(jnp.int32, (1, slots), 1)
    rows_slots = lax.broadcasted_iota(jnp.int32, (elems, slots), 0).astype(jnp.int16)

    columns = lax.broadcasted_iota(jnp.int32, (slots, elems), 1).astype(jnp.int16)

    def slot_row(i):
        if i >= 2:
            return aslots_ref[i - 2 : i - 1, :]
        return jnp.where(slot_ids < live_ref[:, i : i + 1], sslots_ref[i : i + 1, :], -1)

    def find_slots(i):
        ids = jnp.broadcast_to(slot_row(i), (elems, slots)).astype(jnp.int16)
        oh_ref[i] = one_hot(rows_slots == ids)

    def find_places(i):
        ids = jnp.broadcast_to(slot_row(i), (128, slots)).T
        ids = jnp.concatenate([ids] * tiles, axis=1).astype(jnp.int16)
        place_ref[i] = one_hot(columns == ids)

    def take_trace(t, face):
        lanes = slice(128 * t, 128 * t + 128)
        for c in range(5):
            hi, lo = split2(face_rows(x_ref, t, c, face))
            tr_ref[face, 16 * c : 16 * c + 16, lanes] = hi
            tr_ref[face, 80 + 16 * c : 96 + 16 * c, lanes] = lo

    def fill_send(i):
        face = SIDES[i]
        for t in range(tiles):
            take_trace(t, face)
        both = dot(tr_ref[face], oh_ref[i])
        both = both[:80] + both[80:]
        if i < 2:
            send_ref[i] = both
            return
        for n in range(0, slots, 128):
            parts = [both[16 * h : 16 * h + 16, n : n + 128] for h in range(5)]
            for c in range(5):
                value = mixed(coef_ref, 9 - face, c, parts)
                send_ref[i, 16 * c : 16 * c + 16, n : n + 128] = value

    for k in (9, 8, 10):
        loads[k].wait()
    for i in range(4):
        find_slots(i)
    loads[6].wait()
    for c in range(5):
        for h in range(5):
            coef_ref[5 * c + h] = jnp.broadcast_to(0.1 * nbrmat_ref[c][:, h : h + 1], (6, 128))
    @pl.when(has_high)
    def _():
        for h in (1, 2, 3):
            for t in range(tiles):
                fields[t, h].wait()

    for h in (0, 4):
        for t in range(tiles):
            fields[t, h].wait()
    fill_send(2)
    fill_send(3)

    @pl.when(jnp.logical_and(has_low, has_high))
    def _():
        pl.semaphore_wait(barrier, 4)

    @pl.when(jnp.logical_not(has_low))
    def _():
        pl.semaphore_wait(barrier, 3)

    @pl.when(has_high)
    def _():
        up_z.start()

    @pl.when(has_low)
    def _():
        down_z.start()

    @pl.when(jnp.logical_not(has_low))
    def _():
        recv_ref[2] = jnp.zeros((80, slots), F32)

    @pl.when(jnp.logical_not(has_high))
    def _():
        recv_ref[3] = jnp.zeros((80, slots), F32)

    fill_send(0)
    fill_send(1)
    up_x.start()
    down_x.start()

    @pl.when(has_high)
    def _():
        sum_blocks()
        up_b.start()

    @pl.when(jnp.logical_and(has_low, has_high))
    def _():
        down_b.start()

    for k in (7, 12, 4, 5):
        loads[k].wait()
    for i in range(4):
        find_places(i)

    spread = jnp.minimum(lax.broadcasted_iota(jnp.int32, (5, 384), 1) // 64, 4)
    spread = jnp.where(spread == lax.broadcasted_iota(jnp.int32, (5, 384), 0), 1.0, 0.0)
    for c in range(5):
        rows = slice(64 * c, 64 * c + 64)
        jac = jac_ref[0][:, c : c + 1] * spread[0:1, :]
        face = own_ref[c][:, 0:1] * spread[0:1, :]
        for h in range(1, 5):
            jac += jac_ref[h][:, c : c + 1] * spread[h : h + 1, :]
            face += own_ref[c][:, h : h + 1] * spread[h : h + 1, :]
        for t in range(3):
            lanes = slice(128 * t, 128 * t + 128)
            total = mats_ref[0] * jac[0:1, lanes]
            for j in range(1, 9):
                row = jac[j : j + 1, lanes] if j < 3 else face[j - 3 : j - 2, lanes]
                total += mats_ref[j] * row
            hi, lo = split2(total)
            places = ((768, hi), (896, lo)) if t == 2 else ((0, hi), (256, hi), (512, lo))
            for base, part in places:
                base += 128 * t if t < 2 else 0
                a_ref[rows, base : base + 128] = part

    for t in range(tiles):
        lanes = slice(128 * t, 128 * t + 128)
        for h in range(5):
            hi, lo = split2(x_ref[t, h])
            for base, part in ((0, hi), (256, lo)) if h < 4 else ((256, hi), (320, lo)):
                xs_ref[64 * h + base : 64 * h + base + 64, lanes] = part
        for face in (2, 3):
            take_trace(t, face)

    xs = [xs_ref[rows, :] for rows in (slice(0, 512), slice(0, 256), slice(512, 640), slice(512, 576))]
    own = dot(a_ref[:, 0:960], jnp.concatenate(xs, axis=0))
    keep = 1.0 - 0.1 * drag_ref[...]
    for t in range(tiles):
        lanes = slice(128 * t, 128 * t + 128)
        for c in range(5):
            x = x_ref[t, c]
            scaled = x * keep[:, lanes] if 1 <= c <= 3 else x
            acc_ref[t, c] = scaled + own[64 * c : 64 * c + 64, lanes]

    rows_src = lax.broadcasted_iota(jnp.int32, (elems, elems), 0).astype(jnp.int16)
    def gather(f, i=None):
        g = f + 1 - 2 * (f % 2)
        ids = jnp.broadcast_to(nbr_ref[f : f + 1, :], (elems, elems)).astype(jnp.int16)
        sources, places = tr_ref[g], one_hot(rows_src == ids)
        if i is not None:
            got = jnp.concatenate(split2(recv_ref[i]), axis=0)
            sources = jnp.concatenate([sources, got], axis=1)
            places = jnp.concatenate([places, place_ref[i]], axis=0)
        both = dot(sources, places)
        both = both[:80] + both[80:]
        for t in range(tiles):
            parts = [both[16 * h : 16 * h + 16, 128 * t : 128 * t + 128] for h in range(5)]
            add_face(acc_ref, t, f, [mixed(coef_ref, f, c, parts) for c in range(5)])

    for f in (2, 3, 4, 5):
        gather(f)
    up_x.wait()
    down_x.wait()
    gather(0, 0)

    @pl.when(jnp.logical_not(has_low))
    def _():
        pl.semaphore_wait(far_sem, 1)
        down_b.start()

    gather(1, 1)

    @pl.when(has_high)
    def _():
        up_z.wait_send()
        down_z.wait_recv()

    @pl.when(has_low)
    def _():
        down_z.wait_send()
        up_z.wait_recv()

    for i in (2, 3):
        both = dot(jnp.concatenate(split2(recv_ref[i]), axis=0), place_ref[i])
        both = both[:80] + both[80:]
        for t in range(tiles):
            lanes = slice(128 * t, 128 * t + 128)
            rows = [both[16 * c : 16 * c + 16, lanes] for c in range(5)]
            add_face(acc_ref, t, SIDES[i], rows)

    up_b.wait()
    down_b.wait()
    sums = bsend_ref[1] + brecv_ref[0] + brecv_ref[1]
    grad_ref[...] = sums[0, :owned]


def finish(acc_ref, sums_ref, out_ref, grad_ref, sem):
    tiles = acc_ref.shape[0]
    copies = [pltpu.make_async_copy(sums_ref, grad_ref, sem.at[tiles])]
    for t in range(tiles):
        place = out_ref.at[:, :, pl.ds(128 * t, 128)]
        copies.append(pltpu.make_async_copy(acc_ref.at[t], place, sem.at[t]))
    for copy in copies:
        copy.start()
    for copy in copies:
        copy.wait()


def on_device(
    sectors,
    slabs,
    adjoint,
    velocity,
    drag,
    block_weight,
    flux_jac,
    face_own,
    face_nbr,
    nbr_local,
    sector_slots,
    axial_slots,
    sector_live,
    elem_block,
):
    elems = adjoint.shape[2]
    tiles = elems // 128
    slots = sector_slots.shape[1]
    owned = BLOCKS // (sectors * slabs)
    width = -(-owned // 128) * 128
    operands = (
        adjoint,
        velocity,
        drag.reshape(1, elems),
        block_weight.reshape(1, elems),
        jnp.transpose(flux_jac, (1, 0, 2)),
        jnp.transpose(face_own, (1, 0, 2)),
        jnp.transpose(face_nbr, (1, 0, 2)),
        nbr_local,
        sector_slots,
        axial_slots,
        sector_live.reshape(1, 2),
        elem_block.reshape(1, elems),
        *constant_tables(),
    )
    vmem = pl.BlockSpec(memory_space=pltpu.VMEM)
    hbm = pl.BlockSpec(memory_space=pltpu.HBM)
    handed = pl.pallas_call(
        functools.partial(exchange, sectors, slabs, owned),
        out_shape=(
            pltpu.VMEM((tiles, 5, 64, 128), F32),
            pltpu.VMEM((owned,), F32),
        ),
        in_specs=[hbm] * INPUTS,
        out_specs=(vmem,) * 2,
        scratch_shapes=[pltpu.VMEM((tiles, 5, 64, 128), F32)]
        + [pltpu.VMEM(a.shape, a.dtype) for a in operands[1:]]
        + [
            pltpu.VMEM((640, elems), BF),
            pltpu.VMEM((6, 160, elems), BF),
            pltpu.VMEM((4, elems, slots), BF),
            pltpu.VMEM((4, slots, elems), BF),
            pltpu.VMEM((4, 80, slots), F32),
            pltpu.VMEM((4, 80, slots), F32),
            pltpu.VMEM((320, 1024), BF),
            pltpu.VMEM((25, 6, 128), F32),
            pltpu.VMEM((3, 8, width), F32),
            pltpu.VMEM((2, 8, width), F32),
            pltpu.SemaphoreType.DMA((6,)),
            pltpu.SemaphoreType.DMA((6,)),
            pltpu.SemaphoreType.REGULAR,
            pltpu.SemaphoreType.DMA((INPUTS,)),
            pltpu.SemaphoreType.DMA((5 * tiles,)),
        ],
        compiler_params=pltpu.CompilerParams(
            collective_id=0, has_side_effects=True, vmem_limit_bytes=60 * 1024 * 1024
        ),
    )(*operands)
    return pl.pallas_call(
        finish,
        out_shape=(
            jax.ShapeDtypeStruct(adjoint.shape, F32),
            jax.ShapeDtypeStruct((owned,), F32),
        ),
        in_specs=[vmem] * 2,
        out_specs=(hbm, hbm),
        scratch_shapes=[
            pltpu.SemaphoreType.DMA((tiles + 1,)),
        ],
        compiler_params=pltpu.CompilerParams(vmem_limit_bytes=40 * 1024 * 1024),
    )(*handed)


def solution(mesh):
    placed = (
        P(None, None, ("sector", "axial")),
        P(None, None, ("sector", "axial")),
        P(("sector", "axial")),
        P(("sector", "axial")),
        P(),
        P(),
        P(),
        P(None, ("sector", "axial")),
        P(None, ("sector", "axial")),
        P(None, ("sector", "axial")),
        P("sector", "axial", None),
        P(("sector", "axial")),
    )
    return jax.shard_map(
        functools.partial(on_device, mesh.shape["sector"], mesh.shape["axial"]),
        mesh=mesh,
        in_specs=placed,
        out_specs=(P(None, None, ("sector", "axial")), P(("sector", "axial"))),
        check_vma=False,
    )
```

```python
import functools

import jax
import jax.numpy as jnp
import numpy as np
from jax import lax
from jax.experimental import pallas as pl
from jax.experimental.pallas import tpu as pltpu
from jax.sharding import PartitionSpec as P

BLOCKS = 4096
BF = jnp.bfloat16
F32 = jnp.float32
MESH = pl.DeviceIdType.MESH
INPUTS = 14
SIDES = (0, 1, 4, 5)


def lobatto_tables():
    points = np.array([-1.0, -1.0 / np.sqrt(5.0), 1.0 / np.sqrt(5.0), 1.0])
    weights = np.array([1.0, 5.0, 5.0, 1.0]) / 6.0
    scales = np.array(
        [np.prod([points[i] - points[k] for k in range(4) if k != i]) for i in range(4)]
    )
    derivative = np.zeros((4, 4))
    for i in range(4):
        for p in range(4):
            if i != p:
                derivative[i, p] = scales[i] / scales[p] / (points[i] - points[p])
            else:
                derivative[i, p] = sum((1.0 / (points[i] - points[k]) for k in range(4) if k != i))
    node_weight = (
        weights[:, None, None] * weights[None, :, None] * weights[None, None, :]
    ).reshape(64) / 8.0
    return (derivative, node_weight)


def constant_tables():
    derivative, node_weight = lobatto_tables()
    eye = np.eye(4)
    step = derivative.T
    mats = [
        np.kron(np.kron(step, eye), eye),
        np.kron(np.kron(eye, step), eye),
        np.kron(np.kron(eye, eye), step),
    ]
    nodes = np.arange(64).reshape(4, 4, 4)
    faces = [nodes[0], nodes[3], nodes[:, 0], nodes[:, 3], nodes[:, :, 0], nodes[:, :, 3]]
    for ids in faces:
        diag = np.zeros((64, 64))
        diag[ids.reshape(16), ids.reshape(16)] = 1.0
        mats.append(diag)
    mats = [0.1 * np.concatenate([m, m], axis=1) for m in mats]
    weights = np.repeat(node_weight[:, None], 128, axis=1)
    return jnp.asarray(np.stack(mats), F32), jnp.asarray(weights, F32)


def split2(x):
    hi = x.astype(BF)
    return hi, (x - hi.astype(F32)).astype(BF)


def dot(a, b):
    return jnp.dot(a, b, preferred_element_type=F32)


def dot_nt(a, b):
    return lax.dot_general(a, b, (((1,), (1,)), ((), ())), preferred_element_type=F32)


def one_hot(mask):
    return jnp.where(mask, jnp.ones((), BF), jnp.zeros((), BF))


def add_face(ref, tile, face, part):
    low = lax.broadcasted_iota(jnp.int32, (8, 128), 0) < 4
    for c in range(5):
        rows = part[c]
        if face < 2:
            ids = pl.ds(48 * face, 16)
            ref[tile, c, ids, :] = ref[tile, c, ids, :] + rows
        elif face >= 4:
            ids = pl.ds(3 * (face - 4), 16, stride=4)
            ref[tile, c, ids, :] = ref[tile, c, ids, :] + rows
        else:
            for v in range(2):
                both = rows[8 * v : 8 * v + 8]
                turned = pltpu.roll(both, 4, 0)
                for k in range(2):
                    ids = pl.ds(32 * v + 16 * k + 8 * (face - 2), 8)
                    value = both if k == face - 2 else turned
                    mask = low if face == 2 else jnp.logical_not(low)
                    ref[tile, c, ids, :] = ref[tile, c, ids, :] + jnp.where(mask, value, 0.0)


def mixed(coef_ref, face, c, parts):
    total = coef_ref[5 * c, face : face + 1, :] * parts[0]
    for h in range(1, 5):
        total += coef_ref[5 * c + h, face : face + 1, :] * parts[h]
    return total


def face_rows(ref, tile, c, face):
    if face < 2:
        return ref[tile, c, 48 * face : 48 * face + 16, :]
    if face >= 4:
        return ref[tile, c, pl.ds(3 * (face - 4), 16, stride=4), :]
    low = lax.broadcasted_iota(jnp.int32, (8, 128), 0) < 4
    out = []
    for v in range(2):
        first = ref[tile, c, 32 * v + 8 * (face - 2) : 32 * v + 8 * (face - 2) + 8, :]
        second = ref[tile, c, 32 * v + 16 + 8 * (face - 2) : 32 * v + 24 + 8 * (face - 2), :]
        if face == 2:
            out.append(jnp.where(low, first, pltpu.roll(second, 4, 0)))
        else:
            out.append(jnp.where(low, pltpu.roll(first, 4, 0), second))
    return jnp.concatenate(out, axis=0)


def exchange(sectors, slabs, owned, *refs):
    hbm_refs = refs[:INPUTS]
    acc_ref, grad_ref = refs[INPUTS : INPUTS + 2]
    x_ref = refs[INPUTS + 2]
    vmem_refs = (None,) + refs[INPUTS + 3 : 2 * INPUTS + 2]
    (
        _,
        vel_ref,
        drag_ref,
        bw_ref,
        jac_ref,
        own_ref,
        nbrmat_ref,
        nbr_ref,
        sslots_ref,
        aslots_ref,
        live_ref,
        eb_ref,
        mats_ref,
        weight_ref,
    ) = vmem_refs
    (
        xs_ref,
        tr_ref,
        oh_ref,
        place_ref,
        send_ref,
        recv_ref,
        a_ref,
        coef_ref,
        bsend_ref,
        brecv_ref,
        send_sem,
        recv_sem,
        far_sem,
        load_sem,
        x_sem,
    ) = refs[2 * INPUTS + 2 :]
    tiles = x_ref.shape[0]
    elems = tiles * 128
    slots = sslots_ref.shape[1]
    width = bsend_ref.shape[2]
    count = sectors * slabs

    loads = {
        k: pltpu.make_async_copy(hbm_refs[k], vmem_refs[k], load_sem.at[k])
        for k in range(1, INPUTS)
    }
    fields = {
        (t, h): pltpu.make_async_copy(
            hbm_refs[0].at[h, :, pl.ds(128 * t, 128)], x_ref.at[t, h], x_sem.at[5 * t + h]
        )
        for h in (1, 2, 3, 0, 4)
        for t in range(tiles)
    }
    sec = lax.axis_index("sector")
    axi = lax.axis_index("axial")
    joint = sec * slabs + axi
    prev = lax.rem(joint + count - 1, count)
    nxt = lax.rem(joint + 1, count)
    dev_prev = (prev // slabs, lax.rem(prev, slabs))
    dev_next = (nxt // slabs, lax.rem(nxt, slabs))
    dev_low = (lax.rem(sec + sectors - 1, sectors), axi)
    dev_high = (lax.rem(sec + 1, sectors), axi)

    has_low = axi > 0
    has_high = axi < slabs - 1

    barrier = pltpu.get_barrier_semaphore()

    def greet(device):
        pl.semaphore_signal(barrier, inc=1, device_id=device, device_id_type=MESH)

    greet(dev_low)
    greet(dev_high)
    greet(dev_prev)

    @pl.when(has_high)
    def _():
        greet(dev_next)

    def start_block_loads():
        for k in (1, 13, 2, 3, 11):
            loads[k].start()

    @pl.when(jnp.logical_not(has_high))
    def _():
        start_block_loads()

    for k in (9, 8, 10, 6):
        loads[k].start()
    for key in fields:
        fields[key].start()

    @pl.when(has_high)
    def _():
        start_block_loads()

    for k in (7, 12, 4, 5):
        loads[k].start()

    def remote(src, dst, k, device):
        return pltpu.make_async_remote_copy(
            src_ref=src,
            dst_ref=dst,
            send_sem=send_sem.at[k],
            recv_sem=recv_sem.at[k],
            device_id=device,
            device_id_type=MESH,
        )

    up_x = remote(send_ref.at[1], recv_ref.at[0], 0, dev_high)
    down_x = remote(send_ref.at[0], recv_ref.at[1], 1, dev_low)
    up_z = remote(send_ref.at[3], recv_ref.at[2], 2, dev_next)
    down_z = remote(send_ref.at[2], recv_ref.at[3], 3, dev_prev)
    up_b = remote(bsend_ref.at[2], brecv_ref.at[0], 4, dev_next)
    down_b = remote(bsend_ref.at[0], brecv_ref.at[1], 5, dev_prev)

    def sum_blocks():
        for k in (1, 13, 2, 3, 11):
            loads[k].wait()
        parts = []
        for t in range(tiles):
            lanes = slice(128 * t, 128 * t + 128)
            total = x_ref[t, 1] * vel_ref[0, :, lanes].astype(F32)
            total += x_ref[t, 2] * vel_ref[1, :, lanes].astype(F32)
            total += x_ref[t, 3] * vel_ref[2, :, lanes].astype(F32)
            parts.append(jnp.sum(total * weight_ref[...], axis=0, keepdims=True))
        elem_grad = drag_ref[...] * jnp.concatenate(parts, axis=1)
        weighted = bw_ref[...] * elem_grad
        w1 = weighted.astype(BF)
        rest = weighted - w1.astype(F32)
        w2 = rest.astype(BF)
        w3 = (rest - w2.astype(F32)).astype(BF).astype(F32)
        row16 = lax.broadcasted_iota(jnp.int32, (16, elems), 0)
        stack = jnp.where(row16 == 0, w1.astype(F32), 0.0)
        stack = jnp.where(row16 == 1, w2.astype(F32), stack)
        stack = jnp.where(row16 == 2, w3, stack).astype(BF)
        rel = eb_ref[...] - (joint - 1) * owned
        rel = jnp.where(rel < 0, rel + BLOCKS, rel)
        rel = jnp.where(rel >= BLOCKS, rel - BLOCKS, rel)
        for j in (1, 0):
            rel = jnp.where(rel >= owned * (j + 1), rel + (width - owned), rel)
        rows_blk = lax.broadcasted_iota(jnp.int32, (3 * width, elems), 0).astype(jnp.int16)
        ids = jnp.broadcast_to(rel, (3 * width, elems)).astype(jnp.int16)
        sums = dot_nt(stack, one_hot(rows_blk == ids))
        total = jnp.sum(sums, axis=0, keepdims=True)
        for j in range(3):
            part = total[:, j * width : (j + 1) * width]
            bsend_ref[j] = jnp.broadcast_to(part, (8, width))

    @pl.when(jnp.logical_not(has_high))
    def _():
        pl.semaphore_wait(barrier, 4)
        pl.semaphore_signal(far_sem, inc=1, device_id=dev_next, device_id_type=MESH)
        for h in (1, 2, 3):
            for t in range(tiles):
                fields[t, h].wait()
        sum_blocks()
        up_b.start()
        down_b.start()

    slot_ids = lax.broadcasted_iota(jnp.int32, (1, slots), 1)
    rows_slots = lax.broadcasted_iota(jnp.int32, (elems, slots), 0).astype(jnp.int16)

    columns = lax.broadcasted_iota(jnp.int32, (slots, elems), 1).astype(jnp.int16)

    def slot_row(i):
        if i >= 2:
            return aslots_ref[i - 2 : i - 1, :]
        return jnp.where(slot_ids < live_ref[:, i : i + 1], sslots_ref[i : i + 1, :], -1)

    def find_slots(i):
        ids = jnp.broadcast_to(slot_row(i), (elems, slots)).astype(jnp.int16)
        oh_ref[i] = one_hot(rows_slots == ids)

    def find_places(i):
        ids = jnp.broadcast_to(slot_row(i), (128, slots)).T
        ids = jnp.concatenate([ids] * tiles, axis=1).astype(jnp.int16)
        place_ref[i] = one_hot(columns == ids)

    def take_trace(t, face):
        lanes = slice(128 * t, 128 * t + 128)
        for c in range(5):
            hi, lo = split2(face_rows(x_ref, t, c, face))
            tr_ref[face, 16 * c : 16 * c + 16, lanes] = hi
            tr_ref[face, 80 + 16 * c : 96 + 16 * c, lanes] = lo

    def fill_send(i):
        face = SIDES[i]
        for t in range(tiles):
            take_trace(t, face)
        both = dot(tr_ref[face], oh_ref[i])
        both = both[:80] + both[80:]
        if i < 2:
            send_ref[i] = both
            return
        for n in range(0, slots, 128):
            parts = [both[16 * h : 16 * h + 16, n : n + 128] for h in range(5)]
            for c in range(5):
                value = mixed(coef_ref, 9 - face, c, parts)
                send_ref[i, 16 * c : 16 * c + 16, n : n + 128] = value

    for k in (9, 8, 10):
        loads[k].wait()
    for i in range(4):
        find_slots(i)
    loads[6].wait()
    for c in range(5):
        for h in range(5):
            coef_ref[5 * c + h] = jnp.broadcast_to(0.1 * nbrmat_ref[c][:, h : h + 1], (6, 128))
    @pl.when(has_high)
    def _():
        for h in (1, 2, 3):
            for t in range(tiles):
                fields[t, h].wait()

    for h in (0, 4):
        for t in range(tiles):
            fields[t, h].wait()
    fill_send(2)
    fill_send(3)

    @pl.when(jnp.logical_and(has_low, has_high))
    def _():
        pl.semaphore_wait(barrier, 4)

    @pl.when(jnp.logical_not(has_low))
    def _():
        pl.semaphore_wait(barrier, 3)

    @pl.when(has_high)
    def _():
        up_z.start()

    @pl.when(has_low)
    def _():
        down_z.start()

    @pl.when(jnp.logical_not(has_low))
    def _():
        recv_ref[2] = jnp.zeros((80, slots), F32)

    @pl.when(jnp.logical_not(has_high))
    def _():
        recv_ref[3] = jnp.zeros((80, slots), F32)

    fill_send(0)
    fill_send(1)
    up_x.start()
    down_x.start()

    @pl.when(has_high)
    def _():
        sum_blocks()
        up_b.start()

    @pl.when(jnp.logical_and(has_low, has_high))
    def _():
        down_b.start()

    for k in (7, 12, 4, 5):
        loads[k].wait()
    for i in range(4):
        find_places(i)

    spread = jnp.minimum(lax.broadcasted_iota(jnp.int32, (5, 384), 1) // 64, 4)
    spread = jnp.where(spread == lax.broadcasted_iota(jnp.int32, (5, 384), 0), 1.0, 0.0)
    for c in range(5):
        rows = slice(64 * c, 64 * c + 64)
        jac = jac_ref[0][:, c : c + 1] * spread[0:1, :]
        face = own_ref[c][:, 0:1] * spread[0:1, :]
        for h in range(1, 5):
            jac += jac_ref[h][:, c : c + 1] * spread[h : h + 1, :]
            face += own_ref[c][:, h : h + 1] * spread[h : h + 1, :]
        for t in range(3):
            lanes = slice(128 * t, 128 * t + 128)
            total = mats_ref[0] * jac[0:1, lanes]
            for j in range(1, 9):
                row = jac[j : j + 1, lanes] if j < 3 else face[j - 3 : j - 2, lanes]
                total += mats_ref[j] * row
            hi, lo = split2(total)
            places = ((768, hi), (896, lo)) if t == 2 else ((0, hi), (256, hi), (512, lo))
            for base, part in places:
                base += 128 * t if t < 2 else 0
                a_ref[rows, base : base + 128] = part

    for t in range(tiles):
        lanes = slice(128 * t, 128 * t + 128)
        for h in range(5):
            hi, lo = split2(x_ref[t, h])
            for base, part in ((0, hi), (256, lo)) if h < 4 else ((256, hi), (320, lo)):
                xs_ref[64 * h + base : 64 * h + base + 64, lanes] = part
        for face in (2, 3):
            take_trace(t, face)

    xs = [xs_ref[rows, :] for rows in (slice(0, 512), slice(0, 256), slice(512, 640), slice(512, 576))]
    own = dot(a_ref[:, 0:960], jnp.concatenate(xs, axis=0))
    keep = 1.0 - 0.1 * drag_ref[...]
    for t in range(tiles):
        lanes = slice(128 * t, 128 * t + 128)
        for c in range(5):
            x = x_ref[t, c]
            scaled = x * keep[:, lanes] if 1 <= c <= 3 else x
            acc_ref[t, c] = scaled + own[64 * c : 64 * c + 64, lanes]

    rows_src = lax.broadcasted_iota(jnp.int32, (elems, elems), 0).astype(jnp.int16)
    def gather(f, i=None):
        g = f + 1 - 2 * (f % 2)
        ids = jnp.broadcast_to(nbr_ref[f : f + 1, :], (elems, elems)).astype(jnp.int16)
        sources, places = tr_ref[g], one_hot(rows_src == ids)
        if i is not None:
            got = jnp.concatenate(split2(recv_ref[i]), axis=0)
            sources = jnp.concatenate([sources, got], axis=1)
            places = jnp.concatenate([places, place_ref[i]], axis=0)
        both = dot(sources, places)
        both = both[:80] + both[80:]
        for t in range(tiles):
            parts = [both[16 * h : 16 * h + 16, 128 * t : 128 * t + 128] for h in range(5)]
            add_face(acc_ref, t, f, [mixed(coef_ref, f, c, parts) for c in range(5)])

    for f in (2, 3, 4, 5):
        gather(f)

    @pl.when(jnp.logical_not(has_low))
    def _():
        pl.semaphore_wait(far_sem, 1)
        down_b.start()

    up_x.wait()
    down_x.wait()
    gather(0, 0)
    gather(1, 1)

    @pl.when(has_high)
    def _():
        up_z.wait_send()
        down_z.wait_recv()

    @pl.when(has_low)
    def _():
        down_z.wait_send()
        up_z.wait_recv()

    for i in (2, 3):
        both = dot(jnp.concatenate(split2(recv_ref[i]), axis=0), place_ref[i])
        both = both[:80] + both[80:]
        for t in range(tiles):
            lanes = slice(128 * t, 128 * t + 128)
            rows = [both[16 * c : 16 * c + 16, lanes] for c in range(5)]
            add_face(acc_ref, t, SIDES[i], rows)

    up_b.wait()
    down_b.wait()
    sums = bsend_ref[1] + brecv_ref[0] + brecv_ref[1]
    grad_ref[...] = sums[0, :owned]


def finish(acc_ref, sums_ref, out_ref, grad_ref, sem):
    tiles = acc_ref.shape[0]
    copies = [pltpu.make_async_copy(sums_ref, grad_ref, sem.at[tiles])]
    for t in range(tiles):
        place = out_ref.at[:, :, pl.ds(128 * t, 128)]
        copies.append(pltpu.make_async_copy(acc_ref.at[t], place, sem.at[t]))
    for copy in copies:
        copy.start()
    for copy in copies:
        copy.wait()


def on_device(
    sectors,
    slabs,
    adjoint,
    velocity,
    drag,
    block_weight,
    flux_jac,
    face_own,
    face_nbr,
    nbr_local,
    sector_slots,
    axial_slots,
    sector_live,
    elem_block,
):
    elems = adjoint.shape[2]
    tiles = elems // 128
    slots = sector_slots.shape[1]
    owned = BLOCKS // (sectors * slabs)
    width = -(-owned // 128) * 128
    operands = (
        adjoint,
        velocity,
        drag.reshape(1, elems),
        block_weight.reshape(1, elems),
        jnp.transpose(flux_jac, (1, 0, 2)),
        jnp.transpose(face_own, (1, 0, 2)),
        jnp.transpose(face_nbr, (1, 0, 2)),
        nbr_local,
        sector_slots,
        axial_slots,
        sector_live.reshape(1, 2),
        elem_block.reshape(1, elems),
        *constant_tables(),
    )
    vmem = pl.BlockSpec(memory_space=pltpu.VMEM)
    hbm = pl.BlockSpec(memory_space=pltpu.HBM)
    handed = pl.pallas_call(
        functools.partial(exchange, sectors, slabs, owned),
        out_shape=(
            pltpu.VMEM((tiles, 5, 64, 128), F32),
            pltpu.VMEM((owned,), F32),
        ),
        in_specs=[hbm] * INPUTS,
        out_specs=(vmem,) * 2,
        scratch_shapes=[pltpu.VMEM((tiles, 5, 64, 128), F32)]
        + [pltpu.VMEM(a.shape, a.dtype) for a in operands[1:]]
        + [
            pltpu.VMEM((640, elems), BF),
            pltpu.VMEM((6, 160, elems), BF),
            pltpu.VMEM((4, elems, slots), BF),
            pltpu.VMEM((4, slots, elems), BF),
            pltpu.VMEM((4, 80, slots), F32),
            pltpu.VMEM((4, 80, slots), F32),
            pltpu.VMEM((320, 1024), BF),
            pltpu.VMEM((25, 6, 128), F32),
            pltpu.VMEM((3, 8, width), F32),
            pltpu.VMEM((2, 8, width), F32),
            pltpu.SemaphoreType.DMA((6,)),
            pltpu.SemaphoreType.DMA((6,)),
            pltpu.SemaphoreType.REGULAR,
            pltpu.SemaphoreType.DMA((INPUTS,)),
            pltpu.SemaphoreType.DMA((5 * tiles,)),
        ],
        compiler_params=pltpu.CompilerParams(
            collective_id=0, has_side_effects=True, vmem_limit_bytes=60 * 1024 * 1024
        ),
    )(*operands)
    return pl.pallas_call(
        finish,
        out_shape=(
            jax.ShapeDtypeStruct(adjoint.shape, F32),
            jax.ShapeDtypeStruct((owned,), F32),
        ),
        in_specs=[vmem] * 2,
        out_specs=(hbm, hbm),
        scratch_shapes=[
            pltpu.SemaphoreType.DMA((tiles + 1,)),
        ],
        compiler_params=pltpu.CompilerParams(vmem_limit_bytes=40 * 1024 * 1024),
    )(*handed)


def solution(mesh):
    placed = (
        P(None, None, ("sector", "axial")),
        P(None, None, ("sector", "axial")),
        P(("sector", "axial")),
        P(("sector", "axial")),
        P(),
        P(),
        P(),
        P(None, ("sector", "axial")),
        P(None, ("sector", "axial")),
        P(None, ("sector", "axial")),
        P("sector", "axial", None),
        P(("sector", "axial")),
    )
    return jax.shard_map(
        functools.partial(on_device, mesh.shape["sector"], mesh.shape["axial"]),
        mesh=mesh,
        in_specs=placed,
        out_specs=(P(None, None, ("sector", "axial")), P(("sector", "axial"))),
        check_vma=False,
    )
```

```python
import functools

import jax
import jax.numpy as jnp
import numpy as np
from jax import lax
from jax.experimental import pallas as pl
from jax.experimental.pallas import tpu as pltpu
from jax.sharding import PartitionSpec as P

BLOCKS = 4096
BF = jnp.bfloat16
F32 = jnp.float32
MESH = pl.DeviceIdType.MESH
INPUTS = 14
SIDES = (0, 1, 4, 5)


def lobatto_tables():
    points = np.array([-1.0, -1.0 / np.sqrt(5.0), 1.0 / np.sqrt(5.0), 1.0])
    weights = np.array([1.0, 5.0, 5.0, 1.0]) / 6.0
    scales = np.array(
        [np.prod([points[i] - points[k] for k in range(4) if k != i]) for i in range(4)]
    )
    derivative = np.zeros((4, 4))
    for i in range(4):
        for p in range(4):
            if i != p:
                derivative[i, p] = scales[i] / scales[p] / (points[i] - points[p])
            else:
                derivative[i, p] = sum((1.0 / (points[i] - points[k]) for k in range(4) if k != i))
    node_weight = (
        weights[:, None, None] * weights[None, :, None] * weights[None, None, :]
    ).reshape(64) / 8.0
    return (derivative, node_weight)


def constant_tables():
    derivative, node_weight = lobatto_tables()
    eye = np.eye(4)
    step = derivative.T
    mats = [
        np.kron(np.kron(step, eye), eye),
        np.kron(np.kron(eye, step), eye),
        np.kron(np.kron(eye, eye), step),
    ]
    nodes = np.arange(64).reshape(4, 4, 4)
    faces = [nodes[0], nodes[3], nodes[:, 0], nodes[:, 3], nodes[:, :, 0], nodes[:, :, 3]]
    for ids in faces:
        diag = np.zeros((64, 64))
        diag[ids.reshape(16), ids.reshape(16)] = 1.0
        mats.append(diag)
    mats = [0.1 * np.concatenate([m, m], axis=1) for m in mats]
    weights = np.repeat(node_weight[:, None], 128, axis=1)
    return jnp.asarray(np.stack(mats), F32), jnp.asarray(weights, F32)


def split2(x):
    hi = x.astype(BF)
    return hi, (x - hi.astype(F32)).astype(BF)


def dot(a, b):
    return jnp.dot(a, b, preferred_element_type=F32)


def dot_nt(a, b):
    return lax.dot_general(a, b, (((1,), (1,)), ((), ())), preferred_element_type=F32)


def one_hot(mask):
    return jnp.where(mask, jnp.ones((), BF), jnp.zeros((), BF))


def add_face(ref, tile, face, part):
    low = lax.broadcasted_iota(jnp.int32, (8, 128), 0) < 4
    for c in range(5):
        rows = part[c]
        if face < 2:
            ids = pl.ds(48 * face, 16)
            ref[tile, c, ids, :] = ref[tile, c, ids, :] + rows
        elif face >= 4:
            ids = pl.ds(3 * (face - 4), 16, stride=4)
            ref[tile, c, ids, :] = ref[tile, c, ids, :] + rows
        else:
            for v in range(2):
                both = rows[8 * v : 8 * v + 8]
                turned = pltpu.roll(both, 4, 0)
                for k in range(2):
                    ids = pl.ds(32 * v + 16 * k + 8 * (face - 2), 8)
                    value = both if k == face - 2 else turned
                    mask = low if face == 2 else jnp.logical_not(low)
                    ref[tile, c, ids, :] = ref[tile, c, ids, :] + jnp.where(mask, value, 0.0)


def mixed(coef_ref, face, c, parts):
    total = coef_ref[5 * c, face : face + 1, :] * parts[0]
    for h in range(1, 5):
        total += coef_ref[5 * c + h, face : face + 1, :] * parts[h]
    return total


def face_rows(ref, tile, c, face):
    if face < 2:
        return ref[tile, c, 48 * face : 48 * face + 16, :]
    if face >= 4:
        return ref[tile, c, pl.ds(3 * (face - 4), 16, stride=4), :]
    low = lax.broadcasted_iota(jnp.int32, (8, 128), 0) < 4
    out = []
    for v in range(2):
        first = ref[tile, c, 32 * v + 8 * (face - 2) : 32 * v + 8 * (face - 2) + 8, :]
        second = ref[tile, c, 32 * v + 16 + 8 * (face - 2) : 32 * v + 24 + 8 * (face - 2), :]
        if face == 2:
            out.append(jnp.where(low, first, pltpu.roll(second, 4, 0)))
        else:
            out.append(jnp.where(low, pltpu.roll(first, 4, 0), second))
    return jnp.concatenate(out, axis=0)


def exchange(sectors, slabs, owned, *refs):
    hbm_refs = refs[:INPUTS]
    acc_ref, grad_ref = refs[INPUTS : INPUTS + 2]
    x_ref = refs[INPUTS + 2]
    vmem_refs = (None,) + refs[INPUTS + 3 : 2 * INPUTS + 2]
    (
        _,
        vel_ref,
        drag_ref,
        bw_ref,
        jac_ref,
        own_ref,
        nbrmat_ref,
        nbr_ref,
        sslots_ref,
        aslots_ref,
        live_ref,
        eb_ref,
        mats_ref,
        weight_ref,
    ) = vmem_refs
    (
        xs_ref,
        tr_ref,
        oh_ref,
        place_ref,
        send_ref,
        recv_ref,
        a_ref,
        coef_ref,
        bsend_ref,
        brecv_ref,
        send_sem,
        recv_sem,
        far_sem,
        load_sem,
        x_sem,
    ) = refs[2 * INPUTS + 2 :]
    tiles = x_ref.shape[0]
    elems = tiles * 128
    slots = sslots_ref.shape[1]
    width = bsend_ref.shape[2]
    count = sectors * slabs

    loads = {
        k: pltpu.make_async_copy(hbm_refs[k], vmem_refs[k], load_sem.at[k])
        for k in range(1, INPUTS)
    }
    fields = {
        (t, h): pltpu.make_async_copy(
            hbm_refs[0].at[h, :, pl.ds(128 * t, 128)], x_ref.at[t, h], x_sem.at[5 * t + h]
        )
        for t in range(tiles)
        for h in range(5)
    }
    sec = lax.axis_index("sector")
    axi = lax.axis_index("axial")
    joint = sec * slabs + axi
    prev = lax.rem(joint + count - 1, count)
    nxt = lax.rem(joint + 1, count)
    dev_prev = (prev // slabs, lax.rem(prev, slabs))
    dev_next = (nxt // slabs, lax.rem(nxt, slabs))
    dev_low = (lax.rem(sec + sectors - 1, sectors), axi)
    dev_high = (lax.rem(sec + 1, sectors), axi)

    has_low = axi > 0
    has_high = axi < slabs - 1

    barrier = pltpu.get_barrier_semaphore()

    def greet(device):
        pl.semaphore_signal(barrier, inc=1, device_id=device, device_id_type=MESH)

    greet(dev_low)
    greet(dev_high)
    greet(dev_prev)

    @pl.when(has_high)
    def _():
        greet(dev_next)

    def start_block_loads():
        for k in (1, 13, 2, 3, 11):
            loads[k].start()

    def start_fields(*which):
        for t in range(tiles):
            for h in which:
                fields[t, h].start()

    @pl.when(jnp.logical_not(has_high))
    def _():
        start_block_loads()
        start_fields(1, 2, 3)

    for k in (9, 8, 10, 6):
        loads[k].start()

    @pl.when(has_high)
    def _():
        start_fields(1, 2, 3)

    start_fields(0, 4)

    @pl.when(has_high)
    def _():
        start_block_loads()

    for k in (7, 12, 4, 5):
        loads[k].start()

    def remote(src, dst, k, device):
        return pltpu.make_async_remote_copy(
            src_ref=src,
            dst_ref=dst,
            send_sem=send_sem.at[k],
            recv_sem=recv_sem.at[k],
            device_id=device,
            device_id_type=MESH,
        )

    up_x = remote(send_ref.at[1], recv_ref.at[0], 0, dev_high)
    down_x = remote(send_ref.at[0], recv_ref.at[1], 1, dev_low)
    up_z = remote(send_ref.at[3], recv_ref.at[2], 2, dev_next)
    down_z = remote(send_ref.at[2], recv_ref.at[3], 3, dev_prev)
    up_b = remote(bsend_ref.at[2], brecv_ref.at[0], 4, dev_next)
    down_b = remote(bsend_ref.at[0], brecv_ref.at[1], 5, dev_prev)

    def sum_blocks(arriving):
        for k in (1, 13, 2, 3, 11):
            loads[k].wait()
        parts = []
        for t in range(tiles):
            lanes = slice(128 * t, 128 * t + 128)
            if arriving:
                for h in (1, 2, 3):
                    fields[t, h].wait()
            total = x_ref[t, 1] * vel_ref[0, :, lanes].astype(F32)
            total += x_ref[t, 2] * vel_ref[1, :, lanes].astype(F32)
            total += x_ref[t, 3] * vel_ref[2, :, lanes].astype(F32)
            parts.append(jnp.sum(total * weight_ref[...], axis=0, keepdims=True))
        elem_grad = drag_ref[...] * jnp.concatenate(parts, axis=1)
        weighted = bw_ref[...] * elem_grad
        w1 = weighted.astype(BF)
        rest = weighted - w1.astype(F32)
        w2 = rest.astype(BF)
        w3 = (rest - w2.astype(F32)).astype(BF).astype(F32)
        row16 = lax.broadcasted_iota(jnp.int32, (16, elems), 0)
        stack = jnp.where(row16 == 0, w1.astype(F32), 0.0)
        stack = jnp.where(row16 == 1, w2.astype(F32), stack)
        stack = jnp.where(row16 == 2, w3, stack).astype(BF)
        rel = eb_ref[...] - (joint - 1) * owned
        rel = jnp.where(rel < 0, rel + BLOCKS, rel)
        rel = jnp.where(rel >= BLOCKS, rel - BLOCKS, rel)
        for j in (1, 0):
            rel = jnp.where(rel >= owned * (j + 1), rel + (width - owned), rel)
        rows_blk = lax.broadcasted_iota(jnp.int32, (3 * width, elems), 0).astype(jnp.int16)
        ids = jnp.broadcast_to(rel, (3 * width, elems)).astype(jnp.int16)
        sums = dot_nt(stack, one_hot(rows_blk == ids))
        total = jnp.sum(sums, axis=0, keepdims=True)
        for j in range(3):
            part = total[:, j * width : (j + 1) * width]
            bsend_ref[j] = jnp.broadcast_to(part, (8, width))

    @pl.when(jnp.logical_not(has_high))
    def _():
        pl.semaphore_wait(barrier, 4)
        pl.semaphore_signal(far_sem, inc=1, device_id=dev_next, device_id_type=MESH)
        sum_blocks(True)
        up_b.start()
        down_b.start()

    slot_ids = lax.broadcasted_iota(jnp.int32, (1, slots), 1)
    rows_slots = lax.broadcasted_iota(jnp.int32, (elems, slots), 0).astype(jnp.int16)

    columns = lax.broadcasted_iota(jnp.int32, (slots, elems), 1).astype(jnp.int16)

    def slot_row(i):
        if i >= 2:
            return aslots_ref[i - 2 : i - 1, :]
        return jnp.where(slot_ids < live_ref[:, i : i + 1], sslots_ref[i : i + 1, :], -1)

    def find_slots(i):
        ids = jnp.broadcast_to(slot_row(i), (elems, slots)).astype(jnp.int16)
        oh_ref[i] = one_hot(rows_slots == ids)

    def find_places(i):
        ids = jnp.broadcast_to(slot_row(i), (128, slots)).T
        ids = jnp.concatenate([ids] * tiles, axis=1).astype(jnp.int16)
        place_ref[i] = one_hot(columns == ids)

    def take_trace(t, face):
        lanes = slice(128 * t, 128 * t + 128)
        for c in range(5):
            hi, lo = split2(face_rows(x_ref, t, c, face))
            tr_ref[face, 16 * c : 16 * c + 16, lanes] = hi
            tr_ref[face, 80 + 16 * c : 96 + 16 * c, lanes] = lo

    def fill_send(i):
        face = SIDES[i]
        for t in range(tiles):
            take_trace(t, face)
        both = dot(tr_ref[face], oh_ref[i])
        both = both[:80] + both[80:]
        if i < 2:
            send_ref[i] = both
            return
        for n in range(0, slots, 128):
            parts = [both[16 * h : 16 * h + 16, n : n + 128] for h in range(5)]
            for c in range(5):
                value = mixed(coef_ref, 9 - face, c, parts)
                send_ref[i, 16 * c : 16 * c + 16, n : n + 128] = value

    for k in (9, 8, 10):
        loads[k].wait()
    for i in range(4):
        find_slots(i)
    loads[6].wait()
    for c in range(5):
        for h in range(5):
            coef_ref[5 * c + h] = jnp.broadcast_to(0.1 * nbrmat_ref[c][:, h : h + 1], (6, 128))
    @pl.when(has_high)
    def _():
        for h in (1, 2, 3):
            for t in range(tiles):
                fields[t, h].wait()

    for h in (0, 4):
        for t in range(tiles):
            fields[t, h].wait()
    fill_send(2)
    fill_send(3)

    @pl.when(jnp.logical_and(has_low, has_high))
    def _():
        pl.semaphore_wait(barrier, 4)

    @pl.when(jnp.logical_not(has_low))
    def _():
        pl.semaphore_wait(barrier, 3)

    @pl.when(has_high)
    def _():
        up_z.start()

    @pl.when(has_low)
    def _():
        down_z.start()

    @pl.when(jnp.logical_not(has_low))
    def _():
        recv_ref[2] = jnp.zeros((80, slots), F32)

    @pl.when(jnp.logical_not(has_high))
    def _():
        recv_ref[3] = jnp.zeros((80, slots), F32)

    fill_send(0)
    fill_send(1)
    up_x.start()
    down_x.start()

    @pl.when(has_high)
    def _():
        sum_blocks(False)
        up_b.start()

    @pl.when(jnp.logical_and(has_low, has_high))
    def _():
        down_b.start()

    for k in (7, 12, 4, 5):
        loads[k].wait()
    for i in range(4):
        find_places(i)

    spread = jnp.minimum(lax.broadcasted_iota(jnp.int32, (5, 384), 1) // 64, 4)
    spread = jnp.where(spread == lax.broadcasted_iota(jnp.int32, (5, 384), 0), 1.0, 0.0)
    for c in range(5):
        rows = slice(64 * c, 64 * c + 64)
        jac = jac_ref[0][:, c : c + 1] * spread[0:1, :]
        face = own_ref[c][:, 0:1] * spread[0:1, :]
        for h in range(1, 5):
            jac += jac_ref[h][:, c : c + 1] * spread[h : h + 1, :]
            face += own_ref[c][:, h : h + 1] * spread[h : h + 1, :]
        for t in range(3):
            lanes = slice(128 * t, 128 * t + 128)
            total = mats_ref[0] * jac[0:1, lanes]
            for j in range(1, 9):
                row = jac[j : j + 1, lanes] if j < 3 else face[j - 3 : j - 2, lanes]
                total += mats_ref[j] * row
            hi, lo = split2(total)
            places = ((768, hi), (896, lo)) if t == 2 else ((0, hi), (256, hi), (512, lo))
            for base, part in places:
                base += 128 * t if t < 2 else 0
                a_ref[rows, base : base + 128] = part

    for t in range(tiles):
        lanes = slice(128 * t, 128 * t + 128)
        for h in range(5):
            hi, lo = split2(x_ref[t, h])
            for base, part in ((0, hi), (256, lo)) if h < 4 else ((256, hi), (320, lo)):
                xs_ref[64 * h + base : 64 * h + base + 64, lanes] = part
        for face in (2, 3):
            take_trace(t, face)

    xs = [xs_ref[rows, :] for rows in (slice(0, 512), slice(0, 256), slice(512, 640), slice(512, 576))]
    own = dot(a_ref[:, 0:960], jnp.concatenate(xs, axis=0))
    keep = 1.0 - 0.1 * drag_ref[...]
    for t in range(tiles):
        lanes = slice(128 * t, 128 * t + 128)
        for c in range(5):
            x = x_ref[t, c]
            scaled = x * keep[:, lanes] if 1 <= c <= 3 else x
            acc_ref[t, c] = scaled + own[64 * c : 64 * c + 64, lanes]

    rows_src = lax.broadcasted_iota(jnp.int32, (elems, elems), 0).astype(jnp.int16)
    def gather(f, i=None):
        g = f + 1 - 2 * (f % 2)
        ids = jnp.broadcast_to(nbr_ref[f : f + 1, :], (elems, elems)).astype(jnp.int16)
        sources, places = tr_ref[g], one_hot(rows_src == ids)
        if i is not None:
            got = jnp.concatenate(split2(recv_ref[i]), axis=0)
            sources = jnp.concatenate([sources, got], axis=1)
            places = jnp.concatenate([places, place_ref[i]], axis=0)
        both = dot(sources, places)
        both = both[:80] + both[80:]
        for t in range(tiles):
            parts = [both[16 * h : 16 * h + 16, 128 * t : 128 * t + 128] for h in range(5)]
            add_face(acc_ref, t, f, [mixed(coef_ref, f, c, parts) for c in range(5)])

    def answer_far(mine):
        @pl.when(jnp.logical_and(jnp.logical_not(has_low), mine))
        def _():
            pl.semaphore_wait(far_sem, 1)
            down_b.start()

    gather(2)
    gather(3)
    gather(4)
    answer_far(sec >= sectors // 2)
    gather(5)

    up_x.wait()
    down_x.wait()
    gather(0, 0)
    gather(1, 1)
    answer_far(sec < sectors // 2)

    @pl.when(has_high)
    def _():
        up_z.wait_send()
        down_z.wait_recv()

    @pl.when(has_low)
    def _():
        down_z.wait_send()
        up_z.wait_recv()

    for i in (2, 3):
        both = dot(jnp.concatenate(split2(recv_ref[i]), axis=0), place_ref[i])
        both = both[:80] + both[80:]
        for t in range(tiles):
            lanes = slice(128 * t, 128 * t + 128)
            rows = [both[16 * c : 16 * c + 16, lanes] for c in range(5)]
            add_face(acc_ref, t, SIDES[i], rows)

    up_b.wait()
    down_b.wait()
    sums = bsend_ref[1] + brecv_ref[0] + brecv_ref[1]
    grad_ref[...] = sums[0, :owned]


def finish(acc_ref, sums_ref, out_ref, grad_ref, sem):
    tiles = acc_ref.shape[0]
    copies = [pltpu.make_async_copy(sums_ref, grad_ref, sem.at[tiles])]
    for t in range(tiles):
        place = out_ref.at[:, :, pl.ds(128 * t, 128)]
        copies.append(pltpu.make_async_copy(acc_ref.at[t], place, sem.at[t]))
    for copy in copies:
        copy.start()
    for copy in copies:
        copy.wait()


def on_device(
    sectors,
    slabs,
    adjoint,
    velocity,
    drag,
    block_weight,
    flux_jac,
    face_own,
    face_nbr,
    nbr_local,
    sector_slots,
    axial_slots,
    sector_live,
    elem_block,
):
    elems = adjoint.shape[2]
    tiles = elems // 128
    slots = sector_slots.shape[1]
    owned = BLOCKS // (sectors * slabs)
    width = -(-owned // 128) * 128
    operands = (
        adjoint,
        velocity,
        drag.reshape(1, elems),
        block_weight.reshape(1, elems),
        jnp.transpose(flux_jac, (1, 0, 2)),
        jnp.transpose(face_own, (1, 0, 2)),
        jnp.transpose(face_nbr, (1, 0, 2)),
        nbr_local,
        sector_slots,
        axial_slots,
        sector_live.reshape(1, 2),
        elem_block.reshape(1, elems),
        *constant_tables(),
    )
    vmem = pl.BlockSpec(memory_space=pltpu.VMEM)
    hbm = pl.BlockSpec(memory_space=pltpu.HBM)
    handed = pl.pallas_call(
        functools.partial(exchange, sectors, slabs, owned),
        out_shape=(
            pltpu.VMEM((tiles, 5, 64, 128), F32),
            pltpu.VMEM((owned,), F32),
        ),
        in_specs=[hbm] * INPUTS,
        out_specs=(vmem,) * 2,
        scratch_shapes=[pltpu.VMEM((tiles, 5, 64, 128), F32)]
        + [pltpu.VMEM(a.shape, a.dtype) for a in operands[1:]]
        + [
            pltpu.VMEM((640, elems), BF),
            pltpu.VMEM((6, 160, elems), BF),
            pltpu.VMEM((4, elems, slots), BF),
            pltpu.VMEM((4, slots, elems), BF),
            pltpu.VMEM((4, 80, slots), F32),
            pltpu.VMEM((4, 80, slots), F32),
            pltpu.VMEM((320, 1024), BF),
            pltpu.VMEM((25, 6, 128), F32),
            pltpu.VMEM((3, 8, width), F32),
            pltpu.VMEM((2, 8, width), F32),
            pltpu.SemaphoreType.DMA((6,)),
            pltpu.SemaphoreType.DMA((6,)),
            pltpu.SemaphoreType.REGULAR,
            pltpu.SemaphoreType.DMA((INPUTS,)),
            pltpu.SemaphoreType.DMA((5 * tiles,)),
        ],
        compiler_params=pltpu.CompilerParams(
            collective_id=0, has_side_effects=True, vmem_limit_bytes=60 * 1024 * 1024
        ),
    )(*operands)
    return pl.pallas_call(
        finish,
        out_shape=(
            jax.ShapeDtypeStruct(adjoint.shape, F32),
            jax.ShapeDtypeStruct((owned,), F32),
        ),
        in_specs=[vmem] * 2,
        out_specs=(hbm, hbm),
        scratch_shapes=[
            pltpu.SemaphoreType.DMA((tiles + 1,)),
        ],
        compiler_params=pltpu.CompilerParams(vmem_limit_bytes=40 * 1024 * 1024),
    )(*handed)


def solution(mesh):
    placed = (
        P(None, None, ("sector", "axial")),
        P(None, None, ("sector", "axial")),
        P(("sector", "axial")),
        P(("sector", "axial")),
        P(),
        P(),
        P(),
        P(None, ("sector", "axial")),
        P(None, ("sector", "axial")),
        P(None, ("sector", "axial")),
        P("sector", "axial", None),
        P(("sector", "axial")),
    )
    return jax.shard_map(
        functools.partial(on_device, mesh.shape["sector"], mesh.shape["axial"]),
        mesh=mesh,
        in_specs=placed,
        out_specs=(P(None, None, ("sector", "axial")), P(("sector", "axial"))),
        check_vma=False,
    )
```

```python
import functools

import jax
import jax.numpy as jnp
import numpy as np
from jax import lax
from jax.experimental import pallas as pl
from jax.experimental.pallas import tpu as pltpu
from jax.sharding import PartitionSpec as P

BLOCKS = 4096
BF = jnp.bfloat16
F32 = jnp.float32
MESH = pl.DeviceIdType.MESH
INPUTS = 14
SIDES = (0, 1, 4, 5)


def lobatto_tables():
    points = np.array([-1.0, -1.0 / np.sqrt(5.0), 1.0 / np.sqrt(5.0), 1.0])
    weights = np.array([1.0, 5.0, 5.0, 1.0]) / 6.0
    scales = np.array(
        [np.prod([points[i] - points[k] for k in range(4) if k != i]) for i in range(4)]
    )
    derivative = np.zeros((4, 4))
    for i in range(4):
        for p in range(4):
            if i != p:
                derivative[i, p] = scales[i] / scales[p] / (points[i] - points[p])
            else:
                derivative[i, p] = sum((1.0 / (points[i] - points[k]) for k in range(4) if k != i))
    node_weight = (
        weights[:, None, None] * weights[None, :, None] * weights[None, None, :]
    ).reshape(64) / 8.0
    return (derivative, node_weight)


def constant_tables():
    derivative, node_weight = lobatto_tables()
    eye = np.eye(4)
    step = derivative.T
    mats = [
        np.kron(np.kron(step, eye), eye),
        np.kron(np.kron(eye, step), eye),
        np.kron(np.kron(eye, eye), step),
    ]
    nodes = np.arange(64).reshape(4, 4, 4)
    faces = [nodes[0], nodes[3], nodes[:, 0], nodes[:, 3], nodes[:, :, 0], nodes[:, :, 3]]
    for ids in faces:
        diag = np.zeros((64, 64))
        diag[ids.reshape(16), ids.reshape(16)] = 1.0
        mats.append(diag)
    mats = [0.1 * np.concatenate([m, m], axis=1) for m in mats]
    weights = np.repeat(node_weight[:, None], 128, axis=1)
    return jnp.asarray(np.stack(mats), F32), jnp.asarray(weights, F32)


def split2(x):
    hi = x.astype(BF)
    return hi, (x - hi.astype(F32)).astype(BF)


def dot(a, b):
    return jnp.dot(a, b, preferred_element_type=F32)


def dot_nt(a, b):
    return lax.dot_general(a, b, (((1,), (1,)), ((), ())), preferred_element_type=F32)


def one_hot(mask):
    return jnp.where(mask, jnp.ones((), BF), jnp.zeros((), BF))


def add_face(ref, tile, face, part):
    low = lax.broadcasted_iota(jnp.int32, (8, 128), 0) < 4
    for c in range(5):
        rows = part[c]
        if face < 2:
            ids = pl.ds(48 * face, 16)
            ref[tile, c, ids, :] = ref[tile, c, ids, :] + rows
        elif face >= 4:
            ids = pl.ds(3 * (face - 4), 16, stride=4)
            ref[tile, c, ids, :] = ref[tile, c, ids, :] + rows
        else:
            for v in range(2):
                both = rows[8 * v : 8 * v + 8]
                turned = pltpu.roll(both, 4, 0)
                for k in range(2):
                    ids = pl.ds(32 * v + 16 * k + 8 * (face - 2), 8)
                    value = both if k == face - 2 else turned
                    mask = low if face == 2 else jnp.logical_not(low)
                    ref[tile, c, ids, :] = ref[tile, c, ids, :] + jnp.where(mask, value, 0.0)


def mixed(coef_ref, face, c, parts):
    total = coef_ref[5 * c, face : face + 1, :] * parts[0]
    for h in range(1, 5):
        total += coef_ref[5 * c + h, face : face + 1, :] * parts[h]
    return total


def face_rows(ref, tile, c, face):
    if face < 2:
        return ref[tile, c, 48 * face : 48 * face + 16, :]
    if face >= 4:
        return ref[tile, c, pl.ds(3 * (face - 4), 16, stride=4), :]
    low = lax.broadcasted_iota(jnp.int32, (8, 128), 0) < 4
    out = []
    for v in range(2):
        first = ref[tile, c, 32 * v + 8 * (face - 2) : 32 * v + 8 * (face - 2) + 8, :]
        second = ref[tile, c, 32 * v + 16 + 8 * (face - 2) : 32 * v + 24 + 8 * (face - 2), :]
        if face == 2:
            out.append(jnp.where(low, first, pltpu.roll(second, 4, 0)))
        else:
            out.append(jnp.where(low, pltpu.roll(first, 4, 0), second))
    return jnp.concatenate(out, axis=0)


def exchange(sectors, slabs, owned, *refs):
    hbm_refs = refs[:INPUTS]
    acc_ref, grad_ref = refs[INPUTS : INPUTS + 2]
    x_ref = refs[INPUTS + 2]
    vmem_refs = (None,) + refs[INPUTS + 3 : 2 * INPUTS + 2]
    (
        _,
        vel_ref,
        drag_ref,
        bw_ref,
        jac_ref,
        own_ref,
        nbrmat_ref,
        nbr_ref,
        sslots_ref,
        aslots_ref,
        live_ref,
        eb_ref,
        mats_ref,
        weight_ref,
    ) = vmem_refs
    (
        xs_ref,
        tr_ref,
        oh_ref,
        place_ref,
        send_ref,
        recv_ref,
        a_ref,
        coef_ref,
        blocks_ref,
        bsend_ref,
        brecv_ref,
        send_sem,
        recv_sem,
        far_sem,
        load_sem,
        x_sem,
    ) = refs[2 * INPUTS + 2 :]
    tiles = x_ref.shape[0]
    elems = tiles * 128
    slots = sslots_ref.shape[1]
    width = bsend_ref.shape[2]
    count = sectors * slabs

    loads = {
        k: pltpu.make_async_copy(hbm_refs[k], vmem_refs[k], load_sem.at[k])
        for k in range(1, INPUTS)
    }
    fields = {
        (t, h): pltpu.make_async_copy(
            hbm_refs[0].at[h, :, pl.ds(128 * t, 128)], x_ref.at[t, h], x_sem.at[5 * t + h]
        )
        for h in (1, 2, 3, 0, 4)
        for t in range(tiles)
    }
    sec = lax.axis_index("sector")
    axi = lax.axis_index("axial")
    joint = sec * slabs + axi
    prev = lax.rem(joint + count - 1, count)
    nxt = lax.rem(joint + 1, count)
    dev_prev = (prev // slabs, lax.rem(prev, slabs))
    dev_next = (nxt // slabs, lax.rem(nxt, slabs))
    dev_low = (lax.rem(sec + sectors - 1, sectors), axi)
    dev_high = (lax.rem(sec + 1, sectors), axi)

    has_low = axi > 0
    has_high = axi < slabs - 1

    barrier = pltpu.get_barrier_semaphore()

    def greet(device):
        pl.semaphore_signal(barrier, inc=1, device_id=device, device_id_type=MESH)

    greet(dev_low)
    greet(dev_high)
    greet(dev_prev)

    @pl.when(has_high)
    def _():
        greet(dev_next)

    def start_block_loads():
        for k in (1, 13, 2, 3):
            loads[k].start()

    loads[11].start()

    @pl.when(jnp.logical_not(has_high))
    def _():
        start_block_loads()

    for k in (9, 8, 10, 6):
        loads[k].start()
    for key in fields:
        fields[key].start()

    @pl.when(has_high)
    def _():
        start_block_loads()

    for k in (7, 12, 4, 5):
        loads[k].start()

    def remote(src, dst, k, device):
        return pltpu.make_async_remote_copy(
            src_ref=src,
            dst_ref=dst,
            send_sem=send_sem.at[k],
            recv_sem=recv_sem.at[k],
            device_id=device,
            device_id_type=MESH,
        )

    up_x = remote(send_ref.at[1], recv_ref.at[0], 0, dev_high)
    down_x = remote(send_ref.at[0], recv_ref.at[1], 1, dev_low)
    up_z = remote(send_ref.at[3], recv_ref.at[2], 2, dev_next)
    down_z = remote(send_ref.at[2], recv_ref.at[3], 3, dev_prev)
    up_b = remote(bsend_ref.at[2], brecv_ref.at[0], 4, dev_next)
    down_b = remote(bsend_ref.at[0], brecv_ref.at[1], 5, dev_prev)

    loads[11].wait()
    rel = eb_ref[...] - (joint - 1) * owned
    rel = jnp.where(rel < 0, rel + BLOCKS, rel)
    rel = jnp.where(rel >= BLOCKS, rel - BLOCKS, rel)
    for j in (1, 0):
        rel = jnp.where(rel >= owned * (j + 1), rel + (width - owned), rel)
    ids = jnp.broadcast_to(rel, (128, elems)).T.astype(jnp.int16)
    for j in range(3 * width // 128):
        lanes = lax.broadcasted_iota(jnp.int32, (elems, 128), 1) + 128 * j
        blocks_ref[:, 128 * j : 128 * j + 128] = one_hot(lanes.astype(jnp.int16) == ids)

    def sum_blocks():
        for k in (1, 13, 2, 3):
            loads[k].wait()
        parts = []
        for t in range(tiles):
            lanes = slice(128 * t, 128 * t + 128)
            total = x_ref[t, 1] * vel_ref[0, :, lanes].astype(F32)
            total += x_ref[t, 2] * vel_ref[1, :, lanes].astype(F32)
            total += x_ref[t, 3] * vel_ref[2, :, lanes].astype(F32)
            parts.append(jnp.sum(total * weight_ref[...], axis=0, keepdims=True))
        elem_grad = drag_ref[...] * jnp.concatenate(parts, axis=1)
        weighted = bw_ref[...] * elem_grad
        w1 = weighted.astype(BF)
        rest = weighted - w1.astype(F32)
        w2 = rest.astype(BF)
        w3 = (rest - w2.astype(F32)).astype(BF).astype(F32)
        row16 = lax.broadcasted_iota(jnp.int32, (16, elems), 0)
        stack = jnp.where(row16 == 0, w1.astype(F32), 0.0)
        stack = jnp.where(row16 == 1, w2.astype(F32), stack)
        stack = jnp.where(row16 == 2, w3, stack).astype(BF)
        sums = dot(stack, blocks_ref[...])
        total = jnp.sum(sums, axis=0, keepdims=True)
        for j in range(3):
            part = total[:, j * width : (j + 1) * width]
            bsend_ref[j] = jnp.broadcast_to(part, (8, width))

    @pl.when(jnp.logical_not(has_high))
    def _():
        pl.semaphore_wait(barrier, 4)
        pl.semaphore_signal(far_sem, inc=1, device_id=dev_next, device_id_type=MESH)
        for h in (1, 2, 3):
            for t in range(tiles):
                fields[t, h].wait()
        sum_blocks()
        up_b.start()
        down_b.start()

    slot_ids = lax.broadcasted_iota(jnp.int32, (1, slots), 1)
    rows_slots = lax.broadcasted_iota(jnp.int32, (elems, slots), 0).astype(jnp.int16)

    columns = lax.broadcasted_iota(jnp.int32, (slots, elems), 1).astype(jnp.int16)

    def slot_row(i):
        if i >= 2:
            return aslots_ref[i - 2 : i - 1, :]
        return jnp.where(slot_ids < live_ref[:, i : i + 1], sslots_ref[i : i + 1, :], -1)

    def find_slots(i):
        ids = jnp.broadcast_to(slot_row(i), (elems, slots)).astype(jnp.int16)
        oh_ref[i] = one_hot(rows_slots == ids)

    def find_places(i):
        ids = jnp.broadcast_to(slot_row(i), (128, slots)).T
        ids = jnp.concatenate([ids] * tiles, axis=1).astype(jnp.int16)
        place_ref[i] = one_hot(columns == ids)

    def take_trace(t, face):
        lanes = slice(128 * t, 128 * t + 128)
        for c in range(5):
            hi, lo = split2(face_rows(x_ref, t, c, face))
            tr_ref[face, 16 * c : 16 * c + 16, lanes] = hi
            tr_ref[face, 80 + 16 * c : 96 + 16 * c, lanes] = lo

    def fill_send(i):
        face = SIDES[i]
        for t in range(tiles):
            take_trace(t, face)
        both = dot(tr_ref[face], oh_ref[i])
        both = both[:80] + both[80:]
        if i < 2:
            send_ref[i] = both
            return
        for n in range(0, slots, 128):
            parts = [both[16 * h : 16 * h + 16, n : n + 128] for h in range(5)]
            for c in range(5):
                value = mixed(coef_ref, 9 - face, c, parts)
                send_ref[i, 16 * c : 16 * c + 16, n : n + 128] = value

    for k in (9, 8, 10):
        loads[k].wait()
    for i in range(4):
        find_slots(i)
    loads[6].wait()
    for c in range(5):
        for h in range(5):
            coef_ref[5 * c + h] = jnp.broadcast_to(0.1 * nbrmat_ref[c][:, h : h + 1], (6, 128))
    @pl.when(has_high)
    def _():
        for h in (1, 2, 3):
            for t in range(tiles):
                fields[t, h].wait()

    for h in (0, 4):
        for t in range(tiles):
            fields[t, h].wait()
    fill_send(2)
    fill_send(3)

    @pl.when(jnp.logical_and(has_low, has_high))
    def _():
        pl.semaphore_wait(barrier, 4)

    @pl.when(jnp.logical_not(has_low))
    def _():
        pl.semaphore_wait(barrier, 3)

    @pl.when(has_high)
    def _():
        up_z.start()

    @pl.when(has_low)
    def _():
        down_z.start()

    @pl.when(jnp.logical_not(has_low))
    def _():
        recv_ref[2] = jnp.zeros((80, slots), F32)

    @pl.when(jnp.logical_not(has_high))
    def _():
        recv_ref[3] = jnp.zeros((80, slots), F32)

    fill_send(0)
    fill_send(1)
    up_x.start()
    down_x.start()

    @pl.when(has_high)
    def _():
        sum_blocks()
        up_b.start()

    @pl.when(jnp.logical_and(has_low, has_high))
    def _():
        down_b.start()

    for k in (7, 12, 4, 5):
        loads[k].wait()
    for i in range(4):
        find_places(i)

    spread = jnp.minimum(lax.broadcasted_iota(jnp.int32, (5, 384), 1) // 64, 4)
    spread = jnp.where(spread == lax.broadcasted_iota(jnp.int32, (5, 384), 0), 1.0, 0.0)
    for c in range(5):
        rows = slice(64 * c, 64 * c + 64)
        jac = jac_ref[0][:, c : c + 1] * spread[0:1, :]
        face = own_ref[c][:, 0:1] * spread[0:1, :]
        for h in range(1, 5):
            jac += jac_ref[h][:, c : c + 1] * spread[h : h + 1, :]
            face += own_ref[c][:, h : h + 1] * spread[h : h + 1, :]
        for t in range(3):
            lanes = slice(128 * t, 128 * t + 128)
            total = mats_ref[0] * jac[0:1, lanes]
            for j in range(1, 9):
                row = jac[j : j + 1, lanes] if j < 3 else face[j - 3 : j - 2, lanes]
                total += mats_ref[j] * row
            hi, lo = split2(total)
            places = ((768, hi), (896, lo)) if t == 2 else ((0, hi), (256, hi), (512, lo))
            for base, part in places:
                base += 128 * t if t < 2 else 0
                a_ref[rows, base : base + 128] = part

    for t in range(tiles):
        lanes = slice(128 * t, 128 * t + 128)
        for h in range(5):
            hi, lo = split2(x_ref[t, h])
            for base, part in ((0, hi), (256, lo)) if h < 4 else ((256, hi), (320, lo)):
                xs_ref[64 * h + base : 64 * h + base + 64, lanes] = part
        for face in (2, 3):
            take_trace(t, face)

    xs = [xs_ref[rows, :] for rows in (slice(0, 512), slice(0, 256), slice(512, 640), slice(512, 576))]
    own = dot(a_ref[:, 0:960], jnp.concatenate(xs, axis=0))
    keep = 1.0 - 0.1 * drag_ref[...]
    for t in range(tiles):
        lanes = slice(128 * t, 128 * t + 128)
        for c in range(5):
            x = x_ref[t, c]
            scaled = x * keep[:, lanes] if 1 <= c <= 3 else x
            acc_ref[t, c] = scaled + own[64 * c : 64 * c + 64, lanes]

    rows_src = lax.broadcasted_iota(jnp.int32, (elems, elems), 0).astype(jnp.int16)
    def gather(f, i=None):
        g = f + 1 - 2 * (f % 2)
        ids = jnp.broadcast_to(nbr_ref[f : f + 1, :], (elems, elems)).astype(jnp.int16)
        sources, places = tr_ref[g], one_hot(rows_src == ids)
        if i is not None:
            got = jnp.concatenate(split2(recv_ref[i]), axis=0)
            sources = jnp.concatenate([sources, got], axis=1)
            places = jnp.concatenate([places, place_ref[i]], axis=0)
        both = dot(sources, places)
        both = both[:80] + both[80:]
        for t in range(tiles):
            parts = [both[16 * h : 16 * h + 16, 128 * t : 128 * t + 128] for h in range(5)]
            add_face(acc_ref, t, f, [mixed(coef_ref, f, c, parts) for c in range(5)])

    def answer_far(mine):
        @pl.when(jnp.logical_and(jnp.logical_not(has_low), mine))
        def _():
            pl.semaphore_wait(far_sem, 1)
            down_b.start()

    for f in (2, 3, 4, 5):
        gather(f)
    answer_far(sec >= sectors // 2)
    up_x.wait()
    down_x.wait()
    gather(0, 0)
    answer_far(sec < sectors // 2)
    gather(1, 1)

    @pl.when(has_high)
    def _():
        up_z.wait_send()
        down_z.wait_recv()

    @pl.when(has_low)
    def _():
        down_z.wait_send()
        up_z.wait_recv()

    for i in (2, 3):
        both = dot(jnp.concatenate(split2(recv_ref[i]), axis=0), place_ref[i])
        both = both[:80] + both[80:]
        for t in range(tiles):
            lanes = slice(128 * t, 128 * t + 128)
            rows = [both[16 * c : 16 * c + 16, lanes] for c in range(5)]
            add_face(acc_ref, t, SIDES[i], rows)

    up_b.wait()
    down_b.wait()
    sums = bsend_ref[1] + brecv_ref[0] + brecv_ref[1]
    grad_ref[...] = sums[0, :owned]


def finish(acc_ref, sums_ref, out_ref, grad_ref, sem):
    tiles = acc_ref.shape[0]
    copies = [pltpu.make_async_copy(sums_ref, grad_ref, sem.at[tiles])]
    for t in range(tiles):
        place = out_ref.at[:, :, pl.ds(128 * t, 128)]
        copies.append(pltpu.make_async_copy(acc_ref.at[t], place, sem.at[t]))
    for copy in copies:
        copy.start()
    for copy in copies:
        copy.wait()


def on_device(
    sectors,
    slabs,
    adjoint,
    velocity,
    drag,
    block_weight,
    flux_jac,
    face_own,
    face_nbr,
    nbr_local,
    sector_slots,
    axial_slots,
    sector_live,
    elem_block,
):
    elems = adjoint.shape[2]
    tiles = elems // 128
    slots = sector_slots.shape[1]
    owned = BLOCKS // (sectors * slabs)
    width = -(-owned // 128) * 128
    operands = (
        adjoint,
        velocity,
        drag.reshape(1, elems),
        block_weight.reshape(1, elems),
        jnp.transpose(flux_jac, (1, 0, 2)),
        jnp.transpose(face_own, (1, 0, 2)),
        jnp.transpose(face_nbr, (1, 0, 2)),
        nbr_local,
        sector_slots,
        axial_slots,
        sector_live.reshape(1, 2),
        elem_block.reshape(1, elems),
        *constant_tables(),
    )
    vmem = pl.BlockSpec(memory_space=pltpu.VMEM)
    hbm = pl.BlockSpec(memory_space=pltpu.HBM)
    handed = pl.pallas_call(
        functools.partial(exchange, sectors, slabs, owned),
        out_shape=(
            pltpu.VMEM((tiles, 5, 64, 128), F32),
            pltpu.VMEM((owned,), F32),
        ),
        in_specs=[hbm] * INPUTS,
        out_specs=(vmem,) * 2,
        scratch_shapes=[pltpu.VMEM((tiles, 5, 64, 128), F32)]
        + [pltpu.VMEM(a.shape, a.dtype) for a in operands[1:]]
        + [
            pltpu.VMEM((640, elems), BF),
            pltpu.VMEM((6, 160, elems), BF),
            pltpu.VMEM((4, elems, slots), BF),
            pltpu.VMEM((4, slots, elems), BF),
            pltpu.VMEM((4, 80, slots), F32),
            pltpu.VMEM((4, 80, slots), F32),
            pltpu.VMEM((320, 1024), BF),
            pltpu.VMEM((25, 6, 128), F32),
            pltpu.VMEM((elems, 3 * width), BF),
            pltpu.VMEM((3, 8, width), F32),
            pltpu.VMEM((2, 8, width), F32),
            pltpu.SemaphoreType.DMA((6,)),
            pltpu.SemaphoreType.DMA((6,)),
            pltpu.SemaphoreType.REGULAR,
            pltpu.SemaphoreType.DMA((INPUTS,)),
            pltpu.SemaphoreType.DMA((5 * tiles,)),
        ],
        compiler_params=pltpu.CompilerParams(
            collective_id=0, has_side_effects=True, vmem_limit_bytes=60 * 1024 * 1024
        ),
    )(*operands)
    return pl.pallas_call(
        finish,
        out_shape=(
            jax.ShapeDtypeStruct(adjoint.shape, F32),
            jax.ShapeDtypeStruct((owned,), F32),
        ),
        in_specs=[vmem] * 2,
        out_specs=(hbm, hbm),
        scratch_shapes=[
            pltpu.SemaphoreType.DMA((tiles + 1,)),
        ],
        compiler_params=pltpu.CompilerParams(vmem_limit_bytes=40 * 1024 * 1024),
    )(*handed)


def solution(mesh):
    placed = (
        P(None, None, ("sector", "axial")),
        P(None, None, ("sector", "axial")),
        P(("sector", "axial")),
        P(("sector", "axial")),
        P(),
        P(),
        P(),
        P(None, ("sector", "axial")),
        P(None, ("sector", "axial")),
        P(None, ("sector", "axial")),
        P("sector", "axial", None),
        P(("sector", "axial")),
    )
    return jax.shard_map(
        functools.partial(on_device, mesh.shape["sector"], mesh.shape["axial"]),
        mesh=mesh,
        in_specs=placed,
        out_specs=(P(None, None, ("sector", "axial")), P(("sector", "axial"))),
        check_vma=False,
    )
```

```python
import functools

import jax
import jax.numpy as jnp
import numpy as np
from jax import lax
from jax.experimental import pallas as pl
from jax.experimental.pallas import tpu as pltpu
from jax.sharding import PartitionSpec as P

BLOCKS = 4096
BF = jnp.bfloat16
F32 = jnp.float32
MESH = pl.DeviceIdType.MESH
INPUTS = 14
SIDES = (0, 1, 4, 5)


def lobatto_tables():
    points = np.array([-1.0, -1.0 / np.sqrt(5.0), 1.0 / np.sqrt(5.0), 1.0])
    weights = np.array([1.0, 5.0, 5.0, 1.0]) / 6.0
    scales = np.array(
        [np.prod([points[i] - points[k] for k in range(4) if k != i]) for i in range(4)]
    )
    derivative = np.zeros((4, 4))
    for i in range(4):
        for p in range(4):
            if i != p:
                derivative[i, p] = scales[i] / scales[p] / (points[i] - points[p])
            else:
                derivative[i, p] = sum((1.0 / (points[i] - points[k]) for k in range(4) if k != i))
    node_weight = (
        weights[:, None, None] * weights[None, :, None] * weights[None, None, :]
    ).reshape(64) / 8.0
    return (derivative, node_weight)


def constant_tables():
    derivative, node_weight = lobatto_tables()
    eye = np.eye(4)
    step = derivative.T
    mats = [
        np.kron(np.kron(step, eye), eye),
        np.kron(np.kron(eye, step), eye),
        np.kron(np.kron(eye, eye), step),
    ]
    nodes = np.arange(64).reshape(4, 4, 4)
    faces = [nodes[0], nodes[3], nodes[:, 0], nodes[:, 3], nodes[:, :, 0], nodes[:, :, 3]]
    for ids in faces:
        diag = np.zeros((64, 64))
        diag[ids.reshape(16), ids.reshape(16)] = 1.0
        mats.append(diag)
    mats = [0.1 * np.concatenate([m, m], axis=1) for m in mats]
    weights = np.repeat(node_weight[:, None], 128, axis=1)
    return jnp.asarray(np.stack(mats), F32), jnp.asarray(weights, F32)


def split2(x):
    hi = x.astype(BF)
    return hi, (x - hi.astype(F32)).astype(BF)


def dot(a, b):
    return jnp.dot(a, b, preferred_element_type=F32)


def dot_nt(a, b):
    return lax.dot_general(a, b, (((1,), (1,)), ((), ())), preferred_element_type=F32)


def one_hot(mask):
    return jnp.where(mask, jnp.ones((), BF), jnp.zeros((), BF))


def add_face(ref, tile, face, part):
    low = lax.broadcasted_iota(jnp.int32, (8, 128), 0) < 4
    for c in range(5):
        rows = part[c]
        if face < 2:
            ids = pl.ds(48 * face, 16)
            ref[tile, c, ids, :] = ref[tile, c, ids, :] + rows
        elif face >= 4:
            ids = pl.ds(3 * (face - 4), 16, stride=4)
            ref[tile, c, ids, :] = ref[tile, c, ids, :] + rows
        else:
            for v in range(2):
                both = rows[8 * v : 8 * v + 8]
                turned = pltpu.roll(both, 4, 0)
                for k in range(2):
                    ids = pl.ds(32 * v + 16 * k + 8 * (face - 2), 8)
                    value = both if k == face - 2 else turned
                    mask = low if face == 2 else jnp.logical_not(low)
                    ref[tile, c, ids, :] = ref[tile, c, ids, :] + jnp.where(mask, value, 0.0)


def mixed(coef_ref, face, c, parts):
    total = coef_ref[5 * c, face : face + 1, :] * parts[0]
    for h in range(1, 5):
        total += coef_ref[5 * c + h, face : face + 1, :] * parts[h]
    return total


def face_rows(ref, tile, c, face):
    if face < 2:
        return ref[tile, c, 48 * face : 48 * face + 16, :]
    if face >= 4:
        return ref[tile, c, pl.ds(3 * (face - 4), 16, stride=4), :]
    low = lax.broadcasted_iota(jnp.int32, (8, 128), 0) < 4
    out = []
    for v in range(2):
        first = ref[tile, c, 32 * v + 8 * (face - 2) : 32 * v + 8 * (face - 2) + 8, :]
        second = ref[tile, c, 32 * v + 16 + 8 * (face - 2) : 32 * v + 24 + 8 * (face - 2), :]
        if face == 2:
            out.append(jnp.where(low, first, pltpu.roll(second, 4, 0)))
        else:
            out.append(jnp.where(low, pltpu.roll(first, 4, 0), second))
    return jnp.concatenate(out, axis=0)


def exchange(sectors, slabs, owned, *refs):
    hbm_refs = refs[:INPUTS]
    acc_ref, grad_ref = refs[INPUTS : INPUTS + 2]
    x_ref = refs[INPUTS + 2]
    vmem_refs = (None,) + refs[INPUTS + 3 : 2 * INPUTS + 2]
    (
        _,
        vel_ref,
        drag_ref,
        bw_ref,
        jac_ref,
        own_ref,
        nbrmat_ref,
        nbr_ref,
        sslots_ref,
        aslots_ref,
        live_ref,
        eb_ref,
        mats_ref,
        weight_ref,
    ) = vmem_refs
    (
        xs_ref,
        tr_ref,
        oh_ref,
        place_ref,
        send_ref,
        recv_ref,
        a_ref,
        coef_ref,
        bsend_ref,
        brecv_ref,
        send_sem,
        recv_sem,
        far_sem,
        load_sem,
        x_sem,
    ) = refs[2 * INPUTS + 2 :]
    tiles = x_ref.shape[0]
    elems = tiles * 128
    slots = sslots_ref.shape[1]
    width = bsend_ref.shape[2]
    count = sectors * slabs

    loads = {
        k: pltpu.make_async_copy(hbm_refs[k], vmem_refs[k], load_sem.at[k])
        for k in range(1, INPUTS)
    }
    fields = {
        (t, h): pltpu.make_async_copy(
            hbm_refs[0].at[h, :, pl.ds(128 * t, 128)], x_ref.at[t, h], x_sem.at[5 * t + h]
        )
        for h in (1, 2, 3, 0, 4)
        for t in range(tiles)
    }
    sec = lax.axis_index("sector")
    axi = lax.axis_index("axial")
    joint = sec * slabs + axi
    prev = lax.rem(joint + count - 1, count)
    nxt = lax.rem(joint + 1, count)
    dev_prev = (prev // slabs, lax.rem(prev, slabs))
    dev_next = (nxt // slabs, lax.rem(nxt, slabs))
    dev_low = (lax.rem(sec + sectors - 1, sectors), axi)
    dev_high = (lax.rem(sec + 1, sectors), axi)

    has_low = axi > 0
    has_high = axi < slabs - 1

    barrier = pltpu.get_barrier_semaphore()

    def greet(device):
        pl.semaphore_signal(barrier, inc=1, device_id=device, device_id_type=MESH)

    greet(dev_low)
    greet(dev_high)
    greet(dev_prev)

    @pl.when(has_high)
    def _():
        greet(dev_next)

    def start_block_loads():
        for k in (1, 13, 2, 3, 11):
            loads[k].start()

    @pl.when(jnp.logical_not(has_high))
    def _():
        start_block_loads()

    for k in (9, 8, 10, 6):
        loads[k].start()
    for key in fields:
        fields[key].start()

    @pl.when(has_high)
    def _():
        start_block_loads()

    for k in (7, 12, 4, 5):
        loads[k].start()

    def remote(src, dst, k, device):
        return pltpu.make_async_remote_copy(
            src_ref=src,
            dst_ref=dst,
            send_sem=send_sem.at[k],
            recv_sem=recv_sem.at[k],
            device_id=device,
            device_id_type=MESH,
        )

    up_x = remote(send_ref.at[1], recv_ref.at[0], 0, dev_high)
    down_x = remote(send_ref.at[0], recv_ref.at[1], 1, dev_low)
    up_z = remote(send_ref.at[3], recv_ref.at[2], 2, dev_next)
    down_z = remote(send_ref.at[2], recv_ref.at[3], 3, dev_prev)
    up_b = remote(bsend_ref.at[2], brecv_ref.at[0], 4, dev_next)
    down_b = remote(bsend_ref.at[0], brecv_ref.at[1], 5, dev_prev)

    def sum_blocks():
        for k in (1, 13, 2, 3, 11):
            loads[k].wait()
        parts = []
        for t in range(tiles):
            lanes = slice(128 * t, 128 * t + 128)
            total = x_ref[t, 1] * vel_ref[0, :, lanes].astype(F32)
            total += x_ref[t, 2] * vel_ref[1, :, lanes].astype(F32)
            total += x_ref[t, 3] * vel_ref[2, :, lanes].astype(F32)
            parts.append(jnp.sum(total * weight_ref[...], axis=0, keepdims=True))
        elem_grad = drag_ref[...] * jnp.concatenate(parts, axis=1)
        weighted = bw_ref[...] * elem_grad
        w1 = weighted.astype(BF)
        rest = weighted - w1.astype(F32)
        w2 = rest.astype(BF)
        w3 = (rest - w2.astype(F32)).astype(BF).astype(F32)
        row16 = lax.broadcasted_iota(jnp.int32, (16, elems), 0)
        stack = jnp.where(row16 == 0, w1.astype(F32), 0.0)
        stack = jnp.where(row16 == 1, w2.astype(F32), stack)
        stack = jnp.where(row16 == 2, w3, stack).astype(BF)
        rel = eb_ref[...] - (joint - 1) * owned
        rel = jnp.where(rel < 0, rel + BLOCKS, rel)
        rel = jnp.where(rel >= BLOCKS, rel - BLOCKS, rel)
        for j in (1, 0):
            rel = jnp.where(rel >= owned * (j + 1), rel + (width - owned), rel)
        rows_blk = lax.broadcasted_iota(jnp.int32, (3 * width, elems), 0).astype(jnp.int16)
        ids = jnp.broadcast_to(rel, (3 * width, elems)).astype(jnp.int16)
        sums = dot_nt(stack, one_hot(rows_blk == ids))
        total = jnp.sum(sums, axis=0, keepdims=True)
        for j in range(3):
            part = total[:, j * width : (j + 1) * width]
            bsend_ref[j] = jnp.broadcast_to(part, (8, width))

    @pl.when(jnp.logical_not(has_high))
    def _():
        pl.semaphore_wait(barrier, 4)
        pl.semaphore_signal(far_sem, inc=1, device_id=dev_next, device_id_type=MESH)
        for h in (1, 2, 3):
            for t in range(tiles):
                fields[t, h].wait()
        sum_blocks()
        up_b.start()
        down_b.start()

    slot_ids = lax.broadcasted_iota(jnp.int32, (1, slots), 1)
    rows_slots = lax.broadcasted_iota(jnp.int32, (elems, slots), 0).astype(jnp.int16)

    columns = lax.broadcasted_iota(jnp.int32, (slots, elems), 1).astype(jnp.int16)

    def slot_row(i):
        if i >= 2:
            return aslots_ref[i - 2 : i - 1, :]
        return jnp.where(slot_ids < live_ref[:, i : i + 1], sslots_ref[i : i + 1, :], -1)

    def find_slots(i):
        ids = jnp.broadcast_to(slot_row(i), (elems, slots)).astype(jnp.int16)
        oh_ref[i] = one_hot(rows_slots == ids)

    def find_places(i):
        ids = jnp.broadcast_to(slot_row(i), (128, slots)).T
        ids = jnp.concatenate([ids] * tiles, axis=1).astype(jnp.int16)
        place_ref[i] = one_hot(columns == ids)

    def take_trace(t, face):
        lanes = slice(128 * t, 128 * t + 128)
        for c in range(5):
            hi, lo = split2(face_rows(x_ref, t, c, face))
            tr_ref[face, 16 * c : 16 * c + 16, lanes] = hi
            tr_ref[face, 80 + 16 * c : 96 + 16 * c, lanes] = lo

    def fill_send(i):
        face = SIDES[i]
        for t in range(tiles):
            take_trace(t, face)
        both = dot(tr_ref[face], oh_ref[i])
        both = both[:80] + both[80:]
        if i < 2:
            send_ref[i] = both
            return
        for n in range(0, slots, 128):
            parts = [both[16 * h : 16 * h + 16, n : n + 128] for h in range(5)]
            for c in range(5):
                value = mixed(coef_ref, 9 - face, c, parts)
                send_ref[i, 16 * c : 16 * c + 16, n : n + 128] = value

    for k in (9, 8, 10):
        loads[k].wait()
    for i in range(4):
        find_slots(i)
    loads[6].wait()
    for c in range(5):
        for h in range(5):
            coef_ref[5 * c + h] = jnp.broadcast_to(0.1 * nbrmat_ref[c][:, h : h + 1], (6, 128))
    @pl.when(has_high)
    def _():
        for h in (1, 2, 3):
            for t in range(tiles):
                fields[t, h].wait()

    for h in (0, 4):
        for t in range(tiles):
            fields[t, h].wait()
    fill_send(2)
    fill_send(3)

    @pl.when(jnp.logical_and(has_low, has_high))
    def _():
        pl.semaphore_wait(barrier, 4)

    @pl.when(jnp.logical_not(has_low))
    def _():
        pl.semaphore_wait(barrier, 3)

    @pl.when(has_low)
    def _():
        down_z.start()

    @pl.when(has_high)
    def _():
        up_z.start()

    @pl.when(jnp.logical_not(has_low))
    def _():
        recv_ref[2] = jnp.zeros((80, slots), F32)

    @pl.when(jnp.logical_not(has_high))
    def _():
        recv_ref[3] = jnp.zeros((80, slots), F32)

    fill_send(0)
    fill_send(1)
    up_x.start()
    down_x.start()

    @pl.when(has_high)
    def _():
        sum_blocks()
        up_b.start()

    @pl.when(jnp.logical_and(has_low, has_high))
    def _():
        down_b.start()

    for k in (7, 12, 4, 5):
        loads[k].wait()
    for i in range(4):
        find_places(i)

    spread = jnp.minimum(lax.broadcasted_iota(jnp.int32, (5, 384), 1) // 64, 4)
    spread = jnp.where(spread == lax.broadcasted_iota(jnp.int32, (5, 384), 0), 1.0, 0.0)
    for c in range(5):
        rows = slice(64 * c, 64 * c + 64)
        jac = jac_ref[0][:, c : c + 1] * spread[0:1, :]
        face = own_ref[c][:, 0:1] * spread[0:1, :]
        for h in range(1, 5):
            jac += jac_ref[h][:, c : c + 1] * spread[h : h + 1, :]
            face += own_ref[c][:, h : h + 1] * spread[h : h + 1, :]
        for t in range(3):
            lanes = slice(128 * t, 128 * t + 128)
            total = mats_ref[0] * jac[0:1, lanes]
            for j in range(1, 9):
                row = jac[j : j + 1, lanes] if j < 3 else face[j - 3 : j - 2, lanes]
                total += mats_ref[j] * row
            hi, lo = split2(total)
            places = ((768, hi), (896, lo)) if t == 2 else ((0, hi), (256, hi), (512, lo))
            for base, part in places:
                base += 128 * t if t < 2 else 0
                a_ref[rows, base : base + 128] = part

    for t in range(tiles):
        lanes = slice(128 * t, 128 * t + 128)
        for h in range(5):
            hi, lo = split2(x_ref[t, h])
            for base, part in ((0, hi), (256, lo)) if h < 4 else ((256, hi), (320, lo)):
                xs_ref[64 * h + base : 64 * h + base + 64, lanes] = part
        for face in (2, 3):
            take_trace(t, face)

    xs = [xs_ref[rows, :] for rows in (slice(0, 512), slice(0, 256), slice(512, 640), slice(512, 576))]
    own = dot(a_ref[:, 0:960], jnp.concatenate(xs, axis=0))
    keep = 1.0 - 0.1 * drag_ref[...]
    for t in range(tiles):
        lanes = slice(128 * t, 128 * t + 128)
        for c in range(5):
            x = x_ref[t, c]
            scaled = x * keep[:, lanes] if 1 <= c <= 3 else x
            acc_ref[t, c] = scaled + own[64 * c : 64 * c + 64, lanes]

    rows_src = lax.broadcasted_iota(jnp.int32, (elems, elems), 0).astype(jnp.int16)
    def gather(f, i=None):
        g = f + 1 - 2 * (f % 2)
        ids = jnp.broadcast_to(nbr_ref[f : f + 1, :], (elems, elems)).astype(jnp.int16)
        sources, places = tr_ref[g], one_hot(rows_src == ids)
        if i is not None:
            got = jnp.concatenate(split2(recv_ref[i]), axis=0)
            sources = jnp.concatenate([sources, got], axis=1)
            places = jnp.concatenate([places, place_ref[i]], axis=0)
        both = dot(sources, places)
        both = both[:80] + both[80:]
        for t in range(tiles):
            parts = [both[16 * h : 16 * h + 16, 128 * t : 128 * t + 128] for h in range(5)]
            add_face(acc_ref, t, f, [mixed(coef_ref, f, c, parts) for c in range(5)])

    for f in (2, 3, 4, 5):
        gather(f)

    @pl.when(jnp.logical_not(has_low))
    def _():
        pl.semaphore_wait(far_sem, 1)
        down_b.start()

    up_x.wait()
    down_x.wait()
    gather(0, 0)
    gather(1, 1)

    @pl.when(has_high)
    def _():
        up_z.wait_send()
        down_z.wait_recv()

    @pl.when(has_low)
    def _():
        down_z.wait_send()
        up_z.wait_recv()

    for i in (2, 3):
        both = dot(jnp.concatenate(split2(recv_ref[i]), axis=0), place_ref[i])
        both = both[:80] + both[80:]
        for t in range(tiles):
            lanes = slice(128 * t, 128 * t + 128)
            rows = [both[16 * c : 16 * c + 16, lanes] for c in range(5)]
            add_face(acc_ref, t, SIDES[i], rows)

    up_b.wait()
    down_b.wait()
    sums = bsend_ref[1] + brecv_ref[0] + brecv_ref[1]
    grad_ref[...] = sums[0, :owned]


def finish(acc_ref, sums_ref, out_ref, grad_ref, sem):
    tiles = acc_ref.shape[0]
    copies = [pltpu.make_async_copy(sums_ref, grad_ref, sem.at[tiles])]
    for t in range(tiles):
        place = out_ref.at[:, :, pl.ds(128 * t, 128)]
        copies.append(pltpu.make_async_copy(acc_ref.at[t], place, sem.at[t]))
    for copy in copies:
        copy.start()
    for copy in copies:
        copy.wait()


def on_device(
    sectors,
    slabs,
    adjoint,
    velocity,
    drag,
    block_weight,
    flux_jac,
    face_own,
    face_nbr,
    nbr_local,
    sector_slots,
    axial_slots,
    sector_live,
    elem_block,
):
    elems = adjoint.shape[2]
    tiles = elems // 128
    slots = sector_slots.shape[1]
    owned = BLOCKS // (sectors * slabs)
    width = -(-owned // 128) * 128
    operands = (
        adjoint,
        velocity,
        drag.reshape(1, elems),
        block_weight.reshape(1, elems),
        jnp.transpose(flux_jac, (1, 0, 2)),
        jnp.transpose(face_own, (1, 0, 2)),
        jnp.transpose(face_nbr, (1, 0, 2)),
        nbr_local,
        sector_slots,
        axial_slots,
        sector_live.reshape(1, 2),
        elem_block.reshape(1, elems),
        *constant_tables(),
    )
    vmem = pl.BlockSpec(memory_space=pltpu.VMEM)
    hbm = pl.BlockSpec(memory_space=pltpu.HBM)
    handed = pl.pallas_call(
        functools.partial(exchange, sectors, slabs, owned),
        out_shape=(
            pltpu.VMEM((tiles, 5, 64, 128), F32),
            pltpu.VMEM((owned,), F32),
        ),
        in_specs=[hbm] * INPUTS,
        out_specs=(vmem,) * 2,
        scratch_shapes=[pltpu.VMEM((tiles, 5, 64, 128), F32)]
        + [pltpu.VMEM(a.shape, a.dtype) for a in operands[1:]]
        + [
            pltpu.VMEM((640, elems), BF),
            pltpu.VMEM((6, 160, elems), BF),
            pltpu.VMEM((4, elems, slots), BF),
            pltpu.VMEM((4, slots, elems), BF),
            pltpu.VMEM((4, 80, slots), F32),
            pltpu.VMEM((4, 80, slots), F32),
            pltpu.VMEM((320, 1024), BF),
            pltpu.VMEM((25, 6, 128), F32),
            pltpu.VMEM((3, 8, width), F32),
            pltpu.VMEM((2, 8, width), F32),
            pltpu.SemaphoreType.DMA((6,)),
            pltpu.SemaphoreType.DMA((6,)),
            pltpu.SemaphoreType.REGULAR,
            pltpu.SemaphoreType.DMA((INPUTS,)),
            pltpu.SemaphoreType.DMA((5 * tiles,)),
        ],
        compiler_params=pltpu.CompilerParams(
            collective_id=0, has_side_effects=True, vmem_limit_bytes=60 * 1024 * 1024
        ),
    )(*operands)
    return pl.pallas_call(
        finish,
        out_shape=(
            jax.ShapeDtypeStruct(adjoint.shape, F32),
            jax.ShapeDtypeStruct((owned,), F32),
        ),
        in_specs=[vmem] * 2,
        out_specs=(hbm, hbm),
        scratch_shapes=[
            pltpu.SemaphoreType.DMA((tiles + 1,)),
        ],
        compiler_params=pltpu.CompilerParams(vmem_limit_bytes=40 * 1024 * 1024),
    )(*handed)


def solution(mesh):
    placed = (
        P(None, None, ("sector", "axial")),
        P(None, None, ("sector", "axial")),
        P(("sector", "axial")),
        P(("sector", "axial")),
        P(),
        P(),
        P(),
        P(None, ("sector", "axial")),
        P(None, ("sector", "axial")),
        P(None, ("sector", "axial")),
        P("sector", "axial", None),
        P(("sector", "axial")),
    )
    return jax.shard_map(
        functools.partial(on_device, mesh.shape["sector"], mesh.shape["axial"]),
        mesh=mesh,
        in_specs=placed,
        out_specs=(P(None, None, ("sector", "axial")), P(("sector", "axial"))),
        check_vma=False,
    )
```
